32 devices in a mesh: dp: 8 (over y, x, core), mp: 4 (over z).
Axes of the slice: x: 2, y: 2, z: 4, core: 2. Of those that a mesh axis runs over, the one named last changes fastest.
Arguments:
- tokens: bfloat16 [32, 1024, 512], P('dp'), may hold values from -6 to 6
- segment_ids: int32 [32, 1024], P('dp'), may hold values from 0 to 3, never falling along the last dimension, each value on 1 to 512 neighbouring positions
- pad_lengths: int32 [32], P('dp'), may hold values from 0 to 255
- cotangent: bfloat16 [32, 1024, 512], P('dp'), may hold values from -6 to 6
- w_qkv: float32 [512, 3, 512], P('dp', None, 'mp'), may hold values from -0.25 to 0.25
- w_out: float32 [512, 512], P('mp', 'dp'), may hold values from -2 to 2
- w_up: float32 [512, 2048], P('dp', 'mp'), may hold values from -0.25 to 0.25
- w_down: float32 [2048, 512], P('mp', 'dp'), may hold values from -0.125 to 0.125
- qv_bias: float32 [2, 8, 64], P(None, 'mp', 'dp'), may hold values from -3 to 3
- ff_bias: float32 [32, 64], P('mp', 'dp'), may hold values from -3 to 3
- norm_gains: float32 [2, 512], P(None, 'dp'), may hold values from 0.5 to 1.5
- norm_shifts: float32 [4, 512], P(None, 'dp'), may hold values from -2 to 2
- first_qkv: float32 [512, 3, 512], P('dp', None, 'mp'), may hold values from -64 to 64
- first_out: float32 [512, 512], P('mp', 'dp'), may hold values from -64 to 64
- first_up: float32 [512, 2048], P('dp', 'mp'), may hold values from -64 to 64
- first_down: float32 [2048, 512], P('mp', 'dp'), may hold values from -64 to 64
- first_qv_bias: float32 [2, 8, 64], P(None, 'mp', 'dp'), may hold values from -64 to 64
- first_ff_bias: float32 [32, 64], P('mp', 'dp'), may hold values from -64 to 64
- first_gains: float32 [2, 512], P(None, 'dp'), may hold values from -64 to 64
- first_shifts: float32 [4, 512], P(None, 'dp'), may hold values from -64 to 64
- second_qkv: float32 [512, 3, 512], P('dp', None, 'mp'), may hold values from 8.192 to 32.768
- second_out: float32 [512, 512], P('mp', 'dp'), may hold values from 8.192 to 32.768
- second_up: float32 [512, 2048], P('dp', 'mp'), may hold values from 8.192 to 32.768
- second_down: float32 [2048, 512], P('mp', 'dp'), may hold values from 8.192 to 32.768
- second_qv_bias: float32 [2, 8, 64], P(None, 'mp', 'dp'), may hold values from 8.192 to 32.768
- second_ff_bias: float32 [32, 64], P('mp', 'dp'), may hold values from 8.192 to 32.768
- second_gains: float32 [2, 512], P(None, 'dp'), may hold values from 8.192 to 32.768
- second_shifts: float32 [4, 512], P(None, 'dp'), may hold values from 8.192 to 32.768
Outputs:
- layer_out: bfloat16 [32, 1024, 512], P('dp')
- tokens_grad: float32 [32, 1024, 512], P('dp')
- next_w_qkv: float32 [512, 3, 512], P('dp', None, 'mp')
- next_w_out: float32 [512, 512], P('mp', 'dp')
- next_w_up: float32 [512, 2048], P('dp', 'mp')
- next_w_down: float32 [2048, 512], P('mp', 'dp')
- next_qv_bias: float32 [2, 8, 64], P(None, 'mp', 'dp')
- next_ff_bias: float32 [32, 64], P('mp', 'dp')
- next_gains: float32 [2, 512], P(None, 'dp')
- next_shifts: float32 [4, 512], P(None, 'dp')
- next_first_qkv: float32 [512, 3, 512], P('dp', None, 'mp')
- next_first_out: float32 [512, 512], P('mp', 'dp')
- next_first_up: float32 [512, 2048], P('dp', 'mp')
- next_first_down: float32 [2048, 512], P('mp', 'dp')
- next_first_qv_bias: float32 [2, 8, 64], P(None, 'mp', 'dp')
- next_first_ff_bias: float32 [32, 64], P('mp', 'dp')
- next_first_gains: float32 [2, 512], P(None, 'dp')
- next_first_shifts: float32 [4, 512], P(None, 'dp')
- next_second_qkv: float32 [512, 3, 512], P('dp', None, 'mp')
- next_second_out: float32 [512, 512], P('mp', 'dp')
- next_second_up: float32 [512, 2048], P('dp', 'mp')
- next_second_down: float32 [2048, 512], P('mp', 'dp')
- next_second_qv_bias: float32 [2, 8, 64], P(None, 'mp', 'dp')
- next_second_ff_bias: float32 [32, 64], P('mp', 'dp')
- next_second_gains: float32 [2, 512], P(None, 'dp')
- next_second_shifts: float32 [4, 512], P(None, 'dp')
The draws below stay inside these ranges and needn't reach their ends.
Inputs may be any that keep to these rules, and one draw needn't show every extreme that they name: `segment_ids`: within a row the ids never fall; a segment covers at most 512 positions, and one segment of every row exactly that many. The last pad_lengths positions of a row are padding.
All inputs are finite; a program needn't handle non-finite values.
Results may differ from the reference program's by a relative error of at most 0.015.
The reference program's roundings to bfloat16 on the way count: a program that leaves them out, or rounds other values in their place, can miss the bound.
Values may be sent and summed in bfloat16 or wider, within the bound.
No kernel may reach another device: no remote copies, remote signals or barrier semaphores. Data moves between devices by JAX's collectives and lax.ppermute only.
A program may use at most 192 MiB of HBM per device.

```python
import math
import jax
import jax.numpy as jnp
import numpy as np
from jax import lax

D = 512
HEADS = 8
HEAD_DIM = 64
FF = 2048
LEN = 1024
STEP = 10
QBLOCK = 512
ROWS = 32
TOKENS = 32768


def place_ends(values, rng, smallest, top_value):
    shape = values.shape
    index_at = [jax.random.randint(jax.random.fold_in(rng, axis), (), 0, shape[axis]) for axis in range(len(shape))]
    values = values.at[tuple(index_at)].set(smallest)
    longest = shape.index(max(shape))
    index_at[longest] = (index_at[longest] + 1) % shape[longest]
    return values.at[tuple(index_at)].set(top_value)


def block_scale(stream_key, shape, cuts, least, high):
    def one(dim, blocks):
        steps = jax.random.uniform(jax.random.fold_in(jax.random.fold_in(stream_key, 6), dim), (blocks,), jnp.float32, least / len(cuts), high / len(cuts))
        return jnp.repeat(jnp.exp(steps), shape[dim] // blocks).reshape((-1,) + (1,) * (len(shape) - dim - 1))

    level = one(*cuts[0])
    for cut in cuts[1:]:
        level = level * one(*cut)
    return level


def profile(number_of, total, bound, slope):
    portions = [(1 << 20) // math.isqrt(grade ** slope) + 1 for grade in range(2, number_of + 1)]
    spare, given = total - bound - (number_of - 1), [1] * (number_of - 1)
    while spare > 0:
        candidates = [i for i in range(number_of - 1) if given[i] < bound]
        mass, left = sum([portions[i] for i in candidates]), spare
        for i in candidates:
            addition = min(bound - given[i], max(1, left * portions[i] // mass), spare)
            given[i] = given[i] + addition
            spare = spare - addition
    return np.array([bound] + given)


def uneven_parts(stream_key, count, total, reach, lean):
    if count == 2:
        one = jax.random.randint(stream_key, (), max(1, total - reach), min(reach, total - 1) + 1)
        return jnp.stack([one, total - one])
    tallies = jnp.asarray(profile(count, total, reach, lean), jnp.int32)
    twos = (count - 1) // 2
    donor, sink = tallies[1:1 + 2 * twos:2], tallies[2:2 + 2 * twos:2]
    room = jnp.minimum(donor - 1, reach - sink)
    moved = jax.random.randint(jax.random.fold_in(stream_key, 1), (twos,), 0, 1 << 20) % (room + 1)
    tallies = tallies.at[1:1 + 2 * twos:2].set(donor - moved).at[2:2 + 2 * twos:2].set(sink + moved)
    return tallies[jax.random.permutation(jax.random.fold_in(stream_key, 2), count)]


def noise(stream_key, shape, scale, limit, pieces=(), kind=jnp.bfloat16):
    array = jax.random.normal(stream_key, shape, jnp.float32) * scale
    if len(pieces) > 0:
        array = block_scale(stream_key, shape, pieces, -0.22, 0.18) * array
    return jnp.clip(array, min=-limit, max=limit).astype(kind)


def setup_inputs(seed: int = 0) -> dict:
    key_list = jax.random.split(jax.random.key(seed), 29)
    tokens = noise(key_list[0], (ROWS, LEN, D), 1.0, 6.0, ((0, 8),))
    segment_ids = jax.vmap(lambda own: jnp.searchsorted(jnp.cumsum(uneven_parts(own, 4, LEN, LEN // 2, 1)), jnp.arange(LEN), side="right"))(jax.random.split(key_list[1], ROWS)).reshape((ROWS, LEN)).astype(jnp.int32)
    pad_lengths = place_ends(jax.random.randint(key_list[2], (ROWS,), 0, LEN // 4), jax.random.fold_in(key_list[2], 1), 0, (LEN // 4) - 1).astype(jnp.int32)
    cotangent = noise(key_list[3], (ROWS, LEN, D), 1.0, 6.0, ((0, 8),))
    w_qkv = noise(key_list[4], (D, 3, D), D ** -0.5, 0.25, ((0, 8), (2, 4)), jnp.float32)
    w_out = noise(key_list[5], (D, D), (D // 64) ** -0.5, 2.0, ((0, 4), (1, 8)), jnp.float32)
    w_up = noise(key_list[6], (D, FF), D ** -0.5, 0.25, ((0, 8), (1, 4)), jnp.float32)
    w_down = noise(key_list[7], (FF, D), FF ** -0.5, 0.125, ((0, 4), (1, 8)), jnp.float32)
    qv_bias = noise(key_list[8], (2, HEADS, HEAD_DIM), 0.5, 3.0, ((1, 4), (2, 8)), jnp.float32)
    ff_bias = noise(key_list[9], (FF // HEAD_DIM, HEAD_DIM), 0.5, 3.0, ((0, 4), (1, 8)), jnp.float32)
    norm_gains = jnp.clip(1.0 + 0.1 * jax.random.normal(key_list[10], (2, D), jnp.float32), 0.5, 1.5)
    norm_shifts = noise(key_list[11], (4, D), 0.3, 2.0, ((1, 8),), jnp.float32)
    first_qkv = noise(key_list[12], (D, 3, D), (0.055 * TOKENS ** 0.5), 64.0, ((0, 8), (2, 4)), jnp.float32)
    first_out = noise(key_list[13], (D, D), (0.055 * TOKENS ** 0.5), 64.0, ((0, 4), (1, 8)), jnp.float32)
    first_up = noise(key_list[14], (D, FF), (0.055 * TOKENS ** 0.5), 64.0, ((0, 8), (1, 4)), jnp.float32)
    first_down = noise(key_list[15], (FF, D), (0.055 * TOKENS ** 0.5), 64.0, ((0, 4), (1, 8)), jnp.float32)
    first_qv_bias = noise(key_list[16], (2, HEADS, HEAD_DIM), (0.055 * TOKENS ** 0.5), 64.0, ((1, 4), (2, 8)), jnp.float32)
    first_ff_bias = noise(key_list[17], (FF // HEAD_DIM, HEAD_DIM), (0.055 * TOKENS ** 0.5), 64.0, ((0, 4), (1, 8)), jnp.float32)
    first_gains = noise(key_list[18], (2, D), (0.055 * TOKENS ** 0.5), 64.0, ((1, 8),), jnp.float32)
    first_shifts = noise(key_list[19], (4, D), (0.055 * TOKENS ** 0.5), 64.0, ((1, 8),), jnp.float32)
    second_qkv = jnp.clip(jnp.exp(math.log(32.768) - 1.3862944 * jax.random.uniform(key_list[20], (D, 3, D), jnp.float32) ** block_scale(key_list[20], (D, 3, D), ((0, 8), (2, 4)), -0.2, 0.2)), 8.192, 32.768)
    second_out = jnp.clip(jnp.exp(math.log(32.768) - 1.3862944 * jax.random.uniform(key_list[21], (D, D), jnp.float32) ** block_scale(key_list[21], (D, D), ((0, 4), (1, 8)), -0.2, 0.2)), 8.192, 32.768)
    second_up = jnp.clip(jnp.exp(math.log(32.768) - 1.3862944 * jax.random.uniform(key_list[22], (D, FF), jnp.float32) ** block_scale(key_list[22], (D, FF), ((0, 8), (1, 4)), -0.2, 0.2)), 8.192, 32.768)
    second_down = jnp.clip(jnp.exp(math.log(32.768) - 1.3862944 * jax.random.uniform(key_list[23], (FF, D), jnp.float32) ** block_scale(key_list[23], (FF, D), ((0, 4), (1, 8)), -0.2, 0.2)), 8.192, 32.768)
    second_qv_bias = jnp.clip(jnp.exp(math.log(32.768) - 1.3862944 * jax.random.uniform(key_list[24], (2, HEADS, HEAD_DIM), jnp.float32) ** block_scale(key_list[24], (2, HEADS, HEAD_DIM), ((1, 4), (2, 8)), -0.2, 0.2)), 8.192, 32.768)
    second_ff_bias = jnp.clip(jnp.exp(math.log(32.768) - 1.3862944 * jax.random.uniform(key_list[25], (FF // HEAD_DIM, HEAD_DIM), jnp.float32) ** block_scale(key_list[25], (FF // HEAD_DIM, HEAD_DIM), ((0, 4), (1, 8)), -0.2, 0.2)), 8.192, 32.768)
    second_gains = jnp.clip(jnp.exp(math.log(32.768) - 1.3862944 * jax.random.uniform(key_list[26], (2, D), jnp.float32) ** block_scale(key_list[26], (2, D), ((1, 8),), -0.2, 0.2)), 8.192, 32.768)
    second_shifts = jnp.clip(jnp.exp(math.log(32.768) - 1.3862944 * jax.random.uniform(key_list[27], (4, D), jnp.float32) ** block_scale(key_list[27], (4, D), ((1, 8),), -0.2, 0.2)), 8.192, 32.768)
    return {"tokens": tokens, "segment_ids": segment_ids, "pad_lengths": pad_lengths, "cotangent": cotangent, "w_qkv": w_qkv, "w_out": w_out, "w_up": w_up, "w_down": w_down, "qv_bias": qv_bias, "ff_bias": ff_bias, "norm_gains": norm_gains, "norm_shifts": norm_shifts, "first_qkv": first_qkv, "first_out": first_out, "first_up": first_up, "first_down": first_down, "first_qv_bias": first_qv_bias, "first_ff_bias": first_ff_bias, "first_gains": first_gains, "first_shifts": first_shifts, "second_qkv": second_qkv, "second_out": second_out, "second_up": second_up, "second_down": second_down, "second_qv_bias": second_qv_bias, "second_ff_bias": second_ff_bias, "second_gains": second_gains, "second_shifts": second_shifts}


@jax.custom_vjp
def low(v):
    return lax.optimization_barrier(v.astype(jnp.bfloat16)).astype(jnp.float32)

@jax.custom_vjp
def low_back(v):
    return v

def low_keep(v):
    return (low(v), None)

def low_pass(kept, grad):
    return (grad,)

def back_keep(v):
    return (v, None)

def back_low(kept, grad):
    return (low(grad),)
low.defvjp(low_keep, low_pass)
low_back.defvjp(back_keep, back_low)
beta_one = 0.9
beta_two = 0.999
highest = lax.Precision.HIGHEST

def rounded(value):
    return low(low_back(value))

def gelu_exact(value):
    return value * 0.5 * (1.0 + lax.erf(value * 0.7071067811865476))

def norm_rows(value, gain, shift):
    center = value - lax.optimization_barrier(jnp.mean(value, axis=-1, keepdims=True))
    spread = lax.optimization_barrier(jnp.mean(center * center, axis=-1, keepdims=True))
    return center * lax.rsqrt(spread + 1e-05) * gain + shift

def attend_block(block_q, keys_all, values_all, seg_rows, valid_len, offset):
    raw_scores = jnp.einsum('gqhd,gkhd->ghqk', block_q, keys_all, precision=highest)
    scores = low_back(raw_scores) * 0.125
    query_seg = lax.dynamic_slice_in_dim(seg_rows, offset, QBLOCK, 1)
    query_pos = offset + jnp.arange(QBLOCK, dtype=jnp.int32)
    key_pos = jnp.arange(LEN, dtype=jnp.int32)
    same_segment = query_seg[:, :, None] == seg_rows[:, None, :]
    inside = key_pos[None, None, :] < valid_len[:, None, None]
    itself = query_pos[:, None] == key_pos[None, :]
    allowed = same_segment & inside | itself[None]
    scores = jnp.where(allowed[:, None], scores, -1e+30)
    probs_full = jax.nn.softmax(scores, axis=-1)
    return jnp.einsum('ghqk,gkhd->gqhd', low(probs_full), values_all, precision=highest)

def forward(token_rows, params, seg_rows, valid_len):
    qkv_low, out_low, up_low, down_low, bias_low, ff_low, gain_low, shift_low = [low(param) for param in params]
    groups = token_rows.shape[0]
    flat_rows = token_rows.reshape(groups * LEN, D)
    projected = jnp.dot(flat_rows, qkv_low.reshape(D, 3 * D), precision=highest).reshape(groups, LEN, 3, HEADS, HEAD_DIM)
    queries = rounded(projected[:, :, 0] + bias_low[0])
    keys_all = rounded(projected[:, :, 1])
    values_all = rounded(projected[:, :, 2] + bias_low[1])

    def one_block(offset):
        block_q = lax.dynamic_slice_in_dim(queries, offset, QBLOCK, 1)
        return attend_block(block_q, keys_all, values_all, seg_rows, valid_len, offset)
    offsets = jnp.arange(LEN // QBLOCK, dtype=jnp.int32) * QBLOCK
    mixed_heads = lax.map(jax.checkpoint(one_block), offsets)
    heads_out = rounded(jnp.moveaxis(mixed_heads, 0, 1).reshape(groups * LEN, D))
    attention = low_back(jnp.dot(heads_out, out_low, precision=highest)) + shift_low[0]
    normed = norm_rows(flat_rows + attention, gain_low[0], shift_low[2])
    pre_act = low_back(jnp.dot(low(normed), up_low, precision=highest) + ff_low.reshape(FF))
    hidden = low(gelu_exact(pre_act))
    branch = low_back(jnp.dot(hidden, down_low, precision=highest)) + shift_low[1]
    return norm_rows(normed + branch, gain_low[1], shift_low[3]).reshape(groups, LEN, D)

def adam_step(weight, grad_sum, first, second, rate, decay):
    first_new = beta_one * first + (1.0 - beta_one) * grad_sum
    second_new = beta_two * second + (1.0 - beta_two) * grad_sum * grad_sum
    first_hat = first_new / (1.0 - beta_one ** STEP)
    second_hat = second_new / (1.0 - beta_two ** STEP)
    weight_new = weight - rate * (first_hat / (jnp.sqrt(second_hat) + 1e-08) + decay * weight)
    return (weight_new, first_new, second_new)

def reference(tokens, segment_ids, pad_lengths, cotangent, w_qkv, w_out, w_up, w_down, qv_bias, ff_bias, norm_gains, norm_shifts, first_qkv, first_out, first_up, first_down, first_qv_bias, first_ff_bias, first_gains, first_shifts, second_qkv, second_out, second_up, second_down, second_qv_bias, second_ff_bias, second_gains, second_shifts):
    params = (w_qkv, w_out, w_up, w_down, qv_bias, ff_bias, norm_gains, norm_shifts)
    rows_all = tokens.shape[0]
    group_rows = 2
    steps_all = rows_all // group_rows

    def one_group(summed, position):
        offset = position * group_rows
        token_rows = lax.dynamic_slice_in_dim(tokens, offset, group_rows, 0).astype(jnp.float32)
        seg_rows = lax.dynamic_slice_in_dim(segment_ids, offset, group_rows, 0)
        valid_len = LEN - lax.dynamic_slice_in_dim(pad_lengths, offset, group_rows, 0)
        back_rows = lax.dynamic_slice_in_dim(cotangent, offset, group_rows, 0).astype(jnp.float32)

        def run_layer(token_in, weights):
            return forward(token_in, weights, seg_rows, valid_len)
        result, pullback = jax.vjp(run_layer, token_rows, params)
        token_grad, param_grads = pullback(back_rows)
        summed = tuple((earlier + fresh_part for earlier, fresh_part in zip(summed, param_grads)))
        return (summed, (result.astype(jnp.bfloat16), token_grad))
    zeros_init = tuple((jnp.zeros_like(param) for param in params))
    grad_sums, (layer_rows, grad_rows) = lax.scan(one_group, zeros_init, jnp.arange(steps_all, dtype=jnp.int32))
    layer_out = layer_rows.reshape(rows_all, LEN, D)
    tokens_grad = grad_rows.reshape(rows_all, LEN, D)
    step_rates = (D ** (-0.5), (D // 64) ** (-0.5), D ** (-0.5), FF ** (-0.5), 0.3, 0.3, 0.3, 0.3)
    decays = (0.01, 0.01, 0.01, 0.01, 0.0, 0.0, 0.0, 0.0)
    firsts = (first_qkv, first_out, first_up, first_down, first_qv_bias, first_ff_bias, first_gains, first_shifts)
    seconds = (second_qkv, second_out, second_up, second_down, second_qv_bias, second_ff_bias, second_gains, second_shifts)
    updated = [adam_step(params[slot], grad_sums[slot], firsts[slot], seconds[slot], step_rates[slot], decays[slot]) for slot in range(8)]
    return (layer_out, tokens_grad, updated[0][0], updated[1][0], updated[2][0], updated[3][0], updated[4][0], updated[5][0], updated[6][0], updated[7][0], updated[0][1], updated[1][1], updated[2][1], updated[3][1], updated[4][1], updated[5][1], updated[6][1], updated[7][1], updated[0][2], updated[1][2], updated[2][2], updated[3][2], updated[4][2], updated[5][2], updated[6][2], updated[7][2])
```

```python
import functools

import jax
import jax.numpy as jnp
from jax import lax
from jax.experimental import pallas as pl
from jax.experimental.pallas import tpu as pltpu
from jax.sharding import PartitionSpec as P

D = 512
HEADS = 8
HEAD_DIM = 64
FF = 2048
LEN = 1024
STEP = 10
PAIR = 128
TILE = 256
FAR = 1e30

beta_one = 0.9
beta_two = 0.999
BF = jnp.bfloat16
F32 = jnp.float32
NN = (((1,), (0,)), ((), ()))
NT = (((1,), (1,)), ((), ()))


def dot(a, b, dims=NN):
    return lax.dot_general(a, b, dims, preferred_element_type=F32)


def vmem(mib):
    return pltpu.CompilerParams(
        dimension_semantics=("arbitrary",), vmem_limit_bytes=mib * 1024 * 1024
    )


def flip(value, axis, bit):
    size = lax.axis_size(axis)
    return lax.ppermute(value, axis, [(i, i ^ bit) for i in range(size)])


def bits(size):
    out, bit = [], 1
    while bit < size:
        out.append(bit)
        bit *= 2
    return out


def gather_all(part, steps):
    held = part[None]
    for axis, bit in steps:
        held = jnp.concatenate([held, flip(held, axis, bit)], axis=0)
    return held


def reduce_all(parts, steps):
    held = parts
    for axis, bit in reversed(steps):
        half = held.shape[0] // 2
        came = flip(held[half:], axis, bit)
        held = (held[:half].astype(F32) + came.astype(F32)).astype(BF)
    return held[0]


def dp_order(steps):
    marks = [bit for axis, bit in steps if axis == "dp"]
    return [
        sum(bit for k, bit in enumerate(marks) if (j >> k) & 1) for j in range(2 ** len(marks))
    ]


def rows_at(order, j, my_dp, span):
    return pl.ds(pl.multiple_of((order[j] ^ my_dp) * span, span), span)


def head_mask(shape, head):
    lane = lax.broadcasted_iota(jnp.int32, shape, 1)
    return (lane < HEAD_DIM) if head == 0 else (lane >= HEAD_DIM)


def attend_kernel(
    order, ids, x_ref, w_ref, bias_ref, qf_ref, kf_ref, q_ref, k_ref, v_ref, ho_ref, lse_ref,
    w_all, keys, vals_t,
):
    my_dp = ids[2]
    span = w_ref.shape[2]
    for j in range(len(order)):
        w_all[rows_at(order, j, my_dp, span), :] = w_ref[j, 0]

    @pl.when(pl.program_id(0) == 0)
    def _():
        keys[:, PAIR:] = kf_ref[0]

    for t in range(LEN // TILE):
        at = slice(t * TILE, (t + 1) * TILE)
        got = dot(x_ref[0, at], w_all[...])
        q_ref[0, at] = (got[:, :PAIR] + bias_ref[0, 0:1]).astype(BF)
        key = got[:, PAIR : 2 * PAIR].astype(BF)
        k_ref[0, at] = key
        keys[at, :PAIR] = key
        val = (got[:, 2 * PAIR :] + bias_ref[0, 1:2]).astype(BF)
        v_ref[0, at] = val
        vals_t[:, at] = val.T

    for t in range(LEN // TILE):
        at = slice(t * TILE, (t + 1) * TILE)
        query = q_ref[0, at] * BF(0.125)
        mixed = []
        for head in range(2):
            mine = jnp.where(head_mask((TILE, PAIR), head), query, BF(0))
            wide = jnp.concatenate([mine, qf_ref[0, at]], axis=1)
            scores = dot(keys[...], wide, NT)
            top = jnp.max(scores, axis=0, keepdims=True)
            probs = jnp.exp(scores - top)
            total = jnp.sum(probs, axis=0, keepdims=True)
            lse_ref[0, head : head + 1, at] = top + jnp.log(total)
            out = dot(vals_t[head * HEAD_DIM : (head + 1) * HEAD_DIM, :], probs.astype(BF))
            mixed.append(out * (1.0 / total))
        ho_ref[at, :] = jnp.concatenate(mixed, axis=0).T.astype(BF)


def attend(ids, tokens, w_parts, bias, qf, kf, order):
    groups = w_parts.shape[1]
    n_dp, span = len(order), w_parts.shape[2]
    pair = pl.BlockSpec((1, LEN, PAIR), lambda g, ids: (g, 0, 0))
    feats = pl.BlockSpec((1, LEN, PAIR), lambda g, ids: (ids[0], 0, 0))
    return pl.pallas_call(
        functools.partial(attend_kernel, order),
        grid_spec=pltpu.PrefetchScalarGridSpec(
            num_scalar_prefetch=1,
            grid=(groups,),
            in_specs=[
                pl.BlockSpec((1, LEN, D), lambda g, ids: (ids[0], 0, 0)),
                pl.BlockSpec((n_dp, 1, span, 3 * PAIR), lambda g, ids: (0, g, 0, 0)),
                pl.BlockSpec((1, 2, PAIR), lambda g, ids: (g ^ ids[1], 0, 0)),
                feats,
                feats,
            ],
            out_specs=[
                pair,
                pair,
                pair,
                pl.BlockSpec((LEN, PAIR), lambda g, ids: (0, g ^ ids[1])),
                pl.BlockSpec((1, 2, LEN), lambda g, ids: (g, 0, 0)),
            ],
            scratch_shapes=[
                pltpu.VMEM((D, 3 * PAIR), BF),
                pltpu.VMEM((LEN, 2 * PAIR), BF),
                pltpu.VMEM((PAIR, LEN), BF),
            ],
        ),
        out_shape=[
            jax.ShapeDtypeStruct((groups, LEN, PAIR), BF),
            jax.ShapeDtypeStruct((groups, LEN, PAIR), BF),
            jax.ShapeDtypeStruct((groups, LEN, PAIR), BF),
            jax.ShapeDtypeStruct((LEN, D), BF),
            jax.ShapeDtypeStruct((groups, 2, LEN), F32),
        ],
        compiler_params=vmem(48),
        cost_estimate=pl.CostEstimate(
            flops=10_000_000_000, bytes_accessed=8_000_000, transcendentals=8_400_000
        ),
        name="attend",
    )(ids, tokens, w_parts, bias, qf, kf)


def norm_stats(value):
    center = value - jnp.mean(value, axis=-1, keepdims=True)
    spread = jnp.mean(center * center, axis=-1, keepdims=True)
    inverse = lax.rsqrt(spread + 1e-05)
    return center * inverse, inverse


def norm_backward(upstream, normal, inverse, gain):
    scaled = upstream * gain
    return inverse * (
        scaled
        - jnp.mean(scaled, axis=-1, keepdims=True)
        - normal * jnp.mean(scaled * normal, axis=-1, keepdims=True)
    )


def tokenwise_kernel(
    order_a, order_b, keep, ids, x_ref, ho_ref, cot_ref, wa_ref, wb_ref, par_ref, ffb_ref, *rest
):
    if keep:
        (out_ref, gatt_ref, gh_ref, hid_ref, gpre_ref, low_ref, sums_ref, ffs_ref,
         w_out, w_up, w_down, slope, acc) = rest
    else:
        (out_ref, gatt_ref, gh_ref, w_out, w_up, w_down, slope, hid_ref) = rest
    my_mp, my_dp = ids[1], ids[2]
    step = pl.program_id(0)
    span = wa_ref.shape[2]
    groups = wa_ref.shape[1]
    wide = FF // groups

    @pl.when(step == 0)
    def _():
        for g in range(groups):
            col = g ^ my_mp
            narrow_at = pl.ds(pl.multiple_of(col * PAIR, PAIR), PAIR)
            wide_at = pl.ds(pl.multiple_of(col * wide, wide), wide)
            for j in range(len(order_a)):
                row = rows_at(order_a, j, my_dp, span)
                w_out[row, narrow_at] = wa_ref[j, g, :, :PAIR]
                w_up[row, wide_at] = wa_ref[j, g, :, PAIR:]
            for j in range(len(order_b)):
                w_down[rows_at(order_b, j, my_dp, span), wide_at] = wb_ref[j, g]

    gain_one, gain_two = par_ref[0:1], par_ref[1:2]
    shift_att, shift_ffn, shift_one, shift_two = (par_ref[k : k + 1] for k in range(2, 6))
    attention = dot(ho_ref[...], w_out[...], NT) + shift_att
    normal_one, inverse_one = norm_stats(x_ref[0].astype(F32) + attention)
    normed = normal_one * gain_one + shift_one
    normed_low = normed.astype(BF)
    branch = shift_ffn
    chunk = 512
    for c in range(FF // chunk):
        at = slice(c * chunk, (c + 1) * chunk)
        pre = dot(normed_low, w_up[:, at]) + ffb_ref[:, at]
        phi = 0.5 * (1.0 + lax.erf(pre * 0.7071067811865476))
        hidden = (pre * phi).astype(BF)
        hid_ref[:, at] = hidden
        slope[:, at] = phi + pre * jnp.exp(-0.5 * pre * pre) * 0.3989422804014327
        branch = branch + dot(hidden, w_down[:, at], NT)
    normal_two, inverse_two = norm_stats(normed + branch)
    out_ref[...] = (normal_two * gain_two + shift_two).astype(BF)
    upstream = cot_ref[0].astype(F32)
    g_final = norm_backward(upstream, normal_two, inverse_two, gain_two)
    g_final_low = g_final.astype(BF)
    g_normed = g_final
    for c in range(FF // chunk):
        at = slice(c * chunk, (c + 1) * chunk)
        g_pre = (dot(g_final_low, w_down[:, at]) * slope[:, at]).astype(BF)
        if keep:
            gpre_ref[:, at] = g_pre
            here = jnp.sum(g_pre.astype(F32), axis=0, keepdims=True)

            @pl.when(step == 0)
            def _(at=at, here=here):
                ffs_ref[:, at] = here

            @pl.when(step > 0)
            def _(at=at, here=here):
                ffs_ref[:, at] += here

        g_normed = g_normed + dot(g_pre, w_up[:, at], NT)
    g_attention = norm_backward(g_normed, normal_one, inverse_one, gain_one)
    g_attention_low = g_attention.astype(BF)
    gatt_ref[...] = g_attention
    gh_ref[...] = dot(g_attention_low, w_out[...]).astype(BF)
    if keep:
        low_ref[0] = normed_low
        low_ref[1] = g_final_low
        low_ref[2] = g_attention_low
        terms = (g_normed * normal_one, upstream * normal_two, g_attention, g_final, g_normed, upstream)
        for k, term in enumerate(terms):
            part = jnp.sum(term.reshape(TILE // 8, 8, D), axis=0)

            @pl.when(step == 0)
            def _(k=k, part=part):
                acc[k] = part

            @pl.when(step > 0)
            def _(k=k, part=part):
                acc[k] += part

        @pl.when(step == pl.num_programs(0) - 1)
        def _():
            for k in range(6):
                sums_ref[k : k + 1] = jnp.sum(acc[k], axis=0, keepdims=True)


def tokenwise(ids, tokens, heads_out, cotangent, wa, wb, params, ff_shift, order_a, order_b, keep):
    full = lambda shape: pl.BlockSpec(shape, lambda t, ids: (0,) * len(shape))
    row = pl.BlockSpec((1, TILE, D), lambda t, ids: (ids[0], t, 0))
    flat = pl.BlockSpec((TILE, D), lambda t, ids: (t, 0))
    broad = pl.BlockSpec((TILE, FF), lambda t, ids: (t, 0))
    out_specs = [flat, flat, flat]
    out_shape = [
        jax.ShapeDtypeStruct((LEN, D), BF),
        jax.ShapeDtypeStruct((LEN, D), F32),
        jax.ShapeDtypeStruct((LEN, D), BF),
    ]
    scratch = [
        pltpu.VMEM((D, D), BF),
        pltpu.VMEM((D, FF), BF),
        pltpu.VMEM((D, FF), BF),
        pltpu.VMEM((TILE, FF), F32),
    ]
    if keep:
        out_specs += [broad, broad, pl.BlockSpec((3, TILE, D), lambda t, ids: (0, t, 0)), full((6, D)), full((1, FF))]
        out_shape += [
            jax.ShapeDtypeStruct((LEN, FF), BF),
            jax.ShapeDtypeStruct((LEN, FF), BF),
            jax.ShapeDtypeStruct((3, LEN, D), BF),
            jax.ShapeDtypeStruct((6, D), F32),
            jax.ShapeDtypeStruct((1, FF), F32),
        ]
        scratch += [pltpu.VMEM((6, 8, D), F32)]
    else:
        scratch += [pltpu.VMEM((TILE, FF), BF)]
    return pl.pallas_call(
        functools.partial(tokenwise_kernel, order_a, order_b, keep),
        grid_spec=pltpu.PrefetchScalarGridSpec(
            num_scalar_prefetch=1,
            grid=(LEN // TILE,),
            in_specs=[row, flat, row, full(wa.shape), full(wb.shape), full((6, D)), full((1, FF))],
            out_specs=out_specs,
            scratch_shapes=scratch,
        ),
        out_shape=out_shape,
        compiler_params=vmem(48),
        cost_estimate=pl.CostEstimate(
            flops=14_000_000_000, bytes_accessed=20_000_000, transcendentals=4_200_000
        ),
        name="tokenwise_keep" if keep else "tokenwise",
    )(ids, tokens, heads_out, cotangent, wa, wb, params, ff_shift)


def turned(source, order, my_dp, tall, tmp):
    tmp[...] = source.T
    span = D // len(order)
    for j in range(len(order)):
        tall[j * span : (j + 1) * span, :] = tmp[rows_at(order, j, my_dp, span), :]


def weight_kernel(order_a, order_b, ids, low_ref, ho_ref, hid_ref, gpre_ref, ga_ref, gb_ref, up_t, down_t, att_t, tmp):
    my_dp = ids[2]

    @pl.when(pl.program_id(0) == 0)
    def _():
        turned(low_ref[0], order_a, my_dp, up_t, tmp)
        turned(low_ref[1], order_b, my_dp, down_t, tmp)
        turned(low_ref[2], order_a, my_dp, att_t, tmp)

    n_a, n_b = len(order_a), len(order_b)
    ga_ref[:, 0, :, :PAIR] = dot(att_t[...], ho_ref[...]).astype(BF).reshape(n_a, D // n_a, PAIR)
    wide = gpre_ref.shape[1]
    ga_ref[:, 0, :, PAIR:] = dot(up_t[...], gpre_ref[...]).astype(BF).reshape(n_a, D // n_a, wide)
    gb_ref[:, 0] = dot(down_t[...], hid_ref[...]).astype(BF).reshape(n_b, D // n_b, wide)


def weight_grads(ids, lows, heads_out, hidden, g_pre, groups, order_a, order_b):
    wide = FF // groups
    n_a, n_b = len(order_a), len(order_b)
    broad = pl.BlockSpec((LEN, wide), lambda g, ids: (0, g ^ ids[1]))
    return pl.pallas_call(
        functools.partial(weight_kernel, order_a, order_b),
        grid_spec=pltpu.PrefetchScalarGridSpec(
            num_scalar_prefetch=1,
            grid=(groups,),
            in_specs=[
                pl.BlockSpec((3, LEN, D), lambda g, ids: (0, 0, 0)),
                pl.BlockSpec((LEN, PAIR), lambda g, ids: (0, g ^ ids[1])),
                broad,
                broad,
            ],
            out_specs=[
                pl.BlockSpec((n_a, 1, D // n_a, PAIR + wide), lambda g, ids: (0, g, 0, 0)),
                pl.BlockSpec((n_b, 1, D // n_b, wide), lambda g, ids: (0, g, 0, 0)),
            ],
            scratch_shapes=[pltpu.VMEM((D, LEN), BF)] * 4,
        ),
        out_shape=[
            jax.ShapeDtypeStruct((n_a, groups, D // n_a, PAIR + wide), BF),
            jax.ShapeDtypeStruct((n_b, groups, D // n_b, wide), BF),
        ],
        compiler_params=vmem(48),
        cost_estimate=pl.CostEstimate(
            flops=5_000_000_000, bytes_accessed=17_000_000, transcendentals=0
        ),
        name="weight_grads",
    )(ids, lows, heads_out, hidden, g_pre)


def attend_back_kernel(
    order, keep, ids, x_ref, w_ref, qf_ref, kf_ref, q_ref, k_ref, v_ref, ho_ref, lse_ref, gh_ref, gatt_ref, *rest
):
    if keep:
        (tg_ref, gw_ref, gb_ref, w_all, keys, keys_t, delta, dk, dv, grads, x_t, tmp) = rest
    else:
        (tg_ref, w_all, keys, keys_t, delta, dk, dv, grads) = rest
    my_dp = ids[2]
    span = w_ref.shape[2]
    for j in range(len(order)):
        w_all[rows_at(order, j, my_dp, span), :] = w_ref[j, 0]

    @pl.when(pl.program_id(0) == 0)
    def _():
        keys[:, PAIR:] = kf_ref[0]
        tg_ref[...] = gatt_ref[...]
        if keep:
            turned(x_ref[0], order, my_dp, x_t, tmp)

    keys[:, :PAIR] = k_ref[0]
    keys_t[...] = k_ref[0].T
    prod = (gh_ref[...].astype(F32) * ho_ref[...].astype(F32)).T
    delta[0:1] = jnp.sum(prod[:HEAD_DIM], axis=0, keepdims=True)
    delta[1:2] = jnp.sum(prod[HEAD_DIM:], axis=0, keepdims=True)
    dk[...] = jnp.zeros_like(dk)
    dv[...] = jnp.zeros_like(dv)
    for t in range(LEN // TILE):
        at = slice(t * TILE, (t + 1) * TILE)
        query, back = q_ref[0, at], gh_ref[at, :]
        d_query = []
        for head in range(2):
            mask = head_mask((TILE, PAIR), head)
            mine = jnp.where(mask, query, BF(0))
            wide = jnp.concatenate([mine * BF(0.125), qf_ref[0, at]], axis=1)
            own_back = jnp.where(mask, back, BF(0))
            lse, row = lse_ref[0, head : head + 1, at], delta[head : head + 1, at]
            total = None
            for s in range(LEN // TILE):
                kat = slice(s * TILE, (s + 1) * TILE)
                probs = jnp.exp(dot(keys[kat, :], wide, NT) - lse)
                g_probs = dot(v_ref[0, kat], own_back, NT)
                g_raw = (probs * (g_probs - row)).astype(BF)
                dv[kat, :] += dot(probs.astype(BF), own_back)
                dk[kat, :] += dot(g_raw, mine)
                part = dot(keys_t[head * HEAD_DIM : (head + 1) * HEAD_DIM, kat], g_raw)
                total = part if total is None else total + part
            d_query.append(total)
        grads[at, :PAIR] = (jnp.concatenate(d_query, axis=0).T * 0.125).astype(BF)
    grads[:, PAIR : 2 * PAIR] = (dk[...] * 0.125).astype(BF)
    grads[:, 2 * PAIR :] = dv[...].astype(BF)
    for t in range(LEN // TILE):
        at = slice(t * TILE, (t + 1) * TILE)
        tg_ref[at, :] += dot(grads[at, :], w_all[...], NT)
    if keep:
        n = len(order)
        gw_ref[:, 0] = dot(x_t[...], grads[...]).astype(BF).reshape(n, D // n, 3 * PAIR)
        gb_ref[0, 0:1] = jnp.sum(grads[:, :PAIR].astype(F32), axis=0, keepdims=True)
        gb_ref[0, 1:2] = jnp.sum(grads[:, 2 * PAIR :].astype(F32), axis=0, keepdims=True)


def attend_back(ids, tokens, w_parts, qf, kf, q, k, v, heads_out, lse, g_heads, g_att, order, keep):
    groups = w_parts.shape[1]
    n_dp, span = len(order), w_parts.shape[2]
    pair = pl.BlockSpec((1, LEN, PAIR), lambda g, ids: (g, 0, 0))
    feats = pl.BlockSpec((1, LEN, PAIR), lambda g, ids: (ids[0], 0, 0))
    column = pl.BlockSpec((LEN, PAIR), lambda g, ids: (0, g ^ ids[1]))
    full = pl.BlockSpec((LEN, D), lambda g, ids: (0, 0))
    part = pl.BlockSpec((n_dp, 1, span, 3 * PAIR), lambda g, ids: (0, g, 0, 0))
    out_specs, out_shape = [full], [jax.ShapeDtypeStruct((LEN, D), F32)]
    scratch = [
        pltpu.VMEM((D, 3 * PAIR), BF),
        pltpu.VMEM((LEN, 2 * PAIR), BF),
        pltpu.VMEM((PAIR, LEN), BF),
        pltpu.VMEM((2, LEN), F32),
        pltpu.VMEM((LEN, PAIR), F32),
        pltpu.VMEM((LEN, PAIR), F32),
        pltpu.VMEM((LEN, 3 * PAIR), BF),
    ]
    if keep:
        out_specs += [part, pl.BlockSpec((1, 2, PAIR), lambda g, ids: (g ^ ids[1], 0, 0))]
        out_shape += [
            jax.ShapeDtypeStruct((n_dp, groups, span, 3 * PAIR), BF),
            jax.ShapeDtypeStruct((groups, 2, PAIR), F32),
        ]
        scratch += [pltpu.VMEM((D, LEN), BF)] * 2
    return pl.pallas_call(
        functools.partial(attend_back_kernel, order, keep),
        grid_spec=pltpu.PrefetchScalarGridSpec(
            num_scalar_prefetch=1,
            grid=(groups,),
            in_specs=[
                pl.BlockSpec((1, LEN, D), lambda g, ids: (ids[0], 0, 0)),
                part,
                feats,
                feats,
                pair,
                pair,
                pair,
                column,
                pl.BlockSpec((1, 2, LEN), lambda g, ids: (g, 0, 0)),
                column,
                full,
            ],
            out_specs=out_specs,
            scratch_shapes=scratch,
        ),
        out_shape=out_shape,
        compiler_params=vmem(48),
        cost_estimate=pl.CostEstimate(
            flops=20_000_000_000, bytes_accessed=12_000_000, transcendentals=8_400_000
        ),
        name="attend_back_keep" if keep else "attend_back",
    )(ids, tokens, w_parts, qf, kf, q, k, v, heads_out, lse, g_heads, g_att)


def adam_step(weight, grad_sum, first, second, rate, decay):
    first_new = beta_one * first + (1.0 - beta_one) * grad_sum
    second_new = beta_two * second + (1.0 - beta_two) * grad_sum * grad_sum
    first_hat = first_new / (1.0 - beta_one**STEP)
    second_hat = second_new / (1.0 - beta_two**STEP)
    weight_new = weight - rate * (first_hat / (jnp.sqrt(second_hat) + 1e-08) + decay * weight)
    return (weight_new, first_new, second_new)


def features(segment_ids, pad_lengths):
    place = jnp.arange(LEN, dtype=jnp.int32)[None, :, None]
    lane = jnp.arange(PAIR, dtype=jnp.int32)[None, None, :]
    segment = segment_ids[:, :, None]
    padding = place >= (LEN - pad_lengths)[:, None, None]
    high, low = place // 32, place % 32
    hit = (
        ((lane < 4) & (lane == segment))
        | ((lane >= 4) & (lane < 36) & (lane - 4 == high))
        | ((lane >= 36) & (lane < 68) & (lane - 36 == low))
    )
    counts = jnp.where(padding, (lane >= 4) & (lane < 68), lane < 4)
    qf = jnp.where(hit, -FAR, 0.0).astype(BF)
    kf = jnp.where(counts & ~hit, 1.0, 0.0).astype(BF)
    return qf, kf


def per_device(
    tokens, segment_ids, pad_lengths, cotangent,
    w_qkv, w_out, w_up, w_down, qv_bias, ff_bias, norm_gains, norm_shifts,
    first_qkv, first_out, first_up, first_down, first_qv_bias, first_ff_bias, first_gains, first_shifts,
    second_qkv, second_out, second_up, second_down, second_qv_bias, second_ff_bias, second_gains, second_shifts,
):
    n_dp, n_mp = lax.axis_size("dp"), lax.axis_size("mp")
    my_dp, my_mp = lax.axis_index("dp"), lax.axis_index("mp")
    mp_steps = [("mp", bit) for bit in bits(n_mp)]
    near, *far = [("dp", bit) for bit in bits(n_dp)]
    steps_a = mp_steps + far + [near]
    steps_b = mp_steps + far[::-1] + [near]
    order_a, order_b = dp_order(steps_a), dp_order(steps_b)
    span = D // n_dp

    part_qkv = w_qkv.astype(BF).reshape(span, 3 * PAIR)
    part_a = jnp.concatenate([w_out.T, w_up], axis=1).astype(BF)
    part_b = w_down.T.astype(BF)
    small = jnp.concatenate(
        [qv_bias.reshape(-1), ff_bias.reshape(-1), norm_gains.reshape(-1), norm_shifts.reshape(-1)]
    ).astype(BF)
    small_all = lax.all_gather(lax.all_gather(small, "dp", axis=0), "mp", axis=0).astype(F32)
    all_qkv = gather_all(part_qkv, steps_a).reshape(n_dp, n_mp, span, 3 * PAIR)
    all_a = gather_all(part_a, steps_a).reshape(n_dp, n_mp, span, -1)
    all_b = gather_all(part_b, steps_b).reshape(n_dp, n_mp, span, -1)

    cuts = [qv_bias.size, ff_bias.size, norm_gains.size, norm_shifts.size]
    ends = [sum(cuts[: k + 1]) for k in range(4)]
    bias_rows = (
        small_all[:, :, : ends[0]]
        .reshape(n_mp, n_dp, 2, 2, HEAD_DIM // n_dp)
        .transpose(0, 2, 3, 1, 4)
        .reshape(n_mp, 2, PAIR)
    )
    ff_shift = (
        small_all[:, :, ends[0] : ends[1]]
        .reshape(n_mp, n_dp, FF // HEAD_DIM // n_mp, HEAD_DIM // n_dp)
        .transpose(0, 2, 1, 3)
        .reshape(1, FF)
    )
    params = (
        small_all[0, :, ends[1] :]
        .reshape(n_dp, 6, span)
        .transpose(1, 0, 2)
        .reshape(6, D)
    )
    qf, kf = features(segment_ids, pad_lengths)

    def ids_of(row):
        return jnp.stack([row, my_mp, my_dp]).astype(jnp.int32)

    mine, other = ids_of(my_mp), ids_of(my_mp ^ 1)
    q, k, v, heads_out, lse = attend(mine, tokens, all_qkv, bias_rows, qf, kf, order_a)
    own_out, g_att, g_heads, hidden, g_pre, lows, sums, ff_sums = tokenwise(
        mine, tokens, heads_out, cotangent, all_a, all_b, params, ff_shift, order_a, order_b, True
    )
    grad_a, grad_b = weight_grads(mine, lows, heads_out, hidden, g_pre, n_mp, order_a, order_b)
    own_grad, grad_qkv, bias_sums = attend_back(
        mine, tokens, all_qkv, qf, kf, q, k, v, heads_out, lse, g_heads, g_att, order_a, True
    )
    q2, k2, v2, heads_out2, lse2 = attend(other, tokens, all_qkv, bias_rows, qf, kf, order_a)
    other_out, g_att2, g_heads2 = tokenwise(
        other, tokens, heads_out2, cotangent, all_a, all_b, params, ff_shift, order_a, order_b, False
    )
    (other_grad,) = attend_back(
        other, tokens, all_qkv, qf, kf, q2, k2, v2, heads_out2, lse2, g_heads2, g_att2, order_a, False
    )

    middle = (my_mp == 1) | (my_mp == 2)

    def spread(own):
        close = lax.ppermute(own, "mp", [(1, 2), (2, 1)])
        distant = lax.ppermute(own, "mp", [(3, 1), (0, 2)])
        close_on = lax.ppermute(close, "mp", [(1, 0), (2, 3)])
        distant_on = lax.ppermute(distant, "mp", [(1, 0), (2, 3)])
        return jnp.where(middle, close, close_on), jnp.where(middle, distant, distant_on)

    lower = my_mp < 2

    def place(own, other, close, distant):
        even = (my_mp % 2) == 0
        first, second = jnp.where(even, own, other), jnp.where(even, other, own)
        return jnp.stack(
            [
                jnp.where(lower, first, distant),
                jnp.where(lower, second, close),
                jnp.where(lower, close, first),
                jnp.where(lower, distant, second),
            ]
        )

    layer_out = place(own_out, other_out, *spread(own_out))
    close, distant = spread(own_grad.astype(BF))
    tokens_grad = place(own_grad, other_grad, close.astype(F32), distant.astype(F32))

    sum_a = reduce_all(grad_a.reshape(n_dp * n_mp, span, -1), steps_a).astype(F32)
    sum_b = reduce_all(grad_b.reshape(n_dp * n_mp, span, -1), steps_b).astype(F32)
    sum_qkv = reduce_all(grad_qkv.reshape(n_dp * n_mp, span, 3 * PAIR), steps_a).astype(F32)
    small_sum = lax.psum(
        jnp.concatenate([bias_sums.reshape(-1), ff_sums.reshape(-1), sums.reshape(-1)]),
        ("dp", "mp"),
    )
    at_bias = small_sum[: 2 * D].reshape(n_mp, 2, 2, n_dp, HEAD_DIM // n_dp)
    at_ff = small_sum[2 * D : 2 * D + FF].reshape(n_mp, FF // HEAD_DIM // n_mp, n_dp, HEAD_DIM // n_dp)
    at_norm = small_sum[2 * D + FF :].reshape(6, n_dp, span)
    pick = lambda a, axis, index: lax.dynamic_index_in_dim(a, index, axis, keepdims=False)
    norm_mine = pick(at_norm, 1, my_dp)
    final_grads = (
        sum_qkv.reshape(w_qkv.shape),
        sum_a[:, :PAIR].T,
        sum_a[:, PAIR:],
        sum_b.T,
        pick(pick(at_bias, 0, my_mp), 2, my_dp),
        pick(pick(at_ff, 0, my_mp), 1, my_dp),
        norm_mine[:2],
        norm_mine[2:],
    )
    masters = (w_qkv, w_out, w_up, w_down, qv_bias, ff_bias, norm_gains, norm_shifts)
    step_rates = (D ** (-0.5), (D // 64) ** (-0.5), D ** (-0.5), FF ** (-0.5), 0.3, 0.3, 0.3, 0.3)
    decays = (0.01, 0.01, 0.01, 0.01, 0.0, 0.0, 0.0, 0.0)
    firsts = (first_qkv, first_out, first_up, first_down, first_qv_bias, first_ff_bias, first_gains, first_shifts)
    seconds = (second_qkv, second_out, second_up, second_down, second_qv_bias, second_ff_bias, second_gains, second_shifts)
    updated = [
        adam_step(masters[s], final_grads[s], firsts[s], seconds[s], step_rates[s], decays[s])
        for s in range(8)
    ]
    return tuple(
        [layer_out, tokens_grad]
        + [entry[0] for entry in updated]
        + [entry[1] for entry in updated]
        + [entry[2] for entry in updated]
    )


def solution(mesh):
    weights = (
        P("dp", None, "mp"),
        P("mp", "dp"),
        P("dp", "mp"),
        P("mp", "dp"),
        P(None, "mp", "dp"),
        P("mp", "dp"),
        P(None, "dp"),
        P(None, "dp"),
    )
    rows = P("dp", None, None)
    return jax.shard_map(
        per_device,
        mesh=mesh,
        in_specs=(rows, P("dp", None), P("dp"), rows) + weights * 3,
        out_specs=(rows, rows) + weights * 3,
        check_vma=False,
    )
```

```python
import functools

import jax
import jax.numpy as jnp
from jax import lax
from jax.experimental import pallas as pl
from jax.experimental.pallas import tpu as pltpu
from jax.sharding import PartitionSpec as P

D = 512
HEADS = 8
HEAD_DIM = 64
FF = 2048
LEN = 1024
STEP = 10
PAIR = 128
TILE = 256
KEYS = 128
TOKENS_AT_ONCE = 512
FAR = 1e30
EXTRA = 16

beta_one = 0.9
beta_two = 0.999
BF = jnp.bfloat16
F32 = jnp.float32
NN = (((1,), (0,)), ((), ()))
NT = (((1,), (1,)), ((), ()))


def dot(a, b, dims=NN):
    return lax.dot_general(a, b, dims, preferred_element_type=F32)


def vmem(mib):
    return pltpu.CompilerParams(
        dimension_semantics=("arbitrary",), vmem_limit_bytes=mib * 1024 * 1024
    )


def kernel_call(kernel, ids, inputs, in_specs, after, carry, scratch, **kw):
    n, m, c = len(inputs), len(after), len(carry)
    grid, out_specs, mib = kw.pop("grid"), kw.pop("out_specs"), kw.pop("mib")
    outs = len(out_specs)

    def body(ids_ref, *refs):
        given, rest = refs[:n], refs[n + m + c :]
        kernel(ids_ref, *given, *rest[:outs], *rest[outs + c :])

    anywhere = pl.BlockSpec(memory_space=pl.ANY)
    return pl.pallas_call(
        body,
        grid_spec=pltpu.PrefetchScalarGridSpec(
            num_scalar_prefetch=1,
            grid=grid,
            in_specs=list(in_specs) + [anywhere] * (m + c),
            out_specs=list(out_specs) + [anywhere] * c,
            scratch_shapes=scratch,
        ),
        out_shape=list(kw.pop("out_shape")) + [jax.ShapeDtypeStruct(a.shape, a.dtype) for a in carry],
        input_output_aliases={1 + n + m + k: outs + k for k in range(c)},
        compiler_params=vmem(mib),
        cost_estimate=pl.CostEstimate(flops=20_000_000_000, bytes_accessed=1_000_000, transcendentals=0),
        **kw,
    )(ids, *inputs, *after, *carry)


def gate(values, *until):
    n = len(values)
    anywhere = pl.BlockSpec(memory_space=pl.ANY)
    return list(pl.pallas_call(
        lambda *refs: None,
        in_specs=[anywhere] * (n + len(until)),
        out_specs=[anywhere] * n,
        out_shape=[jax.ShapeDtypeStruct(a.shape, a.dtype) for a in values],
        input_output_aliases={k: k for k in range(n)},
        cost_estimate=pl.CostEstimate(flops=0, bytes_accessed=0, transcendentals=0),
        name="gate",
    )(*values, *until))


def flip(value, axis, bit):
    size = lax.axis_size(axis)
    return lax.ppermute(value, axis, [(i, i ^ bit) for i in range(size)])


def bits(size):
    out, bit = [], 1
    while bit < size:
        out.append(bit)
        bit *= 2
    return out


def combos(steps):
    return [sum(bit for k, bit in enumerate(steps) if (j >> k) & 1) for j in range(1, 2 ** len(steps))]


def routes(n_dp):
    near, *far = bits(n_dp)
    return near, [far[k : k + 2] for k in range(0, len(far), 2)]


def dp_order(n_dp):
    near, groups = routes(n_dp)
    order = [0]
    for group in groups:
        order = order + [x ^ y for y in combos(group) for x in order]
    return order + [x ^ near for x in order]


def gather_mp(part):
    return jnp.stack([part] + [flip(part, "mp", j) for j in range(1, lax.axis_size("mp"))])


def gather_mp_steps(part):
    n_mp = lax.axis_size("mp")
    held = {0: part}
    for bit in bits(n_mp)[::-1]:
        came = flip(jnp.stack([held[j] for j in sorted(held)]), "mp", bit)
        held.update({j ^ bit: came[k] for k, j in enumerate(sorted(held))})
    return jnp.stack([held[j] for j in range(n_mp)])


def gather_far(column):
    held = [column]
    for group in routes(lax.axis_size("dp"))[1]:
        held = held + [flip(a, "dp", y) for y in combos(group) for a in held]
    return held


def add_up(*terms):
    total = terms[0].astype(F32)
    for term in terms[1:]:
        total = total + term.astype(F32)
    return total


def scatter_start(held):
    groups = routes(lax.axis_size("dp"))[1]
    size = len(held) // 2 ** len(groups[-1])
    came = [flip(held[(k + 1) * size + i], "dp", y) for k, y in enumerate(combos(groups[-1])) for i in range(size)]
    return held[:size], came


def scatter_end(kept, came):
    held = [add_up(kept[i], *came[i :: len(kept)]).astype(BF) for i in range(len(kept))]
    for group in routes(lax.axis_size("dp"))[1][-2::-1]:
        size = len(held) // 2 ** len(group)
        came = [[flip(held[(k + 1) * size + i], "dp", y) for i in range(size)] for k, y in enumerate(combos(group))]
        held = [add_up(held[i], *(row[i] for row in came)).astype(BF) for i in range(size)]
    return held[0]


def rows_at(order, j, my_dp, span):
    return pl.ds(pl.multiple_of((order[j] ^ my_dp) * span, span), span)


def head_mask(shape, head):
    lane = lax.broadcasted_iota(jnp.int32, shape, 1)
    return (lane < HEAD_DIM) if head == 0 else (lane >= HEAD_DIM)


SPANS = (2, 3, 4, 5, 6, 8)


def by_span(ids, t, with_keys):
    low, number = ids[3 + t], ids[3 + LEN // TILE + t]
    for k, span in enumerate(SPANS):
        fits = number <= span
        if k:
            fits = fits & (number > SPANS[k - 1])

        @pl.when(fits)
        def _(span=span):
            start = jnp.minimum(low, LEN // KEYS - span) * KEYS
            with_keys(pl.multiple_of(start, KEYS), span * KEYS)


def reach(segment_row):
    heads_at, ends_at = segment_row[::TILE], segment_row[TILE - 1 :: TILE]
    low = jnp.sum((segment_row[None] < heads_at[:, None]).astype(jnp.int32), axis=1) // KEYS
    high = (jnp.sum((segment_row[None] <= ends_at[:, None]).astype(jnp.int32), axis=1) + KEYS - 1) // KEYS
    return low, high - low


def lay_out(order, my_dp, w_refs, w_all):
    span, half = D // len(order), len(order) // 2
    for j in range(len(order)):
        piece = w_refs[j][0, :span] if j < half else w_refs[half][j - half, 0, :span]
        w_all[rows_at(order, j, my_dp, span), :] = piece


def column_specs(w_parts, base):
    *ones, stacked = w_parts
    block = (1, *ones[0].shape[1:])
    return [pl.BlockSpec(block, lambda g, ids: (g + base, 0, 0))] * len(ones) + [
        pl.BlockSpec((stacked.shape[0], *block), lambda g, ids: (0, g + base, 0, 0))
    ]


def attend_kernel(order, ids, x_ref, *refs):
    n_w = len(order) // 2 + 1
    bias_ref, qf_ref, kf_ref, q_ref, k_ref, v_ref, ho_ref, lse_ref, w_all, keys, vals = refs[n_w:]
    lay_out(order, ids[2], refs[:n_w], w_all)

    @pl.when(pl.program_id(0) == 0)
    def _():
        keys[:, PAIR:] = kf_ref[0]

    for t in range(LEN // TILE):
        at = slice(t * TILE, (t + 1) * TILE)
        got = dot(x_ref[0, at], w_all[...])
        q_ref[0, at] = (got[:, :PAIR] + bias_ref[0, 0:1]).astype(BF)
        key = got[:, PAIR : 2 * PAIR].astype(BF)
        k_ref[0, at] = key
        keys[at, :PAIR] = key
        val = (got[:, 2 * PAIR :] + bias_ref[0, 1:2]).astype(BF)
        v_ref[0, at] = val
        for head in range(2):
            vals[head, at, :] = jnp.where(head_mask((TILE, PAIR), head), val, BF(1))

    def one_tile(t, carry):
        at = pl.ds(pl.multiple_of(t * TILE, TILE), TILE)
        query = q_ref[0, at] * BF(0.125)

        def with_keys(start, count):
            near = pl.ds(start, count)
            low_lane = head_mask((TILE, PAIR), 0)
            wide0 = jnp.concatenate([jnp.where(head_mask((TILE, PAIR), 0), query, BF(0)), qf_ref[0, at]], axis=1)
            scores0 = dot(wide0, keys[near, :], NT)
            wide1 = jnp.concatenate([jnp.where(head_mask((TILE, PAIR), 1), query, BF(0)), qf_ref[0, at]], axis=1)
            scores1 = dot(wide1, keys[near, :], NT)
            top0 = jnp.max(scores0, axis=1, keepdims=True)
            probs0 = jnp.exp(scores0 - top0).astype(BF)
            top1 = jnp.max(scores1, axis=1, keepdims=True)
            probs1 = jnp.exp(scores1 - top1).astype(BF)
            out0 = dot(probs0, vals[0, near, :])
            out1 = dot(probs1, vals[1, near, :])
            total = pltpu.roll(jnp.where(low_lane, out1, out0), HEAD_DIM, 1)
            ho_ref[0, at] = (jnp.where(low_lane, out0, out1) / total).astype(BF)
            both = (jnp.where(low_lane, top0, top1) + jnp.log(total)).T
            lse_ref[0, 0:1, at] = both[0:1]
            lse_ref[0, 1:2, at] = both[HEAD_DIM : HEAD_DIM + 1]

        by_span(ids, t, with_keys)
        return carry

    lax.fori_loop(0, LEN // TILE, one_tile, 0)


def attend(ids, tokens, w_parts, bias, qf, kf, order, part=(0, 1), after=(), carry=()):
    groups, tall, _ = w_parts[0].shape
    count = groups // part[1]
    base = part[0] * count
    pair = pl.BlockSpec((1, LEN, PAIR), lambda g, ids: (g, 0, 0))
    feats = pl.BlockSpec((1, LEN, PAIR), lambda g, ids: (ids[0], 0, 0))
    return kernel_call(
        functools.partial(attend_kernel, order),
        ids,
        (tokens, *w_parts, bias, qf, kf),
        [pl.BlockSpec((1, LEN, D), lambda g, ids: (ids[0], 0, 0))]
        + column_specs(w_parts, base)
        + [pl.BlockSpec((1, 2, PAIR), lambda g, ids: (g + base, 0, 0)), feats, feats],
        after,
        carry,
        [
            pltpu.VMEM((D, 3 * PAIR), BF),
            pltpu.VMEM((LEN, 2 * PAIR), BF),
            pltpu.VMEM((2, LEN, PAIR), BF),
        ],
        grid=(count,),
        out_specs=[pair, pair, pair, pair, pl.BlockSpec((1, 2, LEN), lambda g, ids: (g, 0, 0))],
        out_shape=[jax.ShapeDtypeStruct((count, LEN, PAIR), BF)] * 4
        + [jax.ShapeDtypeStruct((count, 2, LEN), F32)],
        mib=60,
        name="attend",
    )


def norm_stats(value):
    center = value - jnp.mean(value, axis=-1, keepdims=True)
    spread = jnp.mean(center * center, axis=-1, keepdims=True)
    inverse = lax.rsqrt(spread + 1e-05)
    return center * inverse, inverse


def norm_backward(upstream, normal, inverse, gain):
    scaled = upstream * gain
    return inverse * (
        scaled
        - jnp.mean(scaled, axis=-1, keepdims=True)
        - normal * jnp.mean(scaled * normal, axis=-1, keepdims=True)
    )


CHUNK = 1024


def unpack(order, my_dp, w_refs, w_out, w_up, w_down):
    groups, span, _ = w_refs[0].shape
    wide = FF // groups
    for j in range(len(order)):
        row = rows_at(order, j, my_dp, span)
        for g in range(groups):
            w_out[row, g * PAIR : (g + 1) * PAIR] = w_refs[j][g, :, :PAIR]
            w_up[row, g * wide : (g + 1) * wide] = w_refs[j][g, :, PAIR : PAIR + wide]
            w_down[row, g * wide : (g + 1) * wide] = w_refs[j][g, :, PAIR + wide :]


def up_half(x_ref, heads, cot_ref, par_ref, ffb_ref, w_out, w_up, w_down, keep_hidden, slope_ref):
    gain_one, gain_two = par_ref[0:1], par_ref[1:2]
    shift_att, shift_ffn, shift_one, shift_two = (par_ref[k : k + 1] for k in range(2, 6))
    attention = dot(heads, w_out[...], NT) + shift_att
    normal_one, inverse_one = norm_stats(x_ref[0].astype(F32) + attention)
    normed = normal_one * gain_one + shift_one
    normed_low = normed.astype(BF)
    branch = shift_ffn
    for c in range(FF // CHUNK):
        at = slice(c * CHUNK, (c + 1) * CHUNK)
        pre = dot(normed_low, w_up[:, at]) + ffb_ref[:, at]
        phi = 0.5 * (1.0 + lax.erf(pre * 0.7071067811865476))
        hidden = (pre * phi).astype(BF)
        if keep_hidden is not None:
            keep_hidden(at, hidden)
        slope_ref[:, at] = phi + pre * jnp.exp(-0.5 * pre * pre) * 0.3989422804014327
        branch = branch + dot(hidden, w_down[:, at], NT)
    normal_two, inverse_two = norm_stats(normed + branch)
    final_low = (normal_two * gain_two + shift_two).astype(BF)
    upstream = cot_ref[0].astype(F32)
    g_final = norm_backward(upstream, normal_two, inverse_two, gain_two)
    return normal_one, inverse_one, normed_low, normal_two, final_low, upstream, g_final


def down_half(g_final, normal_one, inverse_one, par_ref, w_out, w_up, w_down, slope_ref, keep_pre):
    g_final_low = g_final.astype(BF)
    g_normed = g_final
    for c in range(FF // CHUNK):
        at = slice(c * CHUNK, (c + 1) * CHUNK)
        g_pre = (dot(g_final_low, w_down[:, at]) * slope_ref[:, at]).astype(BF)
        if keep_pre is not None:
            keep_pre(at, g_pre)
        g_normed = g_normed + dot(g_pre, w_up[:, at], NT)
    g_attention = norm_backward(g_normed, normal_one, inverse_one, par_ref[0:1])
    g_attention_low = g_attention.astype(BF)
    g_heads = dot(g_attention_low, w_out[...]).astype(BF)
    return g_final_low, g_normed, g_attention, g_attention_low, g_heads


def fold(acc, k, term, first):
    part = jnp.sum(term.reshape(TOKENS_AT_ONCE // 8, 8, D), axis=0)

    @pl.when(first)
    def _():
        acc[k] = part

    @pl.when(jnp.logical_not(first))
    def _():
        acc[k] += part


def is_middle(ids):
    return (ids[1] == 1) | (ids[1] == 2)


def heads_of(ids, ho_refs):
    there = [k ^ ids[0] ^ ids[1] for k in range(ho_refs[0].shape[0])]
    if len(ho_refs) == 1:
        return jnp.concatenate([ho_refs[0][k] for k in there], axis=1)
    return jnp.concatenate([jnp.where(is_middle(ids), ho_refs[1][k], ho_refs[0][k]) for k in there], axis=1)


def tokenwise_kernel(order, n_ho, keep, ids, x_ref, cot_ref, *refs):
    ho_refs, refs = refs[:n_ho], refs[n_ho:]
    half = len(order) // 2
    w_refs, refs = [*refs[:half], *(refs[half].at[j] for j in range(half))], refs[half + 1 :]
    par_ref, ffb_ref, out_ref, gatt_ref, gh_ref, *refs = refs
    if keep:
        near_ref, far_ref, sums_ref, ffs_ref, w_out, w_up, w_down, slope, *refs = refs
        acc, hid_all, pre_all, ho_all, up_t, down_t, att_t, gw_all = refs
    else:
        w_out, w_up, w_down, slope = refs
    step = pl.program_id(0)
    tiles = LEN // TOKENS_AT_ONCE
    groups = gh_ref.shape[0]
    my_dp = ids[2]

    @pl.when(step == 0)
    def _():
        unpack(order, my_dp, w_refs, w_out, w_up, w_down)

    def tokens_step():
        rows = pl.ds(pl.multiple_of(jnp.minimum(step, tiles - 1) * TOKENS_AT_ONCE, TOKENS_AT_ONCE), TOKENS_AT_ONCE)
        heads = heads_of(ids, ho_refs)
        keep_hidden = keep_pre = None
        if keep:

            def keep_hidden(at, hidden):
                hid_all[rows, at] = hidden

            def keep_pre(at, g_pre):
                pre_all[rows, at] = g_pre
                here = jnp.sum(g_pre.astype(F32), axis=0, keepdims=True)

                @pl.when(step == 0)
                def _():
                    ffs_ref[:, at] = here

                @pl.when(step > 0)
                def _():
                    ffs_ref[:, at] += here

        normal_one, inverse_one, normed_low, normal_two, final_low, upstream, g_final = up_half(
            x_ref, heads, cot_ref, par_ref, ffb_ref, w_out, w_up, w_down, keep_hidden, slope
        )
        out_ref[...] = final_low
        g_final_low, g_normed, g_attention, g_attention_low, g_heads = down_half(
            g_final, normal_one, inverse_one, par_ref, w_out, w_up, w_down, slope, keep_pre
        )
        gatt_ref[...] = g_attention
        for g in range(groups):
            gh_ref[g] = g_heads[:, g * PAIR : (g + 1) * PAIR]
        if keep:
            ho_all[rows, :] = heads
            down_t[:, rows] = g_final_low.T
            att_t[:, rows] = g_attention_low.T
            up_t[:, rows] = normed_low.T
            terms = (g_normed * normal_one, upstream * normal_two, g_attention, g_final, g_normed, upstream)
            for k, term in enumerate(terms):
                fold(acc, k, term, step == 0)

            @pl.when(step == tiles - 1)
            def _():
                for k in range(6):
                    sums_ref[k : k + 1] = jnp.sum(acc[k], axis=0, keepdims=True)

    if not keep:
        tokens_step()
        return

    pl.when(step < tiles)(tokens_step)

    @pl.when(step >= tiles)
    def _():
        half, _, span, _ = near_ref.shape
        wide = FF // groups
        block = pl.ds(pl.multiple_of((step - tiles) * wide, wide), wide)
        pair = pl.ds(pl.multiple_of((step - tiles) * PAIR, PAIR), PAIR)
        gw_all[:, :PAIR] = dot(att_t[...], ho_all[:, pair]).astype(BF)
        gw_all[:, PAIR : PAIR + wide] = dot(up_t[...], pre_all[:, block]).astype(BF)
        gw_all[:, PAIR + wide :] = dot(down_t[...], hid_all[:, block]).astype(BF)
        for j in range(half):
            near_ref[j, 0] = gw_all[rows_at(order, j, my_dp, span), :]
            far_ref[j, 0] = gw_all[rows_at(order, half + j, my_dp, span), :]


def tokenwise(ids, tokens, heads_out, cotangent, w_parts, params, ff_shift, order, keep, after=(), carry=()):
    tiles = LEN // TOKENS_AT_ONCE
    groups, span, cols = w_parts[0].shape
    early = lambda t: jnp.minimum(t, tiles - 1)
    late = lambda t: jnp.maximum(t - tiles, 0)
    full = lambda shape: pl.BlockSpec(shape, lambda t, ids: (0,) * len(shape))
    row = pl.BlockSpec((1, TOKENS_AT_ONCE, D), lambda t, ids: (ids[0], early(t), 0))
    flat = pl.BlockSpec((TOKENS_AT_ONCE, D), lambda t, ids: (early(t), 0))
    pairs = lambda n: pl.BlockSpec((n, TOKENS_AT_ONCE, PAIR), lambda t, ids: (0, early(t), 0))
    out_specs = [flat, flat, pairs(groups)]
    out_shape = [
        jax.ShapeDtypeStruct((LEN, D), BF),
        jax.ShapeDtypeStruct((LEN, D), F32),
        jax.ShapeDtypeStruct((groups, LEN, PAIR), BF),
    ]
    scratch = [
        pltpu.VMEM((D, D), BF),
        pltpu.VMEM((D, FF), BF),
        pltpu.VMEM((D, FF), BF),
        pltpu.VMEM((TOKENS_AT_ONCE, FF), F32),
    ]
    if keep:
        half = len(order) // 2
        part = pl.BlockSpec((half, 1, span, cols), lambda t, ids: (0, late(t), 0, 0))
        out_specs += [part, part, full((6, D)), full((1, FF))]
        out_shape += [jax.ShapeDtypeStruct((half, groups, span, cols), BF)] * 2
        out_shape += [jax.ShapeDtypeStruct((6, D), F32), jax.ShapeDtypeStruct((1, FF), F32)]
        scratch += [
            pltpu.VMEM((6, 8, D), F32),
            pltpu.VMEM((LEN, FF), BF),
            pltpu.VMEM((LEN, FF), BF),
            pltpu.VMEM((LEN, D), BF),
            pltpu.VMEM((D, LEN), BF),
            pltpu.VMEM((D, LEN), BF),
            pltpu.VMEM((D, LEN), BF),
            pltpu.VMEM((D, cols), BF),
        ]
    return kernel_call(
        functools.partial(tokenwise_kernel, order, len(heads_out), keep),
        ids,
        (tokens, cotangent, *heads_out, *w_parts, params, ff_shift),
        [row, row]
        + [pairs(a.shape[0]) for a in heads_out]
        + [full(a.shape) for a in w_parts]
        + [full((6, D)), full((1, FF))],
        after,
        carry,
        scratch,
        grid=(tiles + groups if keep else tiles,),
        out_specs=out_specs,
        out_shape=out_shape,
        mib=60,
        name="tokenwise_keep" if keep else "tokenwise",
    )


def attend_back_kernel(order, keep, ids, x_ref, *refs):
    n_w = len(order) // 2 + 1
    w_refs, (qf_ref, kf_ref, *refs) = refs[:n_w], refs[n_w:]
    if keep:
        q_ref, k_ref, v_ref, ho_ref, lse_ref, gh_ref, gatt_ref, tg_ref, send_ref, again_ref, near_ref, far_ref, gb_ref, *refs = refs
        w_all, keys, keys_t, delta, dk, dv, grads, x_t, gw_all = refs
    else:
        bias_ref, ho_ref, ho_mid, lse_ref, lse_mid, gh_ref, gatt_ref, tg_ref, *refs = refs
        w_all, keys, keys_t, delta, dk, dv, grads, q_ref, k_ref, v_ref = refs
    my_dp = ids[2]
    lay_out(order, my_dp, w_refs, w_all)

    @pl.when(pl.program_id(0) == 0)
    def _():
        keys[:, PAIR:] = kf_ref[0]
        tg_ref[...] = gatt_ref[...]
        if keep:
            x_t[...] = x_ref[0].T

    if keep:
        heads, logs = ho_ref[0], lse_ref[0]
    else:
        for t in range(LEN // TILE):
            at = slice(t * TILE, (t + 1) * TILE)
            got = dot(x_ref[0, at], w_all[...])
            q_ref[0, at] = (got[:, :PAIR] + bias_ref[0, 0:1]).astype(BF)
            k_ref[0, at] = got[:, PAIR : 2 * PAIR].astype(BF)
            v_ref[0, at] = (got[:, 2 * PAIR :] + bias_ref[0, 1:2]).astype(BF)
        heads = jnp.where(is_middle(ids), ho_mid[0], ho_ref[0])
        logs = jnp.where(is_middle(ids), lse_mid[0], lse_ref[0])
    delta[2:4] = logs
    keys[:, :PAIR] = k_ref[0]
    keys_t[...] = k_ref[0].T
    prod = (gh_ref[0].astype(F32) * heads.astype(F32)).T
    delta[0:1] = jnp.sum(prod[:HEAD_DIM], axis=0, keepdims=True)
    delta[1:2] = jnp.sum(prod[HEAD_DIM:], axis=0, keepdims=True)
    dk[...] = jnp.zeros_like(dk)
    dv[...] = jnp.zeros_like(dv)

    def one_tile(t, carry):
        at = pl.ds(pl.multiple_of(t * TILE, TILE), TILE)
        query, back = q_ref[0, at], gh_ref[0, at]

        def with_keys(start, count):
            near = pl.ds(start, count)
            mine0 = jnp.where(head_mask((TILE, PAIR), 0), query, BF(0))
            back0 = jnp.where(head_mask((TILE, PAIR), 0), back, BF(0))
            wide0 = jnp.concatenate([mine0 * BF(0.125), qf_ref[0, at]], axis=1)
            scores0 = dot(keys[near, :], wide0, NT)
            g_probs0 = dot(v_ref[0, near], back0, NT)
            mine1 = jnp.where(head_mask((TILE, PAIR), 1), query, BF(0))
            back1 = jnp.where(head_mask((TILE, PAIR), 1), back, BF(0))
            wide1 = jnp.concatenate([mine1 * BF(0.125), qf_ref[0, at]], axis=1)
            scores1 = dot(keys[near, :], wide1, NT)
            g_probs1 = dot(v_ref[0, near], back1, NT)
            probs0 = jnp.exp(scores0 - delta[2:3, at])
            g_raw0 = (probs0 * (g_probs0 - delta[0 : 0 + 1, at])).astype(BF)
            low0 = probs0.astype(BF)
            probs1 = jnp.exp(scores1 - delta[3:4, at])
            g_raw1 = (probs1 * (g_probs1 - delta[1 : 1 + 1, at])).astype(BF)
            low1 = probs1.astype(BF)
            d_query0 = dot(keys_t[0 * HEAD_DIM : (0 + 1) * HEAD_DIM, near], g_raw0)
            d_query1 = dot(keys_t[1 * HEAD_DIM : (1 + 1) * HEAD_DIM, near], g_raw1)
            dv[near, :] += dot(jnp.concatenate([low0, low1], axis=1), jnp.concatenate([back0, back1], axis=0))
            dk[near, :] += dot(jnp.concatenate([g_raw0, g_raw1], axis=1), jnp.concatenate([mine0, mine1], axis=0))
            d_query = [d_query0, d_query1]
            grads[at, :PAIR] = (jnp.concatenate(d_query, axis=0).T * 0.125).astype(BF)

        by_span(ids, t, with_keys)
        return carry

    lax.fori_loop(0, LEN // TILE, one_tile, 0)
    grads[:, PAIR : 2 * PAIR] = (dk[...] * 0.125).astype(BF)
    grads[:, 2 * PAIR :] = dv[...].astype(BF)
    for t in range(LEN // TILE):
        at = slice(t * TILE, (t + 1) * TILE)
        tg_ref[at, :] += dot(grads[at, :], w_all[...], NT)
    if keep:
        half, _, span, _ = near_ref.shape
        gw_all[...] = dot(x_t[...], grads[...]).astype(BF)
        for j in range(half):
            near_ref[j, 0] = gw_all[rows_at(order, j, my_dp, span), :]
            far_ref[j, 0] = gw_all[rows_at(order, half + j, my_dp, span), :]
        gb_ref[0, 0:1] = jnp.sum(grads[:, :PAIR].astype(F32), axis=0, keepdims=True)
        gb_ref[0, 1:2] = jnp.sum(grads[:, 2 * PAIR :].astype(F32), axis=0, keepdims=True)

        @pl.when(pl.program_id(0) == pl.num_programs(0) - 1)
        def _():
            send = tg_ref[...].astype(BF)
            send_ref[...] = send
            again_ref[...] = send


def attend_back(ids, tokens, w_parts, qf, kf, saved, g_heads, g_att, order, keep, part=(0, 1), after=(), carry=()):
    n_dp = len(order)
    groups, tall, _ = w_parts[0].shape
    span, half = D // n_dp, n_dp // 2
    count = groups // part[1]
    base = part[0] * count
    there = lambda g, ids: (g + base) ^ ids[0] ^ ids[1]
    pair = pl.BlockSpec((1, LEN, PAIR), lambda g, ids: (there(g, ids), 0, 0))
    logs = pl.BlockSpec((1, 2, LEN), lambda g, ids: (there(g, ids), 0, 0))
    feats = pl.BlockSpec((1, LEN, PAIR), lambda g, ids: (ids[0], 0, 0))
    full = pl.BlockSpec((LEN, D), lambda g, ids: (0, 0))
    out_specs, out_shape = [full], [jax.ShapeDtypeStruct((LEN, D), F32)]
    scratch = [
        pltpu.VMEM((D, 3 * PAIR), BF),
        pltpu.VMEM((LEN, 2 * PAIR), BF),
        pltpu.VMEM((PAIR, LEN), BF),
        pltpu.VMEM((4, LEN), F32),
        pltpu.VMEM((LEN, PAIR), F32),
        pltpu.VMEM((LEN, PAIR), F32),
        pltpu.VMEM((LEN, 3 * PAIR), BF),
    ]
    if keep:
        saved_specs = [pair, pair, pair, pair, logs]
        piece = pl.BlockSpec((half, 1, span, 3 * PAIR), lambda g, ids: (0, g, 0, 0))
        out_specs += [full, full, piece, piece, pl.BlockSpec((1, 2, PAIR), lambda g, ids: (g, 0, 0))]
        out_shape += [jax.ShapeDtypeStruct((LEN, D), BF)] * 2
        out_shape += [jax.ShapeDtypeStruct((half, groups, span, 3 * PAIR), BF)] * 2
        out_shape += [jax.ShapeDtypeStruct((groups, 2, PAIR), F32)]
        scratch += [pltpu.VMEM((D, LEN), BF), pltpu.VMEM((D, 3 * PAIR), BF)]
    else:
        saved_specs = [pl.BlockSpec((1, 2, PAIR), lambda g, ids: (g + base, 0, 0)), pair, pair, logs, logs]
        scratch += [pltpu.VMEM((1, LEN, PAIR), BF)] * 3
    return kernel_call(
        functools.partial(attend_back_kernel, order, keep),
        ids,
        (tokens, *w_parts, qf, kf, *saved, g_heads, g_att),
        [pl.BlockSpec((1, LEN, D), lambda g, ids: (ids[0], 0, 0))]
        + column_specs(w_parts, base)
        + [feats, feats]
        + saved_specs
        + [pl.BlockSpec((1, LEN, PAIR), lambda g, ids: (g + base, 0, 0)), full],
        after,
        carry,
        scratch,
        grid=(count,),
        out_specs=out_specs,
        out_shape=out_shape,
        mib=60,
        name="attend_back_keep" if keep else "attend_back",
    )


RATES = (D ** (-0.5), (D // 64) ** (-0.5), D ** (-0.5), FF ** (-0.5), 0.3, 0.3, 0.3, 0.3)
DECAYS = (0.01, 0.01, 0.01, 0.01, 0.0, 0.0, 0.0, 0.0)


def adam_step(weight, grad_sum, first, second, rate, decay):
    first_new = beta_one * first + (1.0 - beta_one) * grad_sum
    second_new = beta_two * second + (1.0 - beta_two) * grad_sum * grad_sum
    first_hat = first_new / (1.0 - beta_one**STEP)
    second_hat = second_new / (1.0 - beta_two**STEP)
    weight_new = weight - rate * (first_hat / (jnp.sqrt(second_hat) + 1e-08) + decay * weight)
    return (weight_new, first_new, second_new)


def adam_kernel(*refs):
    terms, olds, news = refs[:4], refs[4:28], refs[28:]
    span = olds[2].shape[0]
    wide, per = olds[2].shape[1], olds[5].shape[1]
    total_ab = lambda at: terms[0][:, at].astype(F32) + terms[1][:, at].astype(F32)
    total_qkv = lambda rows, at: terms[2][rows, at].astype(F32) + terms[3][rows, at].astype(F32)

    def step(slot, at, grad):
        old = [olds[8 * k + slot][at] for k in range(3)]
        new = adam_step(old[0], grad, old[1], old[2], RATES[slot], DECAYS[slot])
        for k in range(3):
            news[8 * k + slot][at] = new[k]

    for k in range(3):
        step(0, k, total_qkv(slice(0, span), slice(k * PAIR, (k + 1) * PAIR)))
    step(1, ..., total_ab(slice(0, PAIR)))
    step(2, ..., total_ab(slice(PAIR, PAIR + wide)))
    step(3, ..., total_ab(slice(PAIR + wide, PAIR + 2 * wide)))
    tail = total_qkv(slice(span, span + EXTRA), slice(0, 3 * PAIR))
    for k in range(2):
        step(4, k, tail[2 * k : 2 * k + 2, 2 * PAIR : 2 * PAIR + per])
    step(5, ..., tail[: olds[5].shape[0], PAIR : PAIR + per])
    step(6, ..., tail[:2, :span])
    step(7, ..., tail[2:6, :span])


def adam(last, *sets):
    turn = lambda a: (a[0].transpose(1, 0, 2), a[1].T, a[2], a[3].T, *a[4:])
    olds = [array for group in sets for array in turn(group)]
    news = pl.pallas_call(
        adam_kernel,
        out_shape=[jax.ShapeDtypeStruct(a.shape, F32) for a in olds],
        name="adam",
    )(*last[0], *last[1], *olds)
    return [array for k in range(3) for array in turn(news[8 * k : 8 * k + 8])]


def rows_of(ids):
    z = ids[1]
    by = lambda a, b, c, d: jnp.where(z == 0, a, jnp.where(z == 1, b, jnp.where(z == 2, c, d)))
    return z, by(1, 2, 1, 2), by(2, 0, 3, 1), by(3, 3, 0, 0)


def place_own_kernel(ids, own_ref, other_ref, out_ref):
    own, other, _, _ = rows_of(ids)
    out_ref[own] = own_ref[...]
    out_ref[other] = other_ref[...]


def place_sent_kernel(ids, straight_ref, middle_ref, end_ref, before_ref, out_ref, sems, one, two):
    t, last = pl.program_id(0), pl.num_programs(0) - 1
    _, _, straight, through = rows_of(ids)
    size = one.shape[1]
    slot = lax.rem(t, 2)
    copies = lambda step, slot: [
        pltpu.make_async_copy(buf.at[slot], out_ref.at[row, pl.ds(step * size, size)], sems.at[k, slot])
        for k, (buf, row) in enumerate(((one, straight), (two, through)))
    ]

    @pl.when(t >= 2)
    def _():
        for copy in copies(t - 2, slot):
            copy.wait()

    one[slot] = straight_ref[...].astype(F32)
    two[slot] = jnp.where(is_middle(ids), middle_ref[...], end_ref[...]).astype(F32)
    for copy in copies(t, slot):
        copy.start()

    @pl.when(t == last)
    def _():
        for copy in copies(t - 1, 1 - slot) + copies(t, slot):
            copy.wait()


PLACED = 256


def place_own(ids, own, other):
    block = pl.BlockSpec((PLACED, D), lambda t, ids: (t, 0))
    return kernel_call(
        place_own_kernel, ids, (own, other), [block, block], (), (), [],
        grid=(LEN // PLACED,),
        out_specs=[pl.BlockSpec((4, PLACED, D), lambda t, ids: (0, t, 0))],
        out_shape=[jax.ShapeDtypeStruct((4, LEN, D), F32)],
        mib=60,
        name="place_own",
    )[0]


def place_sent(ids, before, straight, middle, end):
    block = pl.BlockSpec((PLACED, D), lambda t, ids: (t, 0))
    anywhere = pl.BlockSpec(memory_space=pl.ANY)
    return pl.pallas_call(
        place_sent_kernel,
        grid_spec=pltpu.PrefetchScalarGridSpec(
            num_scalar_prefetch=1,
            grid=(LEN // PLACED,),
            in_specs=[block, block, block, anywhere],
            out_specs=anywhere,
            scratch_shapes=[
                pltpu.SemaphoreType.DMA((2, 2)),
                pltpu.VMEM((2, PLACED, D), F32),
                pltpu.VMEM((2, PLACED, D), F32),
            ],
        ),
        out_shape=jax.ShapeDtypeStruct(before.shape, F32),
        input_output_aliases={4: 0},
        compiler_params=vmem(60),
        name="place_sent",
    )(ids, straight, middle, end, before)


def pack_kernel(qkv, out_t, up, down_t, qv, ff, gains, shifts, first_ref, second_ref):
    span, wide = up.shape
    for k in range(3):
        first_ref[:span, k * PAIR : (k + 1) * PAIR] = qkv[k].astype(BF)
    first_ref[span:, :] = jnp.zeros((EXTRA, 3 * PAIR), BF)
    first_ref[span : span + 2, :span] = gains[...].astype(BF)
    first_ref[span + 2 : span + 6, :span] = shifts[...].astype(BF)
    first_ref[span : span + ff.shape[0], PAIR : PAIR + ff.shape[1]] = ff[...].astype(BF)
    for k in range(2):
        first_ref[span + 2 * k : span + 2 * k + 2, 2 * PAIR : 2 * PAIR + qv.shape[2]] = qv[k].astype(BF)
    second_ref[:, :PAIR] = out_t[...].astype(BF)
    second_ref[:, PAIR : PAIR + wide] = up[...].astype(BF)
    second_ref[:, PAIR + wide :] = down_t[...].astype(BF)


def pack(w_qkv, w_out, w_up, w_down, qv_bias, ff_bias, norm_gains, norm_shifts):
    span, wide = w_up.shape
    return pl.pallas_call(
        pack_kernel,
        out_shape=[
            jax.ShapeDtypeStruct((span + EXTRA, 3 * PAIR), BF),
            jax.ShapeDtypeStruct((span, PAIR + 2 * wide), BF),
        ],
        name="pack",
    )(w_qkv.transpose(1, 0, 2), w_out.T, w_up, w_down.T, qv_bias, ff_bias, norm_gains, norm_shifts)


def features(segment_ids, pad_lengths):
    place = jnp.arange(LEN, dtype=jnp.int32)[None, :, None]
    lane = jnp.arange(PAIR, dtype=jnp.int32)[None, None, :]
    segment = segment_ids[:, :, None]
    padding = place >= (LEN - pad_lengths)[:, None, None]
    high, low = place // 32, place % 32
    hit = (
        ((lane < 4) & (lane == segment))
        | ((lane >= 4) & (lane < 36) & (lane - 4 == high))
        | ((lane >= 36) & (lane < 68) & (lane - 36 == low))
    )
    counts = jnp.where(padding, (lane >= 4) & (lane < 68), lane < 4)
    qf = jnp.where(hit, -FAR, 0.0).astype(BF)
    kf = jnp.where(counts & ~hit, 1.0, 0.0).astype(BF)
    return qf, kf


def per_device(
    tokens, segment_ids, pad_lengths, cotangent,
    w_qkv, w_out, w_up, w_down, qv_bias, ff_bias, norm_gains, norm_shifts,
    first_qkv, first_out, first_up, first_down, first_qv_bias, first_ff_bias, first_gains, first_shifts,
    second_qkv, second_out, second_up, second_down, second_qv_bias, second_ff_bias, second_gains, second_shifts,
):
    n_dp, n_mp = lax.axis_size("dp"), lax.axis_size("mp")
    my_dp, my_mp = lax.axis_index("dp"), lax.axis_index("mp")
    order = dp_order(n_dp)
    half = n_dp // 2
    span = D // n_dp
    wide, per = FF // n_mp, HEAD_DIM // n_dp
    ff_rows = wide // HEAD_DIM

    places = ((jnp.array(order, jnp.int32)[:, None] ^ my_dp) == jnp.arange(n_dp, dtype=jnp.int32)[None]).astype(BF)

    def to_near(value):
        return flip(value, "dp", routes(n_dp)[0])

    part_qkv, part_ab = pack(w_qkv, w_out, w_up, w_down, qv_bias, ff_bias, norm_gains, norm_shifts)
    far_qkv = gather_far(gather_mp(part_qkv))
    all_qkv = [*far_qkv, to_near(jnp.stack(far_qkv))]
    far_ab = gather_far(gather_mp_steps(part_ab))
    small_here = jnp.concatenate(
        [jnp.stack([a[:, span : span + 8] for a in all_qkv[:half]]), all_qkv[half][:, :, span : span + 8]]
    ).reshape(n_dp, -1)
    small_all = dot(places, small_here, (((0,), (0,)), ((), ()))).reshape(n_dp, n_mp, 8, 3 * PAIR)
    bias_rows = (
        small_all[:, :, :4, 2 * PAIR : 2 * PAIR + per].reshape(n_dp, n_mp, 2, 2, per).transpose(1, 2, 3, 0, 4)
    ).reshape(n_mp, 2, PAIR)
    ff_shift = small_all[:, :, :ff_rows, PAIR : PAIR + per].transpose(1, 2, 0, 3).reshape(1, FF)
    params = small_all[:, 0, :6, :span].transpose(1, 0, 2).reshape(6, D)
    qf, kf = features(segment_ids, pad_lengths)

    def ids_of(row):
        low, number = reach(lax.dynamic_index_in_dim(segment_ids, row, 0, keepdims=False))
        return jnp.concatenate([jnp.stack([row, my_mp, my_dp]).astype(jnp.int32), low, number])

    middle = (my_mp == 1) | (my_mp == 2)
    second = jnp.where(my_mp < 2, 1, 2) ^ jnp.where(middle, 3, 0)
    mine, other = ids_of(my_mp), ids_of(second)

    saved = attend(mine, tokens, all_qkv, bias_rows, qf, kf, order)
    far_ab = gate(far_ab, saved[4])
    all_ab = [*far_ab, to_near(jnp.stack(far_ab))]
    to_ends, to_middles = [(1, 0), (2, 3)], [(1, 2), (2, 1)]
    across, straight = [(0, 2), (3, 1)], [(0, 1), (3, 2), (1, 3), (2, 0)]
    heads_end, heads_mid = (lax.ppermute(saved[3], "mp", way) for way in (to_ends, to_middles))
    logs_end, logs_mid = (lax.ppermute(saved[4], "mp", way) for way in (to_ends, to_middles))
    own_out, g_att, g_heads, near_ab, far_grad_ab, sums, ff_sums = tokenwise(
        mine, tokens, [saved[3]], cotangent, all_ab, params, ff_shift, order, True
    )
    saved_other = (bias_rows, heads_end, heads_mid, logs_end, logs_mid)
    out_middle = lax.ppermute(own_out, "mp", across)
    out_straight = lax.ppermute(own_out, "mp", straight)
    came_ab = to_near(far_grad_ab)
    own_grad, own_send, send_again, near_qkv, far_grad_qkv, bias_sums = attend_back(
        mine, tokens, all_qkv, qf, kf, saved, g_heads, g_att, order, True, after=saved_other[1:]
    )
    held_ab = [add_up(near_ab[j], came_ab[j]).astype(BF) for j in range(half)]

    def spaced(rows):
        return jnp.pad(rows, [(0, 0), (0, 0), (0, EXTRA - rows.shape[2]), (0, PAIR - rows.shape[3])])

    small_sums = jnp.concatenate(
        [
            spaced(jnp.broadcast_to(sums.reshape(6, n_dp, 1, span).transpose(1, 2, 0, 3), (n_dp, n_mp, 6, span))),
            spaced(ff_sums.reshape(n_mp, ff_rows, n_dp, per).transpose(2, 0, 1, 3)),
            spaced(bias_sums.reshape(n_mp, 4, n_dp, per).transpose(2, 0, 1, 3)),
        ],
        axis=-1,
    ).astype(BF)
    small_sums = dot(places, small_sums.reshape(n_dp, -1)).astype(BF).reshape(n_dp, n_mp, EXTRA, 3 * PAIR)
    came_qkv = to_near(jnp.concatenate([far_grad_qkv, small_sums[half:]], axis=2))
    near_qkv = jnp.concatenate([near_qkv, small_sums[:half]], axis=2)
    own_send, out_middle, out_straight, came_qkv, *held_ab = gate((own_send, out_middle, out_straight, came_qkv, *held_ab))
    grad_middle = lax.ppermute(own_send, "mp", across)
    out_end = lax.ppermute(out_middle, "mp", to_ends)
    kept_ab, far_sums_ab = scatter_start(held_ab)
    other_out, g_att2, g_heads2 = tokenwise(
        other, tokens, [heads_end, heads_mid], cotangent, all_ab, params, ff_shift, order, False,
        after=(own_send,),
    )
    send_again, grad_middle, out_end, came_qkv, *far_sums_ab = gate(
        (send_again, grad_middle, out_end, came_qkv, *far_sums_ab), g_heads2
    )
    grad_straight = lax.ppermute(send_again, "mp", straight)
    grad_end = lax.ppermute(grad_middle, "mp", to_ends)
    held_qkv = [add_up(near_qkv[j], came_qkv[j]).astype(BF) for j in range(half)]
    kept_qkv, far_sums_qkv = scatter_start(held_qkv)
    column_ab = scatter_end(kept_ab, far_sums_ab)
    (half_grad,) = attend_back(
        other, tokens, all_qkv, qf, kf, saved_other, g_heads2, g_att2, order, False, (0, 2),
        after=(grad_middle, *held_qkv, column_ab),
    )
    column_ab, *far_sums_qkv = gate((column_ab, *far_sums_qkv), half_grad)
    column_qkv = scatter_end(kept_qkv, far_sums_qkv)
    came_mp = [flip(jnp.stack([a[1], a[3]]), "mp", 1) for a in (column_ab, column_qkv)]
    (other_grad,) = attend_back(
        other, tokens, all_qkv, qf, kf, saved_other, g_heads2, half_grad, order, False, (1, 2), after=(column_qkv,)
    )
    came_mp = gate(came_mp, other_grad)
    pairs = [add_up(jnp.stack([a[0], a[2]]), b).astype(BF) for a, b in zip((column_ab, column_qkv), came_mp)]
    last = [(a[0], flip(a[1], "mp", 2)) for a in pairs]

    def arrange(own, other, straight, through):
        at = lambda k: my_mp == k
        pick = lambda a, b, c, d: jnp.where(at(0), a, jnp.where(at(1), b, jnp.where(at(2), c, d)))
        return jnp.stack(
            [
                pick(own, straight, through, through),
                pick(other, own, other, straight),
                pick(straight, other, own, other),
                pick(through, through, straight, own),
            ]
        )

    layer_out = arrange(own_out, other_out, out_straight, jnp.where(middle, out_middle, out_end))
    tokens_grad = place_sent(mine, place_own(mine, own_grad, other_grad), grad_straight, grad_middle, grad_end)

    masters = (w_qkv, w_out, w_up, w_down, qv_bias, ff_bias, norm_gains, norm_shifts)
    firsts = (first_qkv, first_out, first_up, first_down, first_qv_bias, first_ff_bias, first_gains, first_shifts)
    seconds = (second_qkv, second_out, second_up, second_down, second_qv_bias, second_ff_bias, second_gains, second_shifts)
    updated = adam(last, masters, firsts, seconds)
    return (layer_out, tokens_grad, *updated)


def solution(mesh):
    weights = (
        P("dp", None, "mp"),
        P("mp", "dp"),
        P("dp", "mp"),
        P("mp", "dp"),
        P(None, "mp", "dp"),
        P("mp", "dp"),
        P(None, "dp"),
        P(None, "dp"),
    )
    rows = P("dp", None, None)
    return jax.shard_map(
        per_device,
        mesh=mesh,
        in_specs=(rows, P("dp", None), P("dp"), rows) + weights * 3,
        out_specs=(rows, rows) + weights * 3,
        check_vma=False,
    )
```

```python
import functools

import jax
import jax.numpy as jnp
from jax import lax
from jax.experimental import pallas as pl
from jax.experimental.pallas import tpu as pltpu
from jax.sharding import PartitionSpec as P

D = 512
HEADS = 8
HEAD_DIM = 64
FF = 2048
LEN = 1024
STEP = 10
PAIR = 128
TILE = 256
KEYS = 128
TOKENS_AT_ONCE = 512
FAR = 1e30
EXTRA = 16
LOGS = 2 * LEN // PAIR

beta_one = 0.9
beta_two = 0.999
BF = jnp.bfloat16
F32 = jnp.float32
NN = (((1,), (0,)), ((), ()))
NT = (((1,), (1,)), ((), ()))


def dot(a, b, dims=NN):
    return lax.dot_general(a, b, dims, preferred_element_type=F32)


def vmem(mib):
    return pltpu.CompilerParams(
        dimension_semantics=("arbitrary",), vmem_limit_bytes=mib * 1024 * 1024
    )


def kernel_call(kernel, ids, inputs, in_specs, after, into, scratch, **kw):
    n, m, c = len(inputs), len(after), len(into)
    grid, out_specs, mib, flops = kw.pop("grid"), kw.pop("out_specs"), kw.pop("mib"), kw.pop("flops", 20_000_000_000)

    def body(ids_ref, *refs):
        given, rest = refs[:n], refs[n + m + c :]
        kernel(ids_ref, *given, *rest)

    anywhere = pl.BlockSpec(memory_space=pl.ANY)
    return pl.pallas_call(
        body,
        grid_spec=pltpu.PrefetchScalarGridSpec(
            num_scalar_prefetch=1,
            grid=grid,
            in_specs=list(in_specs) + [anywhere] * (m + c),
            out_specs=list(out_specs),
            scratch_shapes=scratch,
        ),
        input_output_aliases={1 + n + m + i: k for i, (_, k) in enumerate(into)},
        compiler_params=vmem(mib),
        cost_estimate=pl.CostEstimate(flops=flops, bytes_accessed=1_000_000, transcendentals=0),
        **kw,
    )(ids, *inputs, *after, *(a for a, _ in into))


def gate(values, *until):
    n = len(values)
    anywhere = pl.BlockSpec(memory_space=pl.ANY)
    return list(pl.pallas_call(
        lambda *refs: None,
        in_specs=[anywhere] * (n + len(until)),
        out_specs=[anywhere] * n,
        out_shape=[jax.ShapeDtypeStruct(a.shape, a.dtype) for a in values],
        input_output_aliases={k: k for k in range(n)},
        cost_estimate=pl.CostEstimate(flops=0, bytes_accessed=0, transcendentals=0),
        name="gate",
    )(*values, *until))


def flip(value, axis, bit):
    size = lax.axis_size(axis)
    return lax.ppermute(value, axis, [(i, i ^ bit) for i in range(size)])


def bits(size):
    out, bit = [], 1
    while bit < size:
        out.append(bit)
        bit *= 2
    return out


def combos(steps):
    return [sum(bit for k, bit in enumerate(steps) if (j >> k) & 1) for j in range(1, 2 ** len(steps))]


def routes(n_dp):
    near, *far = bits(n_dp)
    return near, [far[k : k + 2] for k in range(0, len(far), 2)]


def dp_order(n_dp):
    near, groups = routes(n_dp)
    order = [0]
    for group in groups:
        order = order + [x ^ y for y in combos(group) for x in order]
    return order + [x ^ near for x in order]


def gather_mp(part):
    return jnp.stack([part] + [flip(part, "mp", j) for j in range(1, lax.axis_size("mp"))])


def gather_mp_steps(part):
    n_mp = lax.axis_size("mp")
    held = {0: part}
    for bit in bits(n_mp)[::-1]:
        came = flip(jnp.stack([held[j] for j in sorted(held)]), "mp", bit)
        held.update({j ^ bit: came[k] for k, j in enumerate(sorted(held))})
    return jnp.stack([held[j] for j in range(n_mp)])


def gather_far(column):
    held = [column]
    for group in routes(lax.axis_size("dp"))[1]:
        held = held + [flip(a, "dp", y) for y in combos(group) for a in held]
    return held


def add_up(*terms):
    total = terms[0].astype(F32)
    for term in terms[1:]:
        total = total + term.astype(F32)
    return total


def scatter_start(held):
    groups = routes(lax.axis_size("dp"))[1]
    size = len(held) // 2 ** len(groups[-1])
    sent = [(held[(k + 1) * size + i], y) for k, y in enumerate(combos(groups[-1])) for i in range(size)]
    return held[:size], sent


def scatter_end(kept, came):
    held = [add_up(kept[i], *came[i :: len(kept)]).astype(BF) for i in range(len(kept))]
    for group in routes(lax.axis_size("dp"))[1][-2::-1]:
        size = len(held) // 2 ** len(group)
        came = [[flip(held[(k + 1) * size + i], "dp", y) for i in range(size)] for k, y in enumerate(combos(group))]
        held = [add_up(held[i], *(row[i] for row in came)).astype(BF) for i in range(size)]
    return held[0]


def rows_at(order, j, my_dp, span):
    return pl.ds(pl.multiple_of((order[j] ^ my_dp) * span, span), span)


def head_mask(shape, head):
    lane = lax.broadcasted_iota(jnp.int32, shape, 1)
    return (lane < HEAD_DIM) if head == 0 else (lane >= HEAD_DIM)


SPANS = (2, 3, 4, 5, 6, 8)


def by_span(ids, t, with_keys):
    low, number = ids[3 + t], ids[3 + LEN // TILE + t]
    for k, span in enumerate(SPANS):
        fits = number <= span
        if k:
            fits = fits & (number > SPANS[k - 1])

        @pl.when(fits)
        def _(span=span):
            start = jnp.minimum(low, LEN // KEYS - span) * KEYS
            with_keys(pl.multiple_of(start, KEYS), span * KEYS)


def reach(segment_row):
    heads_at, ends_at = segment_row[::TILE], segment_row[TILE - 1 :: TILE]
    low = jnp.sum((segment_row[None] < heads_at[:, None]).astype(jnp.int32), axis=1) // KEYS
    high = (jnp.sum((segment_row[None] <= ends_at[:, None]).astype(jnp.int32), axis=1) + KEYS - 1) // KEYS
    return low, high - low


def lay_out(order, my_dp, w_refs, w_all):
    span, half = D // len(order), len(order) // 2
    for j in range(len(order)):
        piece = w_refs[j][0, :span] if j < half else w_refs[half][j - half, 0, :span]
        w_all[rows_at(order, j, my_dp, span), :] = piece


def column_specs(w_parts, base):
    *ones, stacked = w_parts
    block = (1, *ones[0].shape[1:])
    return [pl.BlockSpec(block, lambda g, ids: (g + base, 0, 0))] * len(ones) + [
        pl.BlockSpec((stacked.shape[0], *block), lambda g, ids: (0, g + base, 0, 0))
    ]


def attend_kernel(order, ids, x_ref, *refs):
    n_w = len(order) // 2 + 1
    bias_ref, qf_ref, kf_ref, q_ref, k_ref, v_ref, ho_ref, lse_ref, w_all, keys, vals, rows = refs[n_w:]
    lay_out(order, ids[2], refs[:n_w], w_all)

    @pl.when(pl.program_id(0) == 0)
    def _():
        keys[:, PAIR:] = kf_ref[0]

    for t in range(LEN // TILE):
        at = slice(t * TILE, (t + 1) * TILE)
        got = dot(x_ref[0, at], w_all[...])
        q_ref[0, at] = (got[:, :PAIR] + bias_ref[0, 0:1]).astype(BF)
        key = got[:, PAIR : 2 * PAIR].astype(BF)
        k_ref[0, at] = key
        keys[at, :PAIR] = key
        val = (got[:, 2 * PAIR :] + bias_ref[0, 1:2]).astype(BF)
        v_ref[0, at] = val
        for head in range(2):
            vals[head, at, :] = jnp.where(head_mask((TILE, PAIR), head), val, BF(1))

    def one_tile(t, carry):
        at = pl.ds(pl.multiple_of(t * TILE, TILE), TILE)
        query = q_ref[0, at] * BF(0.125)

        def with_keys(start, count):
            near = pl.ds(start, count)
            low_lane = head_mask((TILE, PAIR), 0)
            wide0 = jnp.concatenate([jnp.where(head_mask((TILE, PAIR), 0), query, BF(0)), qf_ref[0, at]], axis=1)
            scores0 = dot(wide0, keys[near, :], NT)
            wide1 = jnp.concatenate([jnp.where(head_mask((TILE, PAIR), 1), query, BF(0)), qf_ref[0, at]], axis=1)
            scores1 = dot(wide1, keys[near, :], NT)
            top0 = jnp.max(scores0, axis=1, keepdims=True)
            probs0 = jnp.exp(scores0 - top0).astype(BF)
            top1 = jnp.max(scores1, axis=1, keepdims=True)
            probs1 = jnp.exp(scores1 - top1).astype(BF)
            out0 = dot(probs0, vals[0, near, :])
            out1 = dot(probs1, vals[1, near, :])
            total = pltpu.roll(jnp.where(low_lane, out1, out0), HEAD_DIM, 1)
            ho_ref[0, at] = (jnp.where(low_lane, out0, out1) / total).astype(BF)
            both = (jnp.where(low_lane, top0, top1) + jnp.log(total)).T
            lse_ref[0, 0:1, at] = both[0:1]
            lse_ref[0, 1:2, at] = both[HEAD_DIM : HEAD_DIM + 1]

        by_span(ids, t, with_keys)
        return carry

    lax.fori_loop(0, LEN // TILE, one_tile, 0)
    for head in range(2):
        for c in range(LEN // PAIR):
            at = head * (LEN // PAIR) + c
            rows[at : at + 1] = lse_ref[0, head : head + 1, c * PAIR : (c + 1) * PAIR]
    rest = rows[...]
    for k in range(3):
        part = rest.astype(BF)
        ho_ref[0, LEN + k * LOGS : LEN + (k + 1) * LOGS] = part
        rest = rest - part.astype(F32)


def sent_logs(ho_ref, logs):
    part = lambda k: ho_ref[0, LEN + k * LOGS : LEN + (k + 1) * LOGS].astype(F32)
    rows = part(0) + part(1) + part(2)
    for head in range(2):
        for c in range(LEN // PAIR):
            at = head * (LEN // PAIR) + c
            logs[2 + head : 3 + head, c * PAIR : (c + 1) * PAIR] = rows[at : at + 1]


def attend(ids, tokens, w_parts, bias, qf, kf, order, part=(0, 1), after=(), into=()):
    groups, tall, _ = w_parts[0].shape
    count = groups // part[1]
    base = part[0] * count
    pair = pl.BlockSpec((1, LEN, PAIR), lambda g, ids: (g, 0, 0))
    feats = pl.BlockSpec((1, LEN, PAIR), lambda g, ids: (ids[0], 0, 0))
    return kernel_call(
        functools.partial(attend_kernel, order),
        ids,
        (tokens, *w_parts, bias, qf, kf),
        [pl.BlockSpec((1, LEN, D), lambda g, ids: (ids[0], 0, 0))]
        + column_specs(w_parts, base)
        + [pl.BlockSpec((1, 2, PAIR), lambda g, ids: (g + base, 0, 0)), feats, feats],
        after,
        into,
        [
            pltpu.VMEM((D, 3 * PAIR), BF),
            pltpu.VMEM((LEN, 2 * PAIR), BF),
            pltpu.VMEM((2, LEN, PAIR), BF),
            pltpu.VMEM((LOGS, PAIR), F32),
        ],
        grid=(count,),
        out_specs=[
            pair,
            pair,
            pair,
            pl.BlockSpec((1, LEN + 3 * LOGS, PAIR), lambda g, ids: (g, 0, 0)),
            pl.BlockSpec((1, 2, LEN), lambda g, ids: (g, 0, 0)),
        ],
        out_shape=[jax.ShapeDtypeStruct((count, LEN, PAIR), BF)] * 3
        + [jax.ShapeDtypeStruct((count, LEN + 3 * LOGS, PAIR), BF), jax.ShapeDtypeStruct((count, 2, LEN), F32)],
        mib=60,
        name="attend",
    )


def norm_stats(value):
    center = value - jnp.mean(value, axis=-1, keepdims=True)
    spread = jnp.mean(center * center, axis=-1, keepdims=True)
    inverse = lax.rsqrt(spread + 1e-05)
    return center * inverse, inverse


def norm_backward(upstream, normal, inverse, gain):
    scaled = upstream * gain
    return inverse * (
        scaled
        - jnp.mean(scaled, axis=-1, keepdims=True)
        - normal * jnp.mean(scaled * normal, axis=-1, keepdims=True)
    )


CHUNK = 1024


def unpack(order, my_dp, w_refs, w_out, w_up, w_down):
    groups, span, _ = w_refs[0].shape
    wide = FF // groups
    for j in range(len(order)):
        row = rows_at(order, j, my_dp, span)
        for g in range(groups):
            w_out[row, g * PAIR : (g + 1) * PAIR] = w_refs[j][g, :, :PAIR]
            w_up[row, g * wide : (g + 1) * wide] = w_refs[j][g, :, PAIR : PAIR + wide]
            w_down[row, g * wide : (g + 1) * wide] = w_refs[j][g, :, PAIR + wide :]


def up_half(x_ref, heads, cot_ref, par_ref, ffb_ref, w_out, w_up, w_down, keep_hidden, slope_ref):
    gain_one, gain_two = par_ref[0:1], par_ref[1:2]
    shift_att, shift_ffn, shift_one, shift_two = (par_ref[k : k + 1] for k in range(2, 6))
    attention = dot(heads, w_out[...], NT) + shift_att
    normal_one, inverse_one = norm_stats(x_ref[0].astype(F32) + attention)
    normed = normal_one * gain_one + shift_one
    normed_low = normed.astype(BF)
    branch = shift_ffn
    for c in range(FF // CHUNK):
        at = slice(c * CHUNK, (c + 1) * CHUNK)
        pre = dot(normed_low, w_up[:, at]) + ffb_ref[:, at]
        phi = 0.5 * (1.0 + lax.erf(pre * 0.7071067811865476))
        hidden = (pre * phi).astype(BF)
        if keep_hidden is not None:
            keep_hidden(at, hidden)
        slope_ref[:, at] = phi + pre * jnp.exp(-0.5 * pre * pre) * 0.3989422804014327
        branch = branch + dot(hidden, w_down[:, at], NT)
    normal_two, inverse_two = norm_stats(normed + branch)
    final_low = (normal_two * gain_two + shift_two).astype(BF)
    upstream = cot_ref[0].astype(F32)
    g_final = norm_backward(upstream, normal_two, inverse_two, gain_two)
    return normal_one, inverse_one, normed_low, normal_two, final_low, upstream, g_final


def down_half(g_final, normal_one, inverse_one, par_ref, w_out, w_up, w_down, slope_ref, keep_pre):
    g_final_low = g_final.astype(BF)
    g_normed = g_final
    for c in range(FF // CHUNK):
        at = slice(c * CHUNK, (c + 1) * CHUNK)
        g_pre = (dot(g_final_low, w_down[:, at]) * slope_ref[:, at]).astype(BF)
        if keep_pre is not None:
            keep_pre(at, g_pre)
        g_normed = g_normed + dot(g_pre, w_up[:, at], NT)
    g_attention = norm_backward(g_normed, normal_one, inverse_one, par_ref[0:1])
    g_attention_low = g_attention.astype(BF)
    g_heads = dot(g_attention_low, w_out[...]).astype(BF)
    return g_final_low, g_normed, g_attention, g_attention_low, g_heads


def fold(acc, k, term, first):
    part = jnp.sum(term.reshape(TOKENS_AT_ONCE // 8, 8, D), axis=0)

    @pl.when(first)
    def _():
        acc[k] = part

    @pl.when(jnp.logical_not(first))
    def _():
        acc[k] += part


def is_middle(ids):
    return (ids[1] == 1) | (ids[1] == 2)


def heads_of(ids, ho_refs):
    there = [k ^ ids[0] ^ ids[1] for k in range(ho_refs[0].shape[0])]
    if len(ho_refs) == 1:
        return jnp.concatenate([ho_refs[0][k] for k in there], axis=1)
    return jnp.concatenate([jnp.where(is_middle(ids), ho_refs[1][k], ho_refs[0][k]) for k in there], axis=1)


def forward_kernel(order, ids, x_ref, ho_ref, *refs):
    half = len(order) // 2
    w_refs, refs = [*refs[:half], *(refs[half].at[j] for j in range(half))], refs[half + 1 :]
    par_ref, ffb_ref, out_ref, w_out, w_up, w_down = refs

    @pl.when(pl.program_id(0) == 0)
    def _():
        unpack(order, ids[2], w_refs, w_out, w_up, w_down)

    shift_att, shift_ffn, shift_one, shift_two = (par_ref[k : k + 1] for k in range(2, 6))
    attention = dot(heads_of(ids, [ho_ref]), w_out[...], NT) + shift_att
    normed = norm_stats(x_ref[0].astype(F32) + attention)[0] * par_ref[0:1] + shift_one
    normed_low = normed.astype(BF)
    branch = shift_ffn
    for c in range(FF // CHUNK):
        at = slice(c * CHUNK, (c + 1) * CHUNK)
        pre = dot(normed_low, w_up[:, at]) + ffb_ref[:, at]
        hidden = (pre * (0.5 * (1.0 + lax.erf(pre * 0.7071067811865476)))).astype(BF)
        branch = branch + dot(hidden, w_down[:, at], NT)
    out_ref[...] = (norm_stats(normed + branch)[0] * par_ref[1:2] + shift_two).astype(BF)


def forward_only(ids, tokens, heads_out, w_parts, params, ff_shift, order, after=(), into=()):
    full = lambda shape: pl.BlockSpec(shape, lambda t, ids: (0,) * len(shape))
    return kernel_call(
        functools.partial(forward_kernel, order),
        ids,
        (tokens, heads_out, *w_parts, params, ff_shift),
        [
            pl.BlockSpec((1, TOKENS_AT_ONCE, D), lambda t, ids: (ids[0], t, 0)),
            pl.BlockSpec((heads_out.shape[0], TOKENS_AT_ONCE, PAIR), lambda t, ids: (0, t, 0)),
        ]
        + [full(a.shape) for a in w_parts]
        + [full((6, D)), full((1, FF))],
        after,
        into,
        [pltpu.VMEM((D, D), BF), pltpu.VMEM((D, FF), BF), pltpu.VMEM((D, FF), BF)],
        grid=(LEN // TOKENS_AT_ONCE,),
        out_specs=[pl.BlockSpec((TOKENS_AT_ONCE, D), lambda t, ids: (t, 0))],
        out_shape=[jax.ShapeDtypeStruct((LEN, D), BF)],
        mib=60,
        name="forward_only",
    )[0]


def tokenwise_kernel(order, n_ho, keep, ids, x_ref, cot_ref, *refs):
    ho_refs, refs = refs[:n_ho], refs[n_ho:]
    half = len(order) // 2
    w_refs, refs = [*refs[:half], *(refs[half].at[j] for j in range(half))], refs[half + 1 :]
    par_ref, ffb_ref, full_ref, gatt_ref, gh_ref, *refs = refs
    if keep:
        near_ref, far_ref, sums_ref, ff_ref, w_out, w_up, w_down, slope, *refs = refs
        acc, ffs_ref, hid_all, pre_all, ho_all, up_t, down_t, att_t, gw_all = refs
    else:
        w_out, w_up, w_down, slope = refs
    step = pl.program_id(0)
    tiles = LEN // TOKENS_AT_ONCE
    groups = gh_ref.shape[0]
    my_dp = ids[2]

    @pl.when(step == 0)
    def _():
        unpack(order, my_dp, w_refs, w_out, w_up, w_down)

    def tokens_step():
        rows = pl.ds(pl.multiple_of(jnp.minimum(step, tiles - 1) * TOKENS_AT_ONCE, TOKENS_AT_ONCE), TOKENS_AT_ONCE)
        heads = heads_of(ids, ho_refs)
        keep_hidden = keep_pre = None
        if keep:

            def keep_hidden(at, hidden):
                hid_all[rows, at] = hidden

            def keep_pre(at, g_pre):
                pre_all[rows, at] = g_pre
                here = jnp.sum(g_pre.astype(F32), axis=0, keepdims=True)

                @pl.when(step == 0)
                def _():
                    ffs_ref[:, at] = here

                @pl.when(step > 0)
                def _():
                    ffs_ref[:, at] += here

        normal_one, inverse_one, normed_low, normal_two, final_low, upstream, g_final = up_half(
            x_ref, heads, cot_ref, par_ref, ffb_ref, w_out, w_up, w_down, keep_hidden, slope
        )
        full_ref[0] = final_low
        g_final_low, g_normed, g_attention, g_attention_low, g_heads = down_half(
            g_final, normal_one, inverse_one, par_ref, w_out, w_up, w_down, slope, keep_pre
        )
        gatt_ref[...] = g_attention
        for g in range(groups):
            gh_ref[g] = g_heads[:, g * PAIR : (g + 1) * PAIR]
        if keep:
            ho_all[rows, :] = heads
            down_t[:, rows] = g_final_low.T
            att_t[:, rows] = g_attention_low.T
            up_t[:, rows] = normed_low.T
            terms = (g_normed * normal_one, upstream * normal_two, g_attention, g_final, g_normed, upstream)
            for k, term in enumerate(terms):
                fold(acc, k, term, step == 0)

            @pl.when(step == tiles - 1)
            def _():
                for k in range(6):
                    total = jnp.sum(acc[k], axis=0, keepdims=True)
                    for c in range(D // PAIR):
                        at = k * (D // PAIR) + c
                        sums_ref[at : at + 1] = total[:, c * PAIR : (c + 1) * PAIR]
                per_group = FF // groups // PAIR
                for c in range(FF // PAIR):
                    ff_ref[c // per_group, c % per_group : c % per_group + 1] = ffs_ref[:, c * PAIR : (c + 1) * PAIR]

    if not keep:
        tokens_step()
        return

    pl.when(step < tiles)(tokens_step)

    @pl.when(step >= tiles)
    def _():
        half, _, span, _ = near_ref.shape
        wide = FF // groups
        block = pl.ds(pl.multiple_of((step - tiles) * wide, wide), wide)
        pair = pl.ds(pl.multiple_of((step - tiles) * PAIR, PAIR), PAIR)
        gw_all[:, :PAIR] = dot(att_t[...], ho_all[:, pair]).astype(BF)
        gw_all[:, PAIR : PAIR + wide] = dot(up_t[...], pre_all[:, block]).astype(BF)
        gw_all[:, PAIR + wide :] = dot(down_t[...], hid_all[:, block]).astype(BF)
        for j in range(half):
            near_ref[j, 0] = gw_all[rows_at(order, j, my_dp, span), :]
            far_ref[j, 0] = gw_all[rows_at(order, half + j, my_dp, span), :]


def tokenwise(ids, tokens, heads_out, cotangent, w_parts, params, ff_shift, order, keep, after=(), into=()):
    tiles = LEN // TOKENS_AT_ONCE
    groups, span, cols = w_parts[0].shape
    early = lambda t: jnp.minimum(t, tiles - 1)
    late = lambda t: jnp.maximum(t - tiles, 0)
    full = lambda shape: pl.BlockSpec(shape, lambda t, ids: (0,) * len(shape))
    row = pl.BlockSpec((1, TOKENS_AT_ONCE, D), lambda t, ids: (ids[0], early(t), 0))
    flat = pl.BlockSpec((TOKENS_AT_ONCE, D), lambda t, ids: (early(t), 0))
    pairs = lambda n: pl.BlockSpec((n, TOKENS_AT_ONCE, PAIR), lambda t, ids: (0, early(t), 0))
    out_specs = [row, flat, pairs(groups)]
    out_shape = [
        jax.ShapeDtypeStruct(tokens.shape, BF),
        jax.ShapeDtypeStruct((LEN, D), F32),
        jax.ShapeDtypeStruct((groups, LEN, PAIR), BF),
    ]
    scratch = [
        pltpu.VMEM((D, D), BF),
        pltpu.VMEM((D, FF), BF),
        pltpu.VMEM((D, FF), BF),
        pltpu.VMEM((TOKENS_AT_ONCE, FF), F32),
    ]
    if keep:
        half = len(order) // 2
        part = pl.BlockSpec((half, 1, span, cols), lambda t, ids: (0, late(t), 0, 0))
        norm_sums, ff_sums = (6 * D // PAIR, PAIR), (groups, FF // groups // PAIR, PAIR)
        out_specs += [part, part, full(norm_sums), full(ff_sums)]
        out_shape += [jax.ShapeDtypeStruct((half, groups, span, cols), BF)] * 2
        out_shape += [jax.ShapeDtypeStruct(norm_sums, F32), jax.ShapeDtypeStruct(ff_sums, F32)]
        scratch += [
            pltpu.VMEM((6, 8, D), F32),
            pltpu.VMEM((1, FF), F32),
            pltpu.VMEM((LEN, FF), BF),
            pltpu.VMEM((LEN, FF), BF),
            pltpu.VMEM((LEN, D), BF),
            pltpu.VMEM((D, LEN), BF),
            pltpu.VMEM((D, LEN), BF),
            pltpu.VMEM((D, LEN), BF),
            pltpu.VMEM((D, cols), BF),
        ]
    return kernel_call(
        functools.partial(tokenwise_kernel, order, len(heads_out), keep),
        ids,
        (tokens, cotangent, *heads_out, *w_parts, params, ff_shift),
        [row, row]
        + [pairs(a.shape[0]) for a in heads_out]
        + [full(a.shape) for a in w_parts]
        + [full((6, D)), full((1, FF))],
        after,
        into,
        scratch,
        grid=(tiles + groups if keep else tiles,),
        out_specs=out_specs,
        out_shape=out_shape,
        mib=60,
        name="tokenwise_keep" if keep else "tokenwise",
    )


def attend_back_kernel(order, keep, whole_row, ids, x_ref, *refs):
    n_w = len(order) // 2 + 1
    w_refs, (qf_ref, kf_ref, *refs) = refs[:n_w], refs[n_w:]
    if keep:
        q_ref, k_ref, v_ref, ho_ref, lse_ref, sums_ref, ff_ref, gh_ref, gatt_ref, *refs = refs
        tg_ref, send_ref, again_ref, near_ref, far_ref, *refs = refs
        w_all, keys, keys_t, delta, dk, dv, grads, x_t, gw_all, extra = refs
    else:
        bias_ref, ho_ref, ho_mid, gh_ref, gatt_ref, tg_ref, *refs = refs
        w_all, keys, keys_t, delta, dk, dv, grads, q_ref, k_ref, v_ref = refs
    my_dp = ids[2]
    if whole_row:
        tg_ref = tg_ref.at[0]
    lay_out(order, my_dp, w_refs, w_all)

    @pl.when(pl.program_id(0) == 0)
    def _():
        keys[:, PAIR:] = kf_ref[0]
        tg_ref[...] = gatt_ref[...]
        if keep:
            x_t[...] = x_ref[0].T
            extra[...] = jnp.zeros_like(extra)
            extra[:12, :PAIR] = sums_ref[:12]
            extra[:12, PAIR : 2 * PAIR] = sums_ref[12:]

    if keep:
        heads = ho_ref[0, :LEN]
        delta[2:4] = lse_ref[0]
    else:
        for t in range(LEN // TILE):
            at = slice(t * TILE, (t + 1) * TILE)
            got = dot(x_ref[0, at], w_all[...])
            q_ref[0, at] = (got[:, :PAIR] + bias_ref[0, 0:1]).astype(BF)
            k_ref[0, at] = got[:, PAIR : 2 * PAIR].astype(BF)
            v_ref[0, at] = (got[:, 2 * PAIR :] + bias_ref[0, 1:2]).astype(BF)
        heads = jnp.where(is_middle(ids), ho_mid[0, :LEN], ho_ref[0, :LEN])

        @pl.when(is_middle(ids))
        def _():
            sent_logs(ho_mid, delta)

        @pl.when(jnp.logical_not(is_middle(ids)))
        def _():
            sent_logs(ho_ref, delta)

    keys[:, :PAIR] = k_ref[0]
    keys_t[...] = k_ref[0].T
    prod = (gh_ref[0].astype(F32) * heads.astype(F32)).T
    delta[0:1] = jnp.sum(prod[:HEAD_DIM], axis=0, keepdims=True)
    delta[1:2] = jnp.sum(prod[HEAD_DIM:], axis=0, keepdims=True)
    dk[...] = jnp.zeros_like(dk)
    dv[...] = jnp.zeros_like(dv)

    def one_tile(t, carry):
        at = pl.ds(pl.multiple_of(t * TILE, TILE), TILE)
        query, back = q_ref[0, at], gh_ref[0, at]

        def with_keys(start, count):
            near = pl.ds(start, count)
            mine0 = jnp.where(head_mask((TILE, PAIR), 0), query, BF(0))
            back0 = jnp.where(head_mask((TILE, PAIR), 0), back, BF(0))
            wide0 = jnp.concatenate([mine0 * BF(0.125), qf_ref[0, at]], axis=1)
            scores0 = dot(keys[near, :], wide0, NT)
            g_probs0 = dot(v_ref[0, near], back0, NT)
            mine1 = jnp.where(head_mask((TILE, PAIR), 1), query, BF(0))
            back1 = jnp.where(head_mask((TILE, PAIR), 1), back, BF(0))
            wide1 = jnp.concatenate([mine1 * BF(0.125), qf_ref[0, at]], axis=1)
            scores1 = dot(keys[near, :], wide1, NT)
            g_probs1 = dot(v_ref[0, near], back1, NT)
            probs0 = jnp.exp(scores0 - delta[2:3, at])
            g_raw0 = (probs0 * (g_probs0 - delta[0 : 0 + 1, at])).astype(BF)
            low0 = probs0.astype(BF)
            probs1 = jnp.exp(scores1 - delta[3:4, at])
            g_raw1 = (probs1 * (g_probs1 - delta[1 : 1 + 1, at])).astype(BF)
            low1 = probs1.astype(BF)
            d_query0 = dot(keys_t[0 * HEAD_DIM : (0 + 1) * HEAD_DIM, near], g_raw0)
            d_query1 = dot(keys_t[1 * HEAD_DIM : (1 + 1) * HEAD_DIM, near], g_raw1)
            dv[near, :] += dot(jnp.concatenate([low0, low1], axis=1), jnp.concatenate([back0, back1], axis=0))
            dk[near, :] += dot(jnp.concatenate([g_raw0, g_raw1], axis=1), jnp.concatenate([mine0, mine1], axis=0))
            d_query = [d_query0, d_query1]
            grads[at, :PAIR] = (jnp.concatenate(d_query, axis=0).T * 0.125).astype(BF)

        by_span(ids, t, with_keys)
        return carry

    lax.fori_loop(0, LEN // TILE, one_tile, 0)
    grads[:, PAIR : 2 * PAIR] = (dk[...] * 0.125).astype(BF)
    grads[:, 2 * PAIR :] = dv[...].astype(BF)
    for t in range(LEN // TILE):
        at = slice(t * TILE, (t + 1) * TILE)
        tg_ref[at, :] += dot(grads[at, :], w_all[...], NT)
    if keep:
        half, span = len(order) // 2, D // len(order)
        gw_all[...] = dot(x_t[...], grads[...]).astype(BF)
        extra[0:1, 2 * PAIR :] = jnp.sum(grads[:, :PAIR].astype(F32), axis=0, keepdims=True)
        extra[1:2, 2 * PAIR :] = jnp.sum(grads[:, 2 * PAIR :].astype(F32), axis=0, keepdims=True)
        extra[2 : 2 + ff_ref.shape[1], 2 * PAIR :] = ff_ref[0]
        vectors = extra[...].astype(BF)
        for j in range(half):
            near_ref[j, 0, :span] = gw_all[rows_at(order, j, my_dp, span), :]
            near_ref[j, 0, span:] = vectors
            far_ref[j, 0, :span] = gw_all[rows_at(order, half + j, my_dp, span), :]
            far_ref[j, 0, span:] = vectors

        @pl.when(pl.program_id(0) == pl.num_programs(0) - 1)
        def _():
            send = tg_ref[...].astype(BF)
            send_ref[...] = send
            again_ref[...] = send


def attend_back(ids, tokens, w_parts, qf, kf, saved, g_heads, g_att, order, keep, part=(0, 1), after=(), into=()):
    groups, tall, _ = w_parts[0].shape
    half = len(order) // 2
    count = groups // part[1]
    base = part[0] * count
    whole_row = part[0] == part[1] - 1
    there = lambda g, ids: (g + base) ^ ids[0] ^ ids[1]
    pair = pl.BlockSpec((1, LEN, PAIR), lambda g, ids: (there(g, ids), 0, 0))
    pair_logs = pl.BlockSpec((1, LEN + 3 * LOGS, PAIR), lambda g, ids: (there(g, ids), 0, 0))
    feats = pl.BlockSpec((1, LEN, PAIR), lambda g, ids: (ids[0], 0, 0))
    full = pl.BlockSpec((LEN, D), lambda g, ids: (0, 0))
    out_specs = [pl.BlockSpec((1, LEN, D), lambda g, ids: (ids[0], 0, 0)) if whole_row else full]
    out_shape = [jax.ShapeDtypeStruct(tokens.shape if whole_row else (LEN, D), F32)]
    scratch = [
        pltpu.VMEM((D, 3 * PAIR), BF),
        pltpu.VMEM((LEN, 2 * PAIR), BF),
        pltpu.VMEM((PAIR, LEN), BF),
        pltpu.VMEM((4, LEN), F32),
        pltpu.VMEM((LEN, PAIR), F32),
        pltpu.VMEM((LEN, PAIR), F32),
        pltpu.VMEM((LEN, 3 * PAIR), BF),
    ]
    if keep:
        saved_specs = [
            pair,
            pair,
            pair,
            pair_logs,
            pl.BlockSpec((1, 2, LEN), lambda g, ids: (g, 0, 0)),
            pl.BlockSpec(saved[5].shape, lambda g, ids: (0, 0)),
            pl.BlockSpec((1, *saved[6].shape[1:]), lambda g, ids: (g, 0, 0)),
        ]
        out_specs += [full, full] + [pl.BlockSpec((half, 1, tall, 3 * PAIR), lambda g, ids: (0, g, 0, 0))] * 2
        out_shape += [jax.ShapeDtypeStruct((LEN, D), BF)] * 2
        out_shape += [jax.ShapeDtypeStruct((half, groups, tall, 3 * PAIR), BF)] * 2
        scratch += [pltpu.VMEM((D, LEN), BF), pltpu.VMEM((D, 3 * PAIR), BF), pltpu.VMEM((EXTRA, 3 * PAIR), F32)]
    else:
        saved_specs = [pl.BlockSpec((1, 2, PAIR), lambda g, ids: (g + base, 0, 0)), pair_logs, pair_logs]
        scratch += [pltpu.VMEM((1, LEN, PAIR), BF)] * 3
    return kernel_call(
        functools.partial(attend_back_kernel, order, keep, whole_row),
        ids,
        (tokens, *w_parts, qf, kf, *saved, g_heads, g_att),
        [pl.BlockSpec((1, LEN, D), lambda g, ids: (ids[0], 0, 0))]
        + column_specs(w_parts, base)
        + [feats, feats]
        + saved_specs
        + [pl.BlockSpec((1, LEN, PAIR), lambda g, ids: (g + base, 0, 0)), full],
        after,
        into,
        scratch,
        grid=(count,),
        out_specs=out_specs,
        out_shape=out_shape,
        mib=60,
        flops=20_000_000_000,
        name="attend_back_keep" if keep else "attend_back",
    )


RATES = (D ** (-0.5), (D // 64) ** (-0.5), D ** (-0.5), FF ** (-0.5), 0.3, 0.3, 0.3, 0.3)
DECAYS = (0.01, 0.01, 0.01, 0.01, 0.0, 0.0, 0.0, 0.0)


def adam_step(weight, grad_sum, first, second, rate, decay):
    first_new = beta_one * first + (1.0 - beta_one) * grad_sum
    second_new = beta_two * second + (1.0 - beta_two) * grad_sum * grad_sum
    first_hat = first_new / (1.0 - beta_one**STEP)
    second_hat = second_new / (1.0 - beta_two**STEP)
    weight_new = weight - rate * (first_hat / (jnp.sqrt(second_hat) + 1e-08) + decay * weight)
    return (weight_new, first_new, second_new)


def adam_kernel(ids, *refs):
    terms, olds, news, whole, mine = refs[:4], refs[4:28], refs[28:52], refs[52], refs[53]
    span = olds[2].shape[0]
    wide, per = olds[2].shape[1], olds[5].shape[1]
    total_ab = lambda at: terms[0][:, at].astype(F32) + terms[1][:, at].astype(F32)
    total_qkv = lambda rows, at: terms[2][rows, at].astype(F32) + terms[3][rows, at].astype(F32)

    def step(slot, at, grad):
        old = [olds[8 * k + slot][at] for k in range(3)]
        new = adam_step(old[0], grad, old[1], old[2], RATES[slot], DECAYS[slot])
        for k in range(3):
            news[8 * k + slot][at] = new[k]

    for k in range(3):
        step(0, k, total_qkv(slice(0, span), slice(k * PAIR, (k + 1) * PAIR)))
    step(1, ..., total_ab(slice(0, PAIR)))
    step(2, ..., total_ab(slice(PAIR, PAIR + wide)))
    step(3, ..., total_ab(slice(PAIR + wide, PAIR + 2 * wide)))
    whole[...] = total_qkv(slice(span, span + EXTRA), slice(0, 3 * PAIR))
    first_norm = ids[2] * span
    turns = (first_norm, first_norm, ids[2] * per)
    for k in range(3):
        back = lax.rem(PAIR - lax.rem(turns[k], PAIR), PAIR)
        mine[k * EXTRA : (k + 1) * EXTRA] = pltpu.roll(whole[:, k * PAIR : (k + 1) * PAIR], back, 1)
    for k in range(6):
        at = (k // 3) * EXTRA + (k % 3) * (D // PAIR) + first_norm // PAIR
        slot, row = (6, k) if k < 2 else (7, k - 2)
        step(slot, slice(row, row + 1), mine[pl.ds(at, 1), :span])
    pieces = lambda row: [mine[2 * EXTRA + row : 2 * EXTRA + row + 1, h * HEAD_DIM : h * HEAD_DIM + per] for h in (0, 1)]
    for kind in range(2):
        for head, grad in enumerate(pieces(kind)):
            step(4, (kind, slice(head, head + 1)), grad)
    for row in range(olds[5].shape[0] // 2):
        for head, grad in enumerate(pieces(2 + row)):
            step(5, slice(2 * row + head, 2 * row + head + 1), grad)


def adam(ids, last, after, *sets):
    turn = lambda a: (a[0].transpose(1, 0, 2), a[1].T, a[2], a[3].T, *a[4:])
    olds = [array for group in sets for array in turn(group)]
    inputs = (*last[0], *last[1], *olds)
    full = lambda a: pl.BlockSpec(a.shape, lambda t, ids: (0,) * a.ndim)
    news = kernel_call(
        adam_kernel, ids, inputs, [full(a) for a in inputs], after, (),
        [pltpu.VMEM((EXTRA, 3 * PAIR), F32), pltpu.VMEM((3 * EXTRA, PAIR), F32)],
        grid=(1,),
        out_specs=[full(a) for a in olds],
        out_shape=[jax.ShapeDtypeStruct(a.shape, F32) for a in olds],
        mib=60,
        name="adam",
    )
    return [array for k in range(3) for array in turn(news[8 * k : 8 * k + 8])]


def rows_of(ids):
    z = ids[1]
    by = lambda a, b, c, d: jnp.where(z == 0, a, jnp.where(z == 1, b, jnp.where(z == 2, c, d)))
    return z, by(1, 2, 1, 2), by(2, 0, 3, 1), by(3, 3, 0, 0)


PLACED = 256


def place_kernel(ids, grad_straight, grad_middle, grad_end, out_straight, out_middle, out_end, _, __, tg_ref, lo_ref, sems, one, two, three, four):
    t, last = pl.program_id(0), pl.num_programs(0) - 1
    _, _, straight, through = rows_of(ids)
    slot = lax.rem(t, 2)
    inside = is_middle(ids)

    def copies(step, slot):
        ways = ((one, tg_ref, straight), (two, tg_ref, through), (three, lo_ref, straight), (four, lo_ref, through))
        return [
            pltpu.make_async_copy(buf.at[slot], ref.at[row, pl.ds(step * PLACED, PLACED)], sems.at[k, slot])
            for k, (buf, ref, row) in enumerate(ways)
        ]

    @pl.when(t >= 2)
    def _():
        for copy in copies(t - 2, slot):
            copy.wait()

    one[slot] = grad_straight[...].astype(F32)
    two[slot] = jnp.where(inside, grad_middle[...], grad_end[...]).astype(F32)
    three[slot] = out_straight[...]
    four[slot] = jnp.where(inside, out_middle[...], out_end[...])
    for copy in copies(t, slot):
        copy.start()

    @pl.when(t == last)
    def _():
        for copy in copies(t - 1, 1 - slot) + copies(t, slot):
            copy.wait()


def place(ids, grads, outs, tokens_grad, layer_out):
    block = pl.BlockSpec((PLACED, D), lambda t, ids: (t, 0))
    chosen = [
        pl.BlockSpec((PLACED, D), lambda t, ids: (jnp.where(is_middle(ids), t, 0), 0)),
        pl.BlockSpec((PLACED, D), lambda t, ids: (jnp.where(is_middle(ids), 0, t), 0)),
    ]
    anywhere = pl.BlockSpec(memory_space=pl.ANY)
    return pl.pallas_call(
        place_kernel,
        grid_spec=pltpu.PrefetchScalarGridSpec(
            num_scalar_prefetch=1,
            grid=(LEN // PLACED,),
            in_specs=[block, *chosen, block, *chosen] + [anywhere] * 2,
            out_specs=[anywhere, anywhere],
            scratch_shapes=[
                pltpu.SemaphoreType.DMA((4, 2)),
                pltpu.VMEM((2, PLACED, D), F32),
                pltpu.VMEM((2, PLACED, D), F32),
                pltpu.VMEM((2, PLACED, D), BF),
                pltpu.VMEM((2, PLACED, D), BF),
            ],
        ),
        out_shape=[jax.ShapeDtypeStruct(a.shape, a.dtype) for a in (tokens_grad, layer_out)],
        input_output_aliases={7: 0, 8: 1},
        compiler_params=vmem(60),
        name="place",
    )(ids, *grads, *outs, tokens_grad, layer_out)


def pack_kernel(qkv, out_t, up, down_t, qv, ff, gains, shifts, first_ref, second_ref):
    span, wide = up.shape
    for k in range(3):
        first_ref[:span, k * PAIR : (k + 1) * PAIR] = qkv[k].astype(BF)
    first_ref[span:, :] = jnp.zeros((EXTRA, 3 * PAIR), BF)
    first_ref[span : span + 2, :span] = gains[...].astype(BF)
    first_ref[span + 2 : span + 6, :span] = shifts[...].astype(BF)
    first_ref[span : span + ff.shape[0], PAIR : PAIR + ff.shape[1]] = ff[...].astype(BF)
    for k in range(2):
        first_ref[span + 2 * k : span + 2 * k + 2, 2 * PAIR : 2 * PAIR + qv.shape[2]] = qv[k].astype(BF)
    second_ref[:, :PAIR] = out_t[...].astype(BF)
    second_ref[:, PAIR : PAIR + wide] = up[...].astype(BF)
    second_ref[:, PAIR + wide :] = down_t[...].astype(BF)


def pack(w_qkv, w_out, w_up, w_down, qv_bias, ff_bias, norm_gains, norm_shifts):
    span, wide = w_up.shape
    return pl.pallas_call(
        pack_kernel,
        out_shape=[
            jax.ShapeDtypeStruct((span + EXTRA, 3 * PAIR), BF),
            jax.ShapeDtypeStruct((span, PAIR + 2 * wide), BF),
        ],
        name="pack",
    )(w_qkv.transpose(1, 0, 2), w_out.T, w_up, w_down.T, qv_bias, ff_bias, norm_gains, norm_shifts)


def features(segment_ids, pad_lengths):
    place = jnp.arange(LEN, dtype=jnp.int32)[None, :, None]
    lane = jnp.arange(PAIR, dtype=jnp.int32)[None, None, :]
    segment = segment_ids[:, :, None]
    padding = place >= (LEN - pad_lengths)[:, None, None]
    high, low = place // 32, place % 32
    hit = (
        ((lane < 4) & (lane == segment))
        | ((lane >= 4) & (lane < 36) & (lane - 4 == high))
        | ((lane >= 36) & (lane < 68) & (lane - 36 == low))
    )
    counts = jnp.where(padding, (lane >= 4) & (lane < 68), lane < 4)
    qf = jnp.where(hit, -FAR, 0.0).astype(BF)
    kf = jnp.where(counts & ~hit, 1.0, 0.0).astype(BF)
    return qf, kf


def per_device(
    tokens, segment_ids, pad_lengths, cotangent,
    w_qkv, w_out, w_up, w_down, qv_bias, ff_bias, norm_gains, norm_shifts,
    first_qkv, first_out, first_up, first_down, first_qv_bias, first_ff_bias, first_gains, first_shifts,
    second_qkv, second_out, second_up, second_down, second_qv_bias, second_ff_bias, second_gains, second_shifts,
):
    n_dp, n_mp = lax.axis_size("dp"), lax.axis_size("mp")
    my_dp, my_mp = lax.axis_index("dp"), lax.axis_index("mp")
    order = dp_order(n_dp)
    half = n_dp // 2
    span = D // n_dp
    wide, per = FF // n_mp, HEAD_DIM // n_dp
    ff_rows = wide // HEAD_DIM

    places = ((jnp.array(order, jnp.int32)[:, None] ^ my_dp) == jnp.arange(n_dp, dtype=jnp.int32)[None]).astype(BF)

    def to_near(value):
        return flip(value, "dp", routes(n_dp)[0])

    part_qkv, part_ab = pack(w_qkv, w_out, w_up, w_down, qv_bias, ff_bias, norm_gains, norm_shifts)
    far_qkv = gather_far(gather_mp(part_qkv))
    all_qkv = [*far_qkv, to_near(jnp.stack(far_qkv))]
    far_ab = gather_far(gather_mp_steps(part_ab))
    small_here = jnp.concatenate(
        [jnp.stack([a[:, span : span + 8] for a in all_qkv[:half]]), all_qkv[half][:, :, span : span + 8]]
    ).reshape(n_dp, -1)
    small_all = dot(places, small_here, (((0,), (0,)), ((), ()))).reshape(n_dp, n_mp, 8, 3 * PAIR)
    bias_rows = (
        small_all[:, :, :4, 2 * PAIR : 2 * PAIR + per].reshape(n_dp, n_mp, 2, 2, per).transpose(1, 2, 3, 0, 4)
    ).reshape(n_mp, 2, PAIR)
    ff_shift = small_all[:, :, :ff_rows, PAIR : PAIR + per].transpose(1, 2, 0, 3).reshape(1, FF)
    params = small_all[:, 0, :6, :span].transpose(1, 0, 2).reshape(6, D)
    qf, kf = features(segment_ids, pad_lengths)

    def ids_of(row):
        low, number = reach(lax.dynamic_index_in_dim(segment_ids, row, 0, keepdims=False))
        return jnp.concatenate([jnp.stack([row, my_mp, my_dp]).astype(jnp.int32), low, number])

    second = jnp.where((my_mp == 0) | (my_mp == 2), 1, 2)
    mine, other = ids_of(my_mp), ids_of(second)

    saved = attend(mine, tokens, all_qkv, bias_rows, qf, kf, order)
    far_ab = gate(far_ab, saved[4])
    all_ab = [*far_ab, to_near(jnp.stack(far_ab))]
    to_ends, to_middles = [(1, 0), (2, 3)], [(1, 2), (2, 1)]
    across, straight = [(0, 2), (3, 1)], [(0, 1), (3, 2), (1, 3), (2, 0)]
    heads_end, heads_mid = (lax.ppermute(saved[3], "mp", way) for way in (to_ends, to_middles))
    own_out = forward_only(mine, tokens, saved[3], all_ab, params, ff_shift, order)
    out_middle = lax.ppermute(own_out, "mp", across)
    layer_out, g_att, g_heads, near_ab, far_grad_ab, sums, ff_sums = tokenwise(
        mine, tokens, [saved[3]], cotangent, all_ab, params, ff_shift, order, True, after=(own_out,)
    )
    out_straight = lax.ppermute(own_out, "mp", straight)
    came_ab = to_near(far_grad_ab)
    tokens_grad, own_send, send_again, near_qkv, far_grad_qkv = attend_back(
        mine, tokens, all_qkv, qf, kf, (*saved, sums, ff_sums), g_heads, g_att, order, True,
        after=(heads_end, heads_mid, out_middle),
    )
    held_ab = [add_up(near_ab[j], came_ab[j]).astype(BF) for j in range(half)]
    own_send, out_middle, out_straight, far_grad_qkv = gate((own_send, out_middle, out_straight, far_grad_qkv))
    came_qkv = to_near(far_grad_qkv)
    grad_middle = lax.ppermute(own_send, "mp", across)
    out_end = lax.ppermute(out_middle, "mp", to_ends)
    kept_ab, sent_ab = scatter_start(held_ab)
    late = len(sent_ab) - len(kept_ab)
    far_sums_ab = [flip(value, "dp", y) for value, y in sent_ab[:late]]
    layer_out, g_att2, g_heads2 = tokenwise(
        other, tokens, [heads_end, heads_mid], cotangent, all_ab, params, ff_shift, order, False,
        after=(own_send,), into=((layer_out, 0),),
    )
    late_ab = [value for value, _ in sent_ab[late:]]
    n_late = len(late_ab)
    send_again, grad_middle, out_end, came_qkv, *moved = gate(
        (send_again, grad_middle, out_end, came_qkv, *late_ab, *far_sums_ab), g_heads2
    )
    late_ab, far_sums_ab = moved[:n_late], moved[n_late:]
    grad_straight = lax.ppermute(send_again, "mp", straight)
    grad_end = lax.ppermute(grad_middle, "mp", to_ends)
    late_ab = [flip(value, "dp", y) for value, (_, y) in zip(late_ab, sent_ab[late:])]
    far_bits = [bit for group in routes(n_dp)[1] for bit in group]
    kept_qkv = near_qkv.shape[0] // 2
    held_qkv = [add_up(near_qkv[k * kept_qkv : (k + 1) * kept_qkv], came_qkv[k * kept_qkv : (k + 1) * kept_qkv]).astype(BF) for k in range(2)]
    came_half = flip(held_qkv[1], "dp", far_bits[-1])
    of_other = (bias_rows, heads_end, heads_mid)
    (half_grad,) = attend_back(
        other, tokens, all_qkv, qf, kf, of_other, g_heads2, g_att2, order, False, (0, 2),
        after=(grad_middle, *held_qkv),
    )
    came_half, *late_ab = gate((came_half, *late_ab), half_grad)
    column_ab = scatter_end(kept_ab, [*far_sums_ab, *late_ab])
    column_qkv = add_up(held_qkv[0], came_half).astype(BF)
    for bit in far_bits[-2::-1]:
        kept_qkv = column_qkv.shape[0] // 2
        came_half = flip(column_qkv[kept_qkv:], "dp", bit)
        column_qkv = (column_qkv[:kept_qkv], came_half)
        if bit != far_bits[0]:
            column_qkv = add_up(*column_qkv).astype(BF)
    come_mp = lambda a: flip(jnp.stack([a[1], a[3]]), "mp", 1)
    keep_mp = lambda a, b: add_up(jnp.stack([a[0], a[2]]), b).astype(BF)
    came_mp_ab = come_mp(column_ab)
    (tokens_grad,) = attend_back(
        other, tokens, all_qkv, qf, kf, of_other, g_heads2, half_grad, order, False, (1, 2),
        after=(column_qkv[0],), into=((tokens_grad, 0),),
    )
    came_mp_ab, came_half = gate((came_mp_ab, column_qkv[1]), tokens_grad)
    column_qkv = add_up(column_qkv[0], came_half)[0].astype(BF)
    pair_ab, pair_qkv = keep_mp(column_ab, came_mp_ab), keep_mp(column_qkv, come_mp(column_qkv))
    last = [(a[0], flip(a[1], "mp", 2)) for a in (pair_ab, pair_qkv)]
    tokens_grad, layer_out = place(
        mine, (grad_straight, grad_middle, grad_end), (out_straight, out_middle, out_end), tokens_grad, layer_out
    )

    masters = (w_qkv, w_out, w_up, w_down, qv_bias, ff_bias, norm_gains, norm_shifts)
    firsts = (first_qkv, first_out, first_up, first_down, first_qv_bias, first_ff_bias, first_gains, first_shifts)
    seconds = (second_qkv, second_out, second_up, second_down, second_qv_bias, second_ff_bias, second_gains, second_shifts)
    updated = adam(mine, last, (tokens_grad,), masters, firsts, seconds)
    return (layer_out, tokens_grad, *updated)


def solution(mesh):
    weights = (
        P("dp", None, "mp"),
        P("mp", "dp"),
        P("dp", "mp"),
        P("mp", "dp"),
        P(None, "mp", "dp"),
        P("mp", "dp"),
        P(None, "dp"),
        P(None, "dp"),
    )
    rows = P("dp", None, None)
    return jax.shard_map(
        per_device,
        mesh=mesh,
        in_specs=(rows, P("dp", None), P("dp"), rows) + weights * 3,
        out_specs=(rows, rows) + weights * 3,
        check_vma=False,
    )
```

```python
import functools

import jax
import jax.numpy as jnp
from jax import lax
from jax.experimental import pallas as pl
from jax.experimental.pallas import tpu as pltpu
from jax.sharding import PartitionSpec as P

D = 512
HEADS = 8
HEAD_DIM = 64
FF = 2048
LEN = 1024
STEP = 10
PAIR = 128
TILE = 256
KEYS = 128
TOKENS_AT_ONCE = 512
FAR = 1e30
EXTRA = 16
LOGS = 2 * LEN // PAIR

beta_one = 0.9
beta_two = 0.999
BF = jnp.bfloat16
F32 = jnp.float32
NN = (((1,), (0,)), ((), ()))
NT = (((1,), (1,)), ((), ()))


def dot(a, b, dims=NN):
    return lax.dot_general(a, b, dims, preferred_element_type=F32)


def vmem(mib):
    return pltpu.CompilerParams(
        dimension_semantics=("arbitrary",), vmem_limit_bytes=mib * 1024 * 1024
    )


def kernel_call(kernel, ids, inputs, in_specs, after, into, scratch, **kw):
    n, m, c = len(inputs), len(after), len(into)
    grid, out_specs, mib, flops = kw.pop("grid"), kw.pop("out_specs"), kw.pop("mib"), kw.pop("flops", 20_000_000_000)

    def body(ids_ref, *refs):
        given, rest = refs[:n], refs[n + m + c :]
        kernel(ids_ref, *given, *rest)

    anywhere = pl.BlockSpec(memory_space=pl.ANY)
    return pl.pallas_call(
        body,
        grid_spec=pltpu.PrefetchScalarGridSpec(
            num_scalar_prefetch=1,
            grid=grid,
            in_specs=list(in_specs) + [anywhere] * (m + c),
            out_specs=list(out_specs),
            scratch_shapes=scratch,
        ),
        input_output_aliases={1 + n + m + i: k for i, (_, k) in enumerate(into)},
        compiler_params=vmem(mib),
        cost_estimate=pl.CostEstimate(flops=flops, bytes_accessed=1_000_000, transcendentals=0),
        **kw,
    )(ids, *inputs, *after, *(a for a, _ in into))


def gate(values, *until):
    n = len(values)
    anywhere = pl.BlockSpec(memory_space=pl.ANY)
    return list(pl.pallas_call(
        lambda *refs: None,
        in_specs=[anywhere] * (n + len(until)),
        out_specs=[anywhere] * n,
        out_shape=[jax.ShapeDtypeStruct(a.shape, a.dtype) for a in values],
        input_output_aliases={k: k for k in range(n)},
        cost_estimate=pl.CostEstimate(flops=0, bytes_accessed=0, transcendentals=0),
        name="gate",
    )(*values, *until))


def flip(value, axis, bit):
    size = lax.axis_size(axis)
    return lax.ppermute(value, axis, [(i, i ^ bit) for i in range(size)])


def bits(size):
    out, bit = [], 1
    while bit < size:
        out.append(bit)
        bit *= 2
    return out


def combos(steps):
    return [sum(bit for k, bit in enumerate(steps) if (j >> k) & 1) for j in range(1, 2 ** len(steps))]


def routes(n_dp):
    near, *far = bits(n_dp)
    return near, [far[k : k + 2] for k in range(0, len(far), 2)]


def dp_order(n_dp):
    near, groups = routes(n_dp)
    order = [0]
    for group in groups:
        order = order + [x ^ y for y in combos(group) for x in order]
    return order + [x ^ near for x in order]


def gather_mp(part):
    return jnp.stack([part] + [flip(part, "mp", j) for j in range(1, lax.axis_size("mp"))])


def gather_mp_steps(part):
    n_mp = lax.axis_size("mp")
    held = {0: part}
    for bit in bits(n_mp)[::-1]:
        came = flip(jnp.stack([held[j] for j in sorted(held)]), "mp", bit)
        held.update({j ^ bit: came[k] for k, j in enumerate(sorted(held))})
    return jnp.stack([held[j] for j in range(n_mp)])


def gather_far(column):
    held = [column]
    for group in routes(lax.axis_size("dp"))[1]:
        held = held + [flip(a, "dp", y) for y in combos(group) for a in held]
    return held


def add_up(*terms):
    total = terms[0].astype(F32)
    for term in terms[1:]:
        total = total + term.astype(F32)
    return total


def scatter_start(held):
    groups = routes(lax.axis_size("dp"))[1]
    size = len(held) // 2 ** len(groups[-1])
    sent = [(held[(k + 1) * size + i], y) for k, y in enumerate(combos(groups[-1])) for i in range(size)]
    return held[:size], sent


def scatter_end(kept, came):
    held = [add_up(kept[i], *came[i :: len(kept)]).astype(BF) for i in range(len(kept))]
    for group in routes(lax.axis_size("dp"))[1][-2::-1]:
        size = len(held) // 2 ** len(group)
        came = [[flip(held[(k + 1) * size + i], "dp", y) for i in range(size)] for k, y in enumerate(combos(group))]
        held = [add_up(held[i], *(row[i] for row in came)).astype(BF) for i in range(size)]
    return held[0]


def rows_at(order, j, my_dp, span):
    return pl.ds(pl.multiple_of((order[j] ^ my_dp) * span, span), span)


def head_mask(shape, head):
    lane = lax.broadcasted_iota(jnp.int32, shape, 1)
    return (lane < HEAD_DIM) if head == 0 else (lane >= HEAD_DIM)


SPANS = (2, 3, 4, 5, 6, 7, 8)


def by_span(ids, t, with_keys):
    low, number = ids[3 + t], ids[3 + LEN // TILE + t]
    for k, span in enumerate(SPANS):
        fits = number <= span
        if k:
            fits = fits & (number > SPANS[k - 1])

        @pl.when(fits)
        def _(span=span):
            start = jnp.minimum(low, LEN // KEYS - span) * KEYS
            with_keys(pl.multiple_of(start, KEYS), span * KEYS)


def reach(segment_row):
    heads_at, ends_at = segment_row[::TILE], segment_row[TILE - 1 :: TILE]
    low = jnp.sum((segment_row[None] < heads_at[:, None]).astype(jnp.int32), axis=1) // KEYS
    high = (jnp.sum((segment_row[None] <= ends_at[:, None]).astype(jnp.int32), axis=1) + KEYS - 1) // KEYS
    return low, high - low


def lay_out(order, my_dp, w_refs, w_all):
    span, half = D // len(order), len(order) // 2
    for j in range(len(order)):
        piece = w_refs[j][0, :span] if j < half else w_refs[half][j - half, 0, :span]
        w_all[rows_at(order, j, my_dp, span), :] = piece


def column_specs(w_parts, base):
    *ones, stacked = w_parts
    block = (1, *ones[0].shape[1:])
    return [pl.BlockSpec(block, lambda g, ids: (g + base, 0, 0))] * len(ones) + [
        pl.BlockSpec((stacked.shape[0], *block), lambda g, ids: (0, g + base, 0, 0))
    ]


def attend_kernel(order, ids, x_ref, *refs):
    n_w = len(order) // 2 + 1
    bias_ref, qf_ref, kf_ref, q_ref, k_ref, v_ref, ho_ref, lse_ref, w_all, keys, vals, rows = refs[n_w:]
    lay_out(order, ids[2], refs[:n_w], w_all)

    @pl.when(pl.program_id(0) == 0)
    def _():
        keys[:, PAIR:] = kf_ref[0]

    for t in range(LEN // TILE):
        at = slice(t * TILE, (t + 1) * TILE)
        got = dot(x_ref[0, at], w_all[...])
        q_ref[0, at] = (got[:, :PAIR] + bias_ref[0, 0:1]).astype(BF)
        key = got[:, PAIR : 2 * PAIR].astype(BF)
        k_ref[0, at] = key
        keys[at, :PAIR] = key
        val = (got[:, 2 * PAIR :] + bias_ref[0, 1:2]).astype(BF)
        v_ref[0, at] = val
        for head in range(2):
            vals[head, at, :] = jnp.where(head_mask((TILE, PAIR), head), val, BF(1))

    def one_tile(t, carry):
        at = pl.ds(pl.multiple_of(t * TILE, TILE), TILE)
        query = q_ref[0, at] * BF(0.125)

        def with_keys(start, count):
            near = pl.ds(start, count)
            low_lane = head_mask((TILE, PAIR), 0)
            wide0 = jnp.concatenate([jnp.where(head_mask((TILE, PAIR), 0), query, BF(0)), qf_ref[0, at]], axis=1)
            scores0 = dot(wide0, keys[near, :], NT)
            wide1 = jnp.concatenate([jnp.where(head_mask((TILE, PAIR), 1), query, BF(0)), qf_ref[0, at]], axis=1)
            scores1 = dot(wide1, keys[near, :], NT)
            top0 = jnp.max(scores0, axis=1, keepdims=True)
            probs0 = jnp.exp(scores0 - top0).astype(BF)
            top1 = jnp.max(scores1, axis=1, keepdims=True)
            probs1 = jnp.exp(scores1 - top1).astype(BF)
            out0 = dot(probs0, vals[0, near, :])
            out1 = dot(probs1, vals[1, near, :])
            total = pltpu.roll(jnp.where(low_lane, out1, out0), HEAD_DIM, 1)
            ho_ref[0, at] = (jnp.where(low_lane, out0, out1) / total).astype(BF)
            both = (jnp.where(low_lane, top0, top1) + jnp.log(total)).T
            lse_ref[0, 0:1, at] = both[0:1]
            lse_ref[0, 1:2, at] = both[HEAD_DIM : HEAD_DIM + 1]

        by_span(ids, t, with_keys)
        return carry

    lax.fori_loop(0, LEN // TILE, one_tile, 0)
    for head in range(2):
        for c in range(LEN // PAIR):
            at = head * (LEN // PAIR) + c
            rows[at : at + 1] = lse_ref[0, head : head + 1, c * PAIR : (c + 1) * PAIR]
    rest = rows[...]
    for k in range(3):
        part = rest.astype(BF)
        ho_ref[0, LEN + k * LOGS : LEN + (k + 1) * LOGS] = part
        rest = rest - part.astype(F32)


def sent_logs(ho_ref, logs):
    part = lambda k: ho_ref[0, LEN + k * LOGS : LEN + (k + 1) * LOGS].astype(F32)
    rows = part(0) + part(1) + part(2)
    for head in range(2):
        for c in range(LEN // PAIR):
            at = head * (LEN // PAIR) + c
            logs[2 + head : 3 + head, c * PAIR : (c + 1) * PAIR] = rows[at : at + 1]


def attend(ids, tokens, w_parts, bias, qf, kf, order, part=(0, 1), after=(), into=()):
    groups, tall, _ = w_parts[0].shape
    count = groups // part[1]
    base = part[0] * count
    pair = pl.BlockSpec((1, LEN, PAIR), lambda g, ids: (g, 0, 0))
    feats = pl.BlockSpec((1, LEN, PAIR), lambda g, ids: (ids[0], 0, 0))
    return kernel_call(
        functools.partial(attend_kernel, order),
        ids,
        (tokens, *w_parts, bias, qf, kf),
        [pl.BlockSpec((1, LEN, D), lambda g, ids: (ids[0], 0, 0))]
        + column_specs(w_parts, base)
        + [pl.BlockSpec((1, 2, PAIR), lambda g, ids: (g + base, 0, 0)), feats, feats],
        after,
        into,
        [
            pltpu.VMEM((D, 3 * PAIR), BF),
            pltpu.VMEM((LEN, 2 * PAIR), BF),
            pltpu.VMEM((2, LEN, PAIR), BF),
            pltpu.VMEM((LOGS, PAIR), F32),
        ],
        grid=(count,),
        out_specs=[
            pair,
            pair,
            pair,
            pl.BlockSpec((1, LEN + 3 * LOGS, PAIR), lambda g, ids: (g, 0, 0)),
            pl.BlockSpec((1, 2, LEN), lambda g, ids: (g, 0, 0)),
        ],
        out_shape=[jax.ShapeDtypeStruct((count, LEN, PAIR), BF)] * 3
        + [jax.ShapeDtypeStruct((count, LEN + 3 * LOGS, PAIR), BF), jax.ShapeDtypeStruct((count, 2, LEN), F32)],
        mib=63,
        name="attend",
    )


def norm_stats(value):
    center = value - jnp.mean(value, axis=-1, keepdims=True)
    spread = jnp.mean(center * center, axis=-1, keepdims=True)
    inverse = lax.rsqrt(spread + 1e-05)
    return center * inverse, inverse


def norm_backward(upstream, normal, inverse, gain):
    scaled = upstream * gain
    return inverse * (
        scaled
        - jnp.mean(scaled, axis=-1, keepdims=True)
        - normal * jnp.mean(scaled * normal, axis=-1, keepdims=True)
    )


CHUNK = 1024


def unpack(order, my_dp, w_refs, w_out, w_up, w_down):
    groups, span, _ = w_refs[0].shape
    wide = FF // groups
    for j in range(len(order)):
        row = rows_at(order, j, my_dp, span)
        for g in range(groups):
            w_out[row, g * PAIR : (g + 1) * PAIR] = w_refs[j][g, :, :PAIR]
            w_up[row, g * wide : (g + 1) * wide] = w_refs[j][g, :, PAIR : PAIR + wide]
            w_down[row, g * wide : (g + 1) * wide] = w_refs[j][g, :, PAIR + wide :]


def up_half(x_ref, heads, cot_ref, par_ref, ffb_ref, w_out, w_up, w_down, keep_hidden, slope_ref):
    gain_one, gain_two = par_ref[0:1], par_ref[1:2]
    shift_att, shift_ffn, shift_one, shift_two = (par_ref[k : k + 1] for k in range(2, 6))
    attention = dot(heads, w_out[...], NT) + shift_att
    normal_one, inverse_one = norm_stats(x_ref[0].astype(F32) + attention)
    normed = normal_one * gain_one + shift_one
    normed_low = normed.astype(BF)
    branch = shift_ffn
    for c in range(FF // CHUNK):
        at = slice(c * CHUNK, (c + 1) * CHUNK)
        pre = dot(normed_low, w_up[:, at]) + ffb_ref[:, at]
        phi = 0.5 * (1.0 + lax.erf(pre * 0.7071067811865476))
        hidden = (pre * phi).astype(BF)
        if keep_hidden is not None:
            keep_hidden(at, hidden)
        slope_ref[:, at] = phi + pre * jnp.exp(-0.5 * pre * pre) * 0.3989422804014327
        branch = branch + dot(hidden, w_down[:, at], NT)
    normal_two, inverse_two = norm_stats(normed + branch)
    final_low = (normal_two * gain_two + shift_two).astype(BF)
    upstream = cot_ref[0].astype(F32)
    g_final = norm_backward(upstream, normal_two, inverse_two, gain_two)
    return normal_one, inverse_one, normed_low, normal_two, final_low, upstream, g_final


def down_half(g_final, normal_one, inverse_one, par_ref, w_out, w_up, w_down, slope_ref, keep_pre):
    g_final_low = g_final.astype(BF)
    g_normed = g_final
    for c in range(FF // CHUNK):
        at = slice(c * CHUNK, (c + 1) * CHUNK)
        g_pre = (dot(g_final_low, w_down[:, at]) * slope_ref[:, at]).astype(BF)
        if keep_pre is not None:
            keep_pre(at, g_pre)
        g_normed = g_normed + dot(g_pre, w_up[:, at], NT)
    g_attention = norm_backward(g_normed, normal_one, inverse_one, par_ref[0:1])
    g_attention_low = g_attention.astype(BF)
    g_heads = dot(g_attention_low, w_out[...]).astype(BF)
    return g_final_low, g_normed, g_attention, g_attention_low, g_heads


def fold(acc, k, term, first):
    part = jnp.sum(term.reshape(TOKENS_AT_ONCE // 8, 8, D), axis=0)

    @pl.when(first)
    def _():
        acc[k] = part

    @pl.when(jnp.logical_not(first))
    def _():
        acc[k] += part


def is_middle(ids):
    return (ids[1] == 1) | (ids[1] == 2)


def heads_of(ids, ho_refs):
    there = [k ^ ids[0] ^ ids[1] for k in range(ho_refs[0].shape[0])]
    if len(ho_refs) == 1:
        return jnp.concatenate([ho_refs[0][k] for k in there], axis=1)
    return jnp.concatenate([jnp.where(is_middle(ids), ho_refs[1][k], ho_refs[0][k]) for k in there], axis=1)


def forward_kernel(order, ids, x_ref, ho_ref, *refs):
    half = len(order) // 2
    w_refs, refs = [*refs[:half], *(refs[half].at[j] for j in range(half))], refs[half + 1 :]
    par_ref, ffb_ref, out_ref, w_out, w_up, w_down = refs

    @pl.when(pl.program_id(0) == 0)
    def _():
        unpack(order, ids[2], w_refs, w_out, w_up, w_down)

    shift_att, shift_ffn, shift_one, shift_two = (par_ref[k : k + 1] for k in range(2, 6))
    attention = dot(heads_of(ids, [ho_ref]), w_out[...], NT) + shift_att
    normed = norm_stats(x_ref[0].astype(F32) + attention)[0] * par_ref[0:1] + shift_one
    normed_low = normed.astype(BF)
    branch = shift_ffn
    for c in range(FF // CHUNK):
        at = slice(c * CHUNK, (c + 1) * CHUNK)
        pre = dot(normed_low, w_up[:, at]) + ffb_ref[:, at]
        hidden = (pre * (0.5 * (1.0 + lax.erf(pre * 0.7071067811865476)))).astype(BF)
        branch = branch + dot(hidden, w_down[:, at], NT)
    out_ref[...] = (norm_stats(normed + branch)[0] * par_ref[1:2] + shift_two).astype(BF)


def forward_only(ids, tokens, heads_out, w_parts, params, ff_shift, order, after=(), into=()):
    full = lambda shape: pl.BlockSpec(shape, lambda t, ids: (0,) * len(shape))
    return kernel_call(
        functools.partial(forward_kernel, order),
        ids,
        (tokens, heads_out, *w_parts, params, ff_shift),
        [
            pl.BlockSpec((1, TOKENS_AT_ONCE, D), lambda t, ids: (ids[0], t, 0)),
            pl.BlockSpec((heads_out.shape[0], TOKENS_AT_ONCE, PAIR), lambda t, ids: (0, t, 0)),
        ]
        + [full(a.shape) for a in w_parts]
        + [full((6, D)), full((1, FF))],
        after,
        into,
        [pltpu.VMEM((D, D), BF), pltpu.VMEM((D, FF), BF), pltpu.VMEM((D, FF), BF)],
        grid=(LEN // TOKENS_AT_ONCE,),
        out_specs=[pl.BlockSpec((TOKENS_AT_ONCE, D), lambda t, ids: (t, 0))],
        out_shape=[jax.ShapeDtypeStruct((LEN, D), BF)],
        mib=63,
        name="forward_only",
    )[0]


def tokenwise_kernel(order, n_ho, keep, ids, x_ref, cot_ref, *refs):
    ho_refs, refs = refs[:n_ho], refs[n_ho:]
    half = len(order) // 2
    w_refs, refs = [*refs[:half], *(refs[half].at[j] for j in range(half))], refs[half + 1 :]
    par_ref, ffb_ref, full_ref, gatt_ref, gh_ref, *refs = refs
    if keep:
        near_ref, far_ref, sums_ref, ff_ref, w_out, w_up, w_down, slope, *refs = refs
        acc, ffs_ref, hid_all, pre_all, ho_all, up_t, down_t, att_t, gw_all = refs
    else:
        w_out, w_up, w_down, slope = refs
    step = pl.program_id(0)
    tiles = LEN // TOKENS_AT_ONCE
    groups = gh_ref.shape[0]
    my_dp = ids[2]

    @pl.when(step == 0)
    def _():
        unpack(order, my_dp, w_refs, w_out, w_up, w_down)

    def tokens_step():
        rows = pl.ds(pl.multiple_of(jnp.minimum(step, tiles - 1) * TOKENS_AT_ONCE, TOKENS_AT_ONCE), TOKENS_AT_ONCE)
        heads = heads_of(ids, ho_refs)
        keep_hidden = keep_pre = None
        if keep:

            def keep_hidden(at, hidden):
                hid_all[rows, at] = hidden

            def keep_pre(at, g_pre):
                pre_all[rows, at] = g_pre
                here = jnp.sum(g_pre.astype(F32), axis=0, keepdims=True)

                @pl.when(step == 0)
                def _():
                    ffs_ref[:, at] = here

                @pl.when(step > 0)
                def _():
                    ffs_ref[:, at] += here

        normal_one, inverse_one, normed_low, normal_two, final_low, upstream, g_final = up_half(
            x_ref, heads, cot_ref, par_ref, ffb_ref, w_out, w_up, w_down, keep_hidden, slope
        )
        full_ref[0] = final_low
        g_final_low, g_normed, g_attention, g_attention_low, g_heads = down_half(
            g_final, normal_one, inverse_one, par_ref, w_out, w_up, w_down, slope, keep_pre
        )
        gatt_ref[...] = g_attention
        for g in range(groups):
            gh_ref[g] = g_heads[:, g * PAIR : (g + 1) * PAIR]
        if keep:
            ho_all[rows, :] = heads
            down_t[:, rows] = g_final_low.T
            att_t[:, rows] = g_attention_low.T
            up_t[:, rows] = normed_low.T
            terms = (g_normed * normal_one, upstream * normal_two, g_attention, g_final, g_normed, upstream)
            for k, term in enumerate(terms):
                fold(acc, k, term, step == 0)

            @pl.when(step == tiles - 1)
            def _():
                for k in range(6):
                    total = jnp.sum(acc[k], axis=0, keepdims=True)
                    for c in range(D // PAIR):
                        at = k * (D // PAIR) + c
                        sums_ref[at : at + 1] = total[:, c * PAIR : (c + 1) * PAIR]
                per_group = FF // groups // PAIR
                for c in range(FF // PAIR):
                    ff_ref[c // per_group, c % per_group : c % per_group + 1] = ffs_ref[:, c * PAIR : (c + 1) * PAIR]

    if not keep:
        tokens_step()
        return

    pl.when(step < tiles)(tokens_step)

    @pl.when(step >= tiles)
    def _():
        half, _, span, _ = near_ref.shape
        wide = FF // groups
        block = pl.ds(pl.multiple_of((step - tiles) * wide, wide), wide)
        pair = pl.ds(pl.multiple_of((step - tiles) * PAIR, PAIR), PAIR)
        gw_all[:, :PAIR] = dot(att_t[...], ho_all[:, pair]).astype(BF)
        gw_all[:, PAIR : PAIR + wide] = dot(up_t[...], pre_all[:, block]).astype(BF)
        gw_all[:, PAIR + wide :] = dot(down_t[...], hid_all[:, block]).astype(BF)
        for j in range(half):
            near_ref[j, 0] = gw_all[rows_at(order, j, my_dp, span), :]
            far_ref[j, 0] = gw_all[rows_at(order, half + j, my_dp, span), :]


def tokenwise(ids, tokens, heads_out, cotangent, w_parts, params, ff_shift, order, keep, after=(), into=()):
    tiles = LEN // TOKENS_AT_ONCE
    groups, span, cols = w_parts[0].shape
    early = lambda t: jnp.minimum(t, tiles - 1)
    late = lambda t: jnp.maximum(t - tiles, 0)
    full = lambda shape: pl.BlockSpec(shape, lambda t, ids: (0,) * len(shape))
    row = pl.BlockSpec((1, TOKENS_AT_ONCE, D), lambda t, ids: (ids[0], early(t), 0))
    flat = pl.BlockSpec((TOKENS_AT_ONCE, D), lambda t, ids: (early(t), 0))
    pairs = lambda n: pl.BlockSpec((n, TOKENS_AT_ONCE, PAIR), lambda t, ids: (0, early(t), 0))
    out_specs = [row, flat, pairs(groups)]
    out_shape = [
        jax.ShapeDtypeStruct(tokens.shape, BF),
        jax.ShapeDtypeStruct((LEN, D), F32),
        jax.ShapeDtypeStruct((groups, LEN, PAIR), BF),
    ]
    scratch = [
        pltpu.VMEM((D, D), BF),
        pltpu.VMEM((D, FF), BF),
        pltpu.VMEM((D, FF), BF),
        pltpu.VMEM((TOKENS_AT_ONCE, FF), F32),
    ]
    if keep:
        half = len(order) // 2
        part = pl.BlockSpec((half, 1, span, cols), lambda t, ids: (0, late(t), 0, 0))
        norm_sums, ff_sums = (6 * D // PAIR, PAIR), (groups, FF // groups // PAIR, PAIR)
        out_specs += [part, part, full(norm_sums), full(ff_sums)]
        out_shape += [jax.ShapeDtypeStruct((half, groups, span, cols), BF)] * 2
        out_shape += [jax.ShapeDtypeStruct(norm_sums, F32), jax.ShapeDtypeStruct(ff_sums, F32)]
        scratch += [
            pltpu.VMEM((6, 8, D), F32),
            pltpu.VMEM((1, FF), F32),
            pltpu.VMEM((LEN, FF), BF),
            pltpu.VMEM((LEN, FF), BF),
            pltpu.VMEM((LEN, D), BF),
            pltpu.VMEM((D, LEN), BF),
            pltpu.VMEM((D, LEN), BF),
            pltpu.VMEM((D, LEN), BF),
            pltpu.VMEM((D, cols), BF),
        ]
    return kernel_call(
        functools.partial(tokenwise_kernel, order, len(heads_out), keep),
        ids,
        (tokens, cotangent, *heads_out, *w_parts, params, ff_shift),
        [row, row]
        + [pairs(a.shape[0]) for a in heads_out]
        + [full(a.shape) for a in w_parts]
        + [full((6, D)), full((1, FF))],
        after,
        into,
        scratch,
        grid=(tiles + groups if keep else tiles,),
        out_specs=out_specs,
        out_shape=out_shape,
        mib=63,
        name="tokenwise_keep" if keep else "tokenwise",
    )


def attend_back_kernel(order, keep, whole_row, ids, x_ref, *refs):
    n_w = len(order) // 2 + 1
    w_refs, (qf_ref, kf_ref, *refs) = refs[:n_w], refs[n_w:]
    if keep:
        q_ref, k_ref, v_ref, ho_ref, lse_ref, sums_ref, ff_ref, gh_ref, gatt_ref, *refs = refs
        tg_ref, send_ref, again_ref, near_ref, far_ref, *refs = refs
        w_all, keys, keys_t, delta, dk, dv, grads, x_t, gw_all, extra = refs
    else:
        bias_ref, ho_ref, ho_mid, gh_ref, gatt_ref, tg_ref, *refs = refs
        w_all, keys, keys_t, delta, dk, dv, grads, q_ref, k_ref, v_ref = refs
    my_dp = ids[2]
    if whole_row:
        tg_ref = tg_ref.at[0]
    lay_out(order, my_dp, w_refs, w_all)

    @pl.when(pl.program_id(0) == 0)
    def _():
        keys[:, PAIR:] = kf_ref[0]
        tg_ref[...] = gatt_ref[...]
        if keep:
            x_t[...] = x_ref[0].T
            extra[...] = jnp.zeros_like(extra)
            extra[:12, :PAIR] = sums_ref[:12]
            extra[:12, PAIR : 2 * PAIR] = sums_ref[12:]

    if keep:
        heads = ho_ref[0, :LEN]
        delta[2:4] = lse_ref[0]
    else:
        for t in range(LEN // TILE):
            at = slice(t * TILE, (t + 1) * TILE)
            got = dot(x_ref[0, at], w_all[...])
            q_ref[0, at] = (got[:, :PAIR] + bias_ref[0, 0:1]).astype(BF)
            k_ref[0, at] = got[:, PAIR : 2 * PAIR].astype(BF)
            v_ref[0, at] = (got[:, 2 * PAIR :] + bias_ref[0, 1:2]).astype(BF)
        heads = jnp.where(is_middle(ids), ho_mid[0, :LEN], ho_ref[0, :LEN])

        @pl.when(is_middle(ids))
        def _():
            sent_logs(ho_mid, delta)

        @pl.when(jnp.logical_not(is_middle(ids)))
        def _():
            sent_logs(ho_ref, delta)

    keys[:, :PAIR] = k_ref[0]
    keys_t[...] = k_ref[0].T
    prod = (gh_ref[0].astype(F32) * heads.astype(F32)).T
    delta[0:1] = jnp.sum(prod[:HEAD_DIM], axis=0, keepdims=True)
    delta[1:2] = jnp.sum(prod[HEAD_DIM:], axis=0, keepdims=True)
    dk[...] = jnp.zeros_like(dk)
    dv[...] = jnp.zeros_like(dv)

    def one_tile(t, carry):
        at = pl.ds(pl.multiple_of(t * TILE, TILE), TILE)
        query, back = q_ref[0, at], gh_ref[0, at]

        def with_keys(start, count):
            near = pl.ds(start, count)
            mine0 = jnp.where(head_mask((TILE, PAIR), 0), query, BF(0))
            back0 = jnp.where(head_mask((TILE, PAIR), 0), back, BF(0))
            wide0 = jnp.concatenate([mine0 * BF(0.125), qf_ref[0, at]], axis=1)
            scores0 = dot(keys[near, :], wide0, NT)
            g_probs0 = dot(v_ref[0, near], back0, NT)
            mine1 = jnp.where(head_mask((TILE, PAIR), 1), query, BF(0))
            back1 = jnp.where(head_mask((TILE, PAIR), 1), back, BF(0))
            wide1 = jnp.concatenate([mine1 * BF(0.125), qf_ref[0, at]], axis=1)
            scores1 = dot(keys[near, :], wide1, NT)
            g_probs1 = dot(v_ref[0, near], back1, NT)
            probs0 = jnp.exp(scores0 - delta[2:3, at])
            g_raw0 = (probs0 * (g_probs0 - delta[0 : 0 + 1, at])).astype(BF)
            low0 = probs0.astype(BF)
            probs1 = jnp.exp(scores1 - delta[3:4, at])
            g_raw1 = (probs1 * (g_probs1 - delta[1 : 1 + 1, at])).astype(BF)
            low1 = probs1.astype(BF)
            d_query0 = dot(keys_t[0 * HEAD_DIM : (0 + 1) * HEAD_DIM, near], g_raw0)
            d_query1 = dot(keys_t[1 * HEAD_DIM : (1 + 1) * HEAD_DIM, near], g_raw1)
            dv[near, :] += dot(jnp.concatenate([low0, low1], axis=1), jnp.concatenate([back0, back1], axis=0))
            dk[near, :] += dot(jnp.concatenate([g_raw0, g_raw1], axis=1), jnp.concatenate([mine0, mine1], axis=0))
            d_query = [d_query0, d_query1]
            grads[at, :PAIR] = (jnp.concatenate(d_query, axis=0).T * 0.125).astype(BF)

        by_span(ids, t, with_keys)
        return carry

    lax.fori_loop(0, LEN // TILE, one_tile, 0)
    grads[:, PAIR : 2 * PAIR] = (dk[...] * 0.125).astype(BF)
    grads[:, 2 * PAIR :] = dv[...].astype(BF)
    for t in range(LEN // TILE):
        at = slice(t * TILE, (t + 1) * TILE)
        tg_ref[at, :] += dot(grads[at, :], w_all[...], NT)
    if keep:
        half, span = len(order) // 2, D // len(order)
        gw_all[...] = dot(x_t[...], grads[...]).astype(BF)
        extra[0:1, 2 * PAIR :] = jnp.sum(grads[:, :PAIR].astype(F32), axis=0, keepdims=True)
        extra[1:2, 2 * PAIR :] = jnp.sum(grads[:, 2 * PAIR :].astype(F32), axis=0, keepdims=True)
        extra[2 : 2 + ff_ref.shape[1], 2 * PAIR :] = ff_ref[0]
        vectors = extra[...].astype(BF)
        for j in range(half):
            near_ref[j, 0, :span] = gw_all[rows_at(order, j, my_dp, span), :]
            near_ref[j, 0, span:] = vectors
            far_ref[j, 0, :span] = gw_all[rows_at(order, half + j, my_dp, span), :]
            far_ref[j, 0, span:] = vectors

        @pl.when(pl.program_id(0) == pl.num_programs(0) - 1)
        def _():
            send = tg_ref[...].astype(BF)
            send_ref[...] = send
            again_ref[...] = send


def attend_back(ids, tokens, w_parts, qf, kf, saved, g_heads, g_att, order, keep, part=(0, 1), after=(), into=()):
    groups, tall, _ = w_parts[0].shape
    half = len(order) // 2
    count = groups // part[1]
    base = part[0] * count
    whole_row = part[0] == part[1] - 1
    there = lambda g, ids: (g + base) ^ ids[0] ^ ids[1]
    pair = pl.BlockSpec((1, LEN, PAIR), lambda g, ids: (there(g, ids), 0, 0))
    pair_logs = pl.BlockSpec((1, LEN + 3 * LOGS, PAIR), lambda g, ids: (there(g, ids), 0, 0))
    feats = pl.BlockSpec((1, LEN, PAIR), lambda g, ids: (ids[0], 0, 0))
    full = pl.BlockSpec((LEN, D), lambda g, ids: (0, 0))
    out_specs = [pl.BlockSpec((1, LEN, D), lambda g, ids: (ids[0], 0, 0)) if whole_row else full]
    out_shape = [jax.ShapeDtypeStruct(tokens.shape if whole_row else (LEN, D), F32)]
    scratch = [
        pltpu.VMEM((D, 3 * PAIR), BF),
        pltpu.VMEM((LEN, 2 * PAIR), BF),
        pltpu.VMEM((PAIR, LEN), BF),
        pltpu.VMEM((4, LEN), F32),
        pltpu.VMEM((LEN, PAIR), F32),
        pltpu.VMEM((LEN, PAIR), F32),
        pltpu.VMEM((LEN, 3 * PAIR), BF),
    ]
    if keep:
        saved_specs = [
            pair,
            pair,
            pair,
            pair_logs,
            pl.BlockSpec((1, 2, LEN), lambda g, ids: (g, 0, 0)),
            pl.BlockSpec(saved[5].shape, lambda g, ids: (0, 0)),
            pl.BlockSpec((1, *saved[6].shape[1:]), lambda g, ids: (g, 0, 0)),
        ]
        out_specs += [full, full] + [pl.BlockSpec((half, 1, tall, 3 * PAIR), lambda g, ids: (0, g, 0, 0))] * 2
        out_shape += [jax.ShapeDtypeStruct((LEN, D), BF)] * 2
        out_shape += [jax.ShapeDtypeStruct((half, groups, tall, 3 * PAIR), BF)] * 2
        scratch += [pltpu.VMEM((D, LEN), BF), pltpu.VMEM((D, 3 * PAIR), BF), pltpu.VMEM((EXTRA, 3 * PAIR), F32)]
    else:
        saved_specs = [pl.BlockSpec((1, 2, PAIR), lambda g, ids: (g + base, 0, 0)), pair_logs, pair_logs]
        scratch += [pltpu.VMEM((1, LEN, PAIR), BF)] * 3
    return kernel_call(
        functools.partial(attend_back_kernel, order, keep, whole_row),
        ids,
        (tokens, *w_parts, qf, kf, *saved, g_heads, g_att),
        [pl.BlockSpec((1, LEN, D), lambda g, ids: (ids[0], 0, 0))]
        + column_specs(w_parts, base)
        + [feats, feats]
        + saved_specs
        + [pl.BlockSpec((1, LEN, PAIR), lambda g, ids: (g + base, 0, 0)), full],
        after,
        into,
        scratch,
        grid=(count,),
        out_specs=out_specs,
        out_shape=out_shape,
        mib=63,
        flops=20_000_000_000,
        name="attend_back_keep" if keep else "attend_back",
    )


RATES = (D ** (-0.5), (D // 64) ** (-0.5), D ** (-0.5), FF ** (-0.5), 0.3, 0.3, 0.3, 0.3)
DECAYS = (0.01, 0.01, 0.01, 0.01, 0.0, 0.0, 0.0, 0.0)


def adam_step(weight, grad_sum, first, second, rate, decay):
    first_new = beta_one * first + (1.0 - beta_one) * grad_sum
    second_new = beta_two * second + (1.0 - beta_two) * grad_sum * grad_sum
    first_hat = first_new / (1.0 - beta_one**STEP)
    second_hat = second_new / (1.0 - beta_two**STEP)
    weight_new = weight - rate * (first_hat / (jnp.sqrt(second_hat) + 1e-08) + decay * weight)
    return (weight_new, first_new, second_new)


def adam_kernel(ids, *refs):
    terms, olds, news, whole, mine = refs[:4], refs[4:28], refs[28:52], refs[52], refs[53]
    span = olds[2].shape[0]
    wide, per = olds[2].shape[1], olds[5].shape[1]
    total_ab = lambda at: terms[0][:, at].astype(F32) + terms[1][:, at].astype(F32)
    total_qkv = lambda rows, at: terms[2][rows, at].astype(F32) + terms[3][rows, at].astype(F32)

    def step(slot, at, grad):
        old = [olds[8 * k + slot][at] for k in range(3)]
        new = adam_step(old[0], grad, old[1], old[2], RATES[slot], DECAYS[slot])
        for k in range(3):
            news[8 * k + slot][at] = new[k]

    for k in range(3):
        step(0, k, total_qkv(slice(0, span), slice(k * PAIR, (k + 1) * PAIR)))
    step(1, ..., total_ab(slice(0, PAIR)))
    step(2, ..., total_ab(slice(PAIR, PAIR + wide)))
    step(3, ..., total_ab(slice(PAIR + wide, PAIR + 2 * wide)))
    whole[...] = total_qkv(slice(span, span + EXTRA), slice(0, 3 * PAIR))
    first_norm = ids[2] * span
    turns = (first_norm, first_norm, ids[2] * per)
    for k in range(3):
        back = lax.rem(PAIR - lax.rem(turns[k], PAIR), PAIR)
        mine[k * EXTRA : (k + 1) * EXTRA] = pltpu.roll(whole[:, k * PAIR : (k + 1) * PAIR], back, 1)
    for k in range(6):
        at = (k // 3) * EXTRA + (k % 3) * (D // PAIR) + first_norm // PAIR
        slot, row = (6, k) if k < 2 else (7, k - 2)
        step(slot, slice(row, row + 1), mine[pl.ds(at, 1), :span])
    pieces = lambda row: [mine[2 * EXTRA + row : 2 * EXTRA + row + 1, h * HEAD_DIM : h * HEAD_DIM + per] for h in (0, 1)]
    for kind in range(2):
        for head, grad in enumerate(pieces(kind)):
            step(4, (kind, slice(head, head + 1)), grad)
    for row in range(olds[5].shape[0] // 2):
        for head, grad in enumerate(pieces(2 + row)):
            step(5, slice(2 * row + head, 2 * row + head + 1), grad)


def adam(ids, last, after, *sets):
    turn = lambda a: (a[0].transpose(1, 0, 2), a[1].T, a[2], a[3].T, *a[4:])
    olds = [array for group in sets for array in turn(group)]
    inputs = (*last[0], *last[1], *olds)
    full = lambda a: pl.BlockSpec(a.shape, lambda t, ids: (0,) * a.ndim)
    news = kernel_call(
        adam_kernel, ids, inputs, [full(a) for a in inputs], after, (),
        [pltpu.VMEM((EXTRA, 3 * PAIR), F32), pltpu.VMEM((3 * EXTRA, PAIR), F32)],
        grid=(1,),
        out_specs=[full(a) for a in olds],
        out_shape=[jax.ShapeDtypeStruct(a.shape, F32) for a in olds],
        mib=63,
        name="adam",
    )
    return [array for k in range(3) for array in turn(news[8 * k : 8 * k + 8])]


def rows_of(ids):
    z = ids[1]
    by = lambda a, b, c, d: jnp.where(z == 0, a, jnp.where(z == 1, b, jnp.where(z == 2, c, d)))
    return z, by(1, 2, 1, 2), by(2, 0, 3, 1), by(3, 3, 0, 0)


PLACED = 256


def place_kernel(ids, grad_straight, grad_middle, grad_end, out_straight, out_middle, out_end, _, __, tg_ref, lo_ref, sems, one, two, three, four):
    t, last = pl.program_id(0), pl.num_programs(0) - 1
    _, _, straight, through = rows_of(ids)
    slot = lax.rem(t, 2)
    inside = is_middle(ids)

    def copies(step, slot):
        ways = ((one, tg_ref, straight), (two, tg_ref, through), (three, lo_ref, straight), (four, lo_ref, through))
        return [
            pltpu.make_async_copy(buf.at[slot], ref.at[row, pl.ds(step * PLACED, PLACED)], sems.at[k, slot])
            for k, (buf, ref, row) in enumerate(ways)
        ]

    @pl.when(t >= 2)
    def _():
        for copy in copies(t - 2, slot):
            copy.wait()

    one[slot] = grad_straight[...].astype(F32)
    two[slot] = jnp.where(inside, grad_middle[...], grad_end[...]).astype(F32)
    three[slot] = out_straight[...]
    four[slot] = jnp.where(inside, out_middle[...], out_end[...])
    for copy in copies(t, slot):
        copy.start()

    @pl.when(t == last)
    def _():
        for copy in copies(t - 1, 1 - slot) + copies(t, slot):
            copy.wait()


def place(ids, grads, outs, tokens_grad, layer_out):
    block = pl.BlockSpec((PLACED, D), lambda t, ids: (t, 0))
    chosen = [
        pl.BlockSpec((PLACED, D), lambda t, ids: (jnp.where(is_middle(ids), t, 0), 0)),
        pl.BlockSpec((PLACED, D), lambda t, ids: (jnp.where(is_middle(ids), 0, t), 0)),
    ]
    anywhere = pl.BlockSpec(memory_space=pl.ANY)
    return pl.pallas_call(
        place_kernel,
        grid_spec=pltpu.PrefetchScalarGridSpec(
            num_scalar_prefetch=1,
            grid=(LEN // PLACED,),
            in_specs=[block, *chosen, block, *chosen] + [anywhere] * 2,
            out_specs=[anywhere, anywhere],
            scratch_shapes=[
                pltpu.SemaphoreType.DMA((4, 2)),
                pltpu.VMEM((2, PLACED, D), F32),
                pltpu.VMEM((2, PLACED, D), F32),
                pltpu.VMEM((2, PLACED, D), BF),
                pltpu.VMEM((2, PLACED, D), BF),
            ],
        ),
        out_shape=[jax.ShapeDtypeStruct(a.shape, a.dtype) for a in (tokens_grad, layer_out)],
        input_output_aliases={7: 0, 8: 1},
        compiler_params=vmem(63),
        name="place",
    )(ids, *grads, *outs, tokens_grad, layer_out)


def pack_kernel(qkv, out_t, up, down_t, qv, ff, gains, shifts, first_ref, second_ref):
    span, wide = up.shape
    for k in range(3):
        first_ref[:span, k * PAIR : (k + 1) * PAIR] = qkv[k].astype(BF)
    first_ref[span:, :] = jnp.zeros((EXTRA, 3 * PAIR), BF)
    first_ref[span : span + 2, :span] = gains[...].astype(BF)
    first_ref[span + 2 : span + 6, :span] = shifts[...].astype(BF)
    first_ref[span : span + ff.shape[0], PAIR : PAIR + ff.shape[1]] = ff[...].astype(BF)
    for k in range(2):
        first_ref[span + 2 * k : span + 2 * k + 2, 2 * PAIR : 2 * PAIR + qv.shape[2]] = qv[k].astype(BF)
    second_ref[:, :PAIR] = out_t[...].astype(BF)
    second_ref[:, PAIR : PAIR + wide] = up[...].astype(BF)
    second_ref[:, PAIR + wide :] = down_t[...].astype(BF)


def pack(w_qkv, w_out, w_up, w_down, qv_bias, ff_bias, norm_gains, norm_shifts):
    span, wide = w_up.shape
    return pl.pallas_call(
        pack_kernel,
        out_shape=[
            jax.ShapeDtypeStruct((span + EXTRA, 3 * PAIR), BF),
            jax.ShapeDtypeStruct((span, PAIR + 2 * wide), BF),
        ],
        name="pack",
    )(w_qkv.transpose(1, 0, 2), w_out.T, w_up, w_down.T, qv_bias, ff_bias, norm_gains, norm_shifts)


def features(segment_ids, pad_lengths):
    place = jnp.arange(LEN, dtype=jnp.int32)[None, :, None]
    lane = jnp.arange(PAIR, dtype=jnp.int32)[None, None, :]
    segment = segment_ids[:, :, None]
    padding = place >= (LEN - pad_lengths)[:, None, None]
    high, low = place // 32, place % 32
    hit = (
        ((lane < 4) & (lane == segment))
        | ((lane >= 4) & (lane < 36) & (lane - 4 == high))
        | ((lane >= 36) & (lane < 68) & (lane - 36 == low))
    )
    counts = jnp.where(padding, (lane >= 4) & (lane < 68), lane < 4)
    qf = jnp.where(hit, -FAR, 0.0).astype(BF)
    kf = jnp.where(counts & ~hit, 1.0, 0.0).astype(BF)
    return qf, kf


def per_device(
    tokens, segment_ids, pad_lengths, cotangent,
    w_qkv, w_out, w_up, w_down, qv_bias, ff_bias, norm_gains, norm_shifts,
    first_qkv, first_out, first_up, first_down, first_qv_bias, first_ff_bias, first_gains, first_shifts,
    second_qkv, second_out, second_up, second_down, second_qv_bias, second_ff_bias, second_gains, second_shifts,
):
    n_dp, n_mp = lax.axis_size("dp"), lax.axis_size("mp")
    my_dp, my_mp = lax.axis_index("dp"), lax.axis_index("mp")
    order = dp_order(n_dp)
    half = n_dp // 2
    span = D // n_dp
    wide, per = FF // n_mp, HEAD_DIM // n_dp
    ff_rows = wide // HEAD_DIM

    places = ((jnp.array(order, jnp.int32)[:, None] ^ my_dp) == jnp.arange(n_dp, dtype=jnp.int32)[None]).astype(BF)

    def to_near(value):
        return flip(value, "dp", routes(n_dp)[0])

    part_qkv, part_ab = pack(w_qkv, w_out, w_up, w_down, qv_bias, ff_bias, norm_gains, norm_shifts)
    far_qkv = gather_far(gather_mp(part_qkv))
    all_qkv = [*far_qkv, to_near(jnp.stack(far_qkv))]
    far_ab = gather_far(gather_mp_steps(part_ab))
    small_here = jnp.concatenate(
        [jnp.stack([a[:, span : span + 8] for a in all_qkv[:half]]), all_qkv[half][:, :, span : span + 8]]
    ).reshape(n_dp, -1)
    small_all = dot(places, small_here, (((0,), (0,)), ((), ()))).reshape(n_dp, n_mp, 8, 3 * PAIR)
    bias_rows = (
        small_all[:, :, :4, 2 * PAIR : 2 * PAIR + per].reshape(n_dp, n_mp, 2, 2, per).transpose(1, 2, 3, 0, 4)
    ).reshape(n_mp, 2, PAIR)
    ff_shift = small_all[:, :, :ff_rows, PAIR : PAIR + per].transpose(1, 2, 0, 3).reshape(1, FF)
    params = small_all[:, 0, :6, :span].transpose(1, 0, 2).reshape(6, D)
    qf, kf = features(segment_ids, pad_lengths)

    def ids_of(row):
        low, number = reach(lax.dynamic_index_in_dim(segment_ids, row, 0, keepdims=False))
        return jnp.concatenate([jnp.stack([row, my_mp, my_dp]).astype(jnp.int32), low, number])

    second = jnp.where((my_mp == 0) | (my_mp == 2), 1, 2)
    mine, other = ids_of(my_mp), ids_of(second)

    saved = attend(mine, tokens, all_qkv, bias_rows, qf, kf, order)
    far_ab = gate(far_ab, saved[4])
    all_ab = [*far_ab, to_near(jnp.stack(far_ab))]
    to_ends, to_middles = [(1, 0), (2, 3)], [(1, 2), (2, 1)]
    across, straight = [(0, 2), (3, 1)], [(0, 1), (3, 2), (1, 3), (2, 0)]
    heads_end, heads_mid = (lax.ppermute(saved[3], "mp", way) for way in (to_ends, to_middles))
    own_out = forward_only(mine, tokens, saved[3], all_ab, params, ff_shift, order)
    out_middle = lax.ppermute(own_out, "mp", across)
    layer_out, g_att, g_heads, near_ab, far_grad_ab, sums, ff_sums = tokenwise(
        mine, tokens, [saved[3]], cotangent, all_ab, params, ff_shift, order, True, after=(own_out,)
    )
    out_straight = lax.ppermute(own_out, "mp", straight)
    came_ab = to_near(far_grad_ab)
    tokens_grad, own_send, send_again, near_qkv, far_grad_qkv = attend_back(
        mine, tokens, all_qkv, qf, kf, (*saved, sums, ff_sums), g_heads, g_att, order, True,
        after=(heads_end, heads_mid, out_middle),
    )
    held_ab = [add_up(near_ab[j], came_ab[j]).astype(BF) for j in range(half)]
    own_send, out_middle, out_straight, far_grad_qkv = gate((own_send, out_middle, out_straight, far_grad_qkv))
    came_qkv = to_near(far_grad_qkv)
    grad_middle = lax.ppermute(own_send, "mp", across)
    out_end = lax.ppermute(out_middle, "mp", to_ends)
    kept_ab, sent_ab = scatter_start(held_ab)
    late = len(sent_ab) - len(kept_ab)
    far_sums_ab = [flip(value, "dp", y) for value, y in sent_ab[:late]]
    layer_out, g_att2, g_heads2 = tokenwise(
        other, tokens, [heads_end, heads_mid], cotangent, all_ab, params, ff_shift, order, False,
        after=(own_send,), into=((layer_out, 0),),
    )
    late_ab = [value for value, _ in sent_ab[late:]]
    n_late = len(late_ab)
    send_again, grad_middle, out_end, came_qkv, *moved = gate(
        (send_again, grad_middle, out_end, came_qkv, *late_ab, *far_sums_ab), g_heads2
    )
    late_ab, far_sums_ab = moved[:n_late], moved[n_late:]
    grad_straight = lax.ppermute(send_again, "mp", straight)
    grad_end = lax.ppermute(grad_middle, "mp", to_ends)
    late_ab = [flip(value, "dp", y) for value, (_, y) in zip(late_ab, sent_ab[late:])]
    far_bits = [bit for group in routes(n_dp)[1] for bit in group]
    kept_qkv = near_qkv.shape[0] // 2
    held_qkv = [add_up(near_qkv[k * kept_qkv : (k + 1) * kept_qkv], came_qkv[k * kept_qkv : (k + 1) * kept_qkv]).astype(BF) for k in range(2)]
    came_half = flip(held_qkv[1], "dp", far_bits[-1])
    of_other = (bias_rows, heads_end, heads_mid)
    (half_grad,) = attend_back(
        other, tokens, all_qkv, qf, kf, of_other, g_heads2, g_att2, order, False, (0, 2),
        after=(grad_middle, *held_qkv),
    )
    came_half, *late_ab = gate((came_half, *late_ab), half_grad)
    column_ab = scatter_end(kept_ab, [*far_sums_ab, *late_ab])
    column_qkv = add_up(held_qkv[0], came_half).astype(BF)
    for bit in far_bits[-2::-1]:
        kept_qkv = column_qkv.shape[0] // 2
        came_half = flip(column_qkv[kept_qkv:], "dp", bit)
        column_qkv = (column_qkv[:kept_qkv], came_half)
        if bit != far_bits[0]:
            column_qkv = add_up(*column_qkv).astype(BF)
    come_mp = lambda a: flip(jnp.stack([a[1], a[3]]), "mp", 1)
    keep_mp = lambda a, b: add_up(jnp.stack([a[0], a[2]]), b).astype(BF)
    came_mp_ab = come_mp(column_ab)
    (tokens_grad,) = attend_back(
        other, tokens, all_qkv, qf, kf, of_other, g_heads2, half_grad, order, False, (1, 2),
        after=(column_qkv[0],), into=((tokens_grad, 0),),
    )
    came_mp_ab, came_half = gate((came_mp_ab, column_qkv[1]), tokens_grad)
    column_qkv = add_up(column_qkv[0], came_half)[0].astype(BF)
    pair_ab, pair_qkv = keep_mp(column_ab, came_mp_ab), keep_mp(column_qkv, come_mp(column_qkv))
    last = [(a[0], flip(a[1], "mp", 2)) for a in (pair_ab, pair_qkv)]
    tokens_grad, layer_out = place(
        mine, (grad_straight, grad_middle, grad_end), (out_straight, out_middle, out_end), tokens_grad, layer_out
    )

    masters = (w_qkv, w_out, w_up, w_down, qv_bias, ff_bias, norm_gains, norm_shifts)
    firsts = (first_qkv, first_out, first_up, first_down, first_qv_bias, first_ff_bias, first_gains, first_shifts)
    seconds = (second_qkv, second_out, second_up, second_down, second_qv_bias, second_ff_bias, second_gains, second_shifts)
    updated = adam(mine, last, (tokens_grad,), masters, firsts, seconds)
    return (layer_out, tokens_grad, *updated)


def solution(mesh):
    weights = (
        P("dp", None, "mp"),
        P("mp", "dp"),
        P("dp", "mp"),
        P("mp", "dp"),
        P(None, "mp", "dp"),
        P("mp", "dp"),
        P(None, "dp"),
        P(None, "dp"),
    )
    rows = P("dp", None, None)
    return jax.shard_map(
        per_device,
        mesh=mesh,
        in_specs=(rows, P("dp", None), P("dp"), rows) + weights * 3,
        out_specs=(rows, rows) + weights * 3,
        check_vma=False,
    )
```

```python
import functools

import jax
import jax.numpy as jnp
from jax import lax
from jax.experimental import pallas as pl
from jax.experimental.pallas import tpu as pltpu
from jax.sharding import PartitionSpec as P

D = 512
HEADS = 8
HEAD_DIM = 64
FF = 2048
LEN = 1024
STEP = 10
PAIR = 128
TILE = 256
KEYS = 128
TOKENS_AT_ONCE = 512
FAR = 1e30
EXTRA = 16
LOGS = 2 * LEN // PAIR

beta_one = 0.9
beta_two = 0.999
BF = jnp.bfloat16
F32 = jnp.float32
NN = (((1,), (0,)), ((), ()))
NT = (((1,), (1,)), ((), ()))


def dot(a, b, dims=NN):
    return lax.dot_general(a, b, dims, preferred_element_type=F32)


def vmem(mib):
    return pltpu.CompilerParams(
        dimension_semantics=("arbitrary",), vmem_limit_bytes=mib * 1024 * 1024
    )


def kernel_call(kernel, ids, inputs, in_specs, after, into, scratch, **kw):
    n, m, c = len(inputs), len(after), len(into)
    grid, out_specs, mib, flops = kw.pop("grid"), kw.pop("out_specs"), kw.pop("mib"), kw.pop("flops", 20_000_000_000)

    def body(ids_ref, *refs):
        given, rest = refs[:n], refs[n + m + c :]
        kernel(ids_ref, *given, *rest)

    anywhere = pl.BlockSpec(memory_space=pl.ANY)
    return pl.pallas_call(
        body,
        grid_spec=pltpu.PrefetchScalarGridSpec(
            num_scalar_prefetch=1,
            grid=grid,
            in_specs=list(in_specs) + [anywhere] * (m + c),
            out_specs=list(out_specs),
            scratch_shapes=scratch,
        ),
        input_output_aliases={1 + n + m + i: k for i, (_, k) in enumerate(into)},
        compiler_params=vmem(mib),
        cost_estimate=pl.CostEstimate(flops=flops, bytes_accessed=1_000_000, transcendentals=0),
        **kw,
    )(ids, *inputs, *after, *(a for a, _ in into))


def gate(values, *until):
    n = len(values)
    anywhere = pl.BlockSpec(memory_space=pl.ANY)
    return list(pl.pallas_call(
        lambda *refs: None,
        in_specs=[anywhere] * (n + len(until)),
        out_specs=[anywhere] * n,
        out_shape=[jax.ShapeDtypeStruct(a.shape, a.dtype) for a in values],
        input_output_aliases={k: k for k in range(n)},
        cost_estimate=pl.CostEstimate(flops=0, bytes_accessed=0, transcendentals=0),
        name="gate",
    )(*values, *until))


def flip(value, axis, bit):
    size = lax.axis_size(axis)
    return lax.ppermute(value, axis, [(i, i ^ bit) for i in range(size)])


def bits(size):
    out, bit = [], 1
    while bit < size:
        out.append(bit)
        bit *= 2
    return out


def combos(steps):
    return [sum(bit for k, bit in enumerate(steps) if (j >> k) & 1) for j in range(1, 2 ** len(steps))]


def routes(n_dp):
    near, *far = bits(n_dp)
    return near, [far[k : k + 2] for k in range(0, len(far), 2)]


def dp_order(n_dp):
    near, groups = routes(n_dp)
    order = [0]
    for group in groups:
        order = order + [x ^ y for y in combos(group) for x in order]
    return order + [x ^ near for x in order]


def gather_mp(part):
    return jnp.stack([part] + [flip(part, "mp", j) for j in range(1, lax.axis_size("mp"))])


def gather_mp_steps(part):
    n_mp = lax.axis_size("mp")
    held = {0: part}
    for bit in bits(n_mp)[::-1]:
        came = flip(jnp.stack([held[j] for j in sorted(held)]), "mp", bit)
        held.update({j ^ bit: came[k] for k, j in enumerate(sorted(held))})
    return jnp.stack([held[j] for j in range(n_mp)])


def gather_far(column):
    held = [column]
    for group in routes(lax.axis_size("dp"))[1]:
        held = held + [flip(a, "dp", y) for y in combos(group) for a in held]
    return held


def add_up(*terms):
    total = terms[0].astype(F32)
    for term in terms[1:]:
        total = total + term.astype(F32)
    return total


def scatter_start(held):
    groups = routes(lax.axis_size("dp"))[1]
    size = len(held) // 2 ** len(groups[-1])
    sent = [(held[(k + 1) * size + i], y) for k, y in enumerate(combos(groups[-1])) for i in range(size)]
    return held[:size], sent


def scatter_end(kept, came):
    held = [add_up(kept[i], *came[i :: len(kept)]).astype(BF) for i in range(len(kept))]
    for group in routes(lax.axis_size("dp"))[1][-2::-1]:
        size = len(held) // 2 ** len(group)
        came = [[flip(held[(k + 1) * size + i], "dp", y) for i in range(size)] for k, y in enumerate(combos(group))]
        held = [add_up(held[i], *(row[i] for row in came)).astype(BF) for i in range(size)]
    return held[0]


def rows_at(order, j, my_dp, span):
    return pl.ds(pl.multiple_of((order[j] ^ my_dp) * span, span), span)


def head_mask(shape, head):
    lane = lax.broadcasted_iota(jnp.int32, shape, 1)
    return (lane < HEAD_DIM) if head == 0 else (lane >= HEAD_DIM)


SPANS = (2, 3, 4, 5, 6, 7, 8)


def by_span(ids, t, with_keys):
    low, number = ids[3 + t], ids[3 + LEN // TILE + t]
    for k, span in enumerate(SPANS):
        fits = number <= span
        if k:
            fits = fits & (number > SPANS[k - 1])

        @pl.when(fits)
        def _(span=span):
            start = jnp.minimum(low, LEN // KEYS - span) * KEYS
            with_keys(pl.multiple_of(start, KEYS), span * KEYS)


def reach(segment_row):
    heads_at, ends_at = segment_row[::TILE], segment_row[TILE - 1 :: TILE]
    low = jnp.sum((segment_row[None] < heads_at[:, None]).astype(jnp.int32), axis=1) // KEYS
    high = (jnp.sum((segment_row[None] <= ends_at[:, None]).astype(jnp.int32), axis=1) + KEYS - 1) // KEYS
    return low, high - low


def lay_out(order, my_dp, w_refs, w_all):
    span, half = D // len(order), len(order) // 2
    for j in range(len(order)):
        piece = w_refs[j][0, :span] if j < half else w_refs[half][j - half, 0, :span]
        w_all[rows_at(order, j, my_dp, span), :] = piece


def column_specs(w_parts, base):
    *ones, stacked = w_parts
    block = (1, *ones[0].shape[1:])
    return [pl.BlockSpec(block, lambda g, ids: (g + base, 0, 0))] * len(ones) + [
        pl.BlockSpec((stacked.shape[0], *block), lambda g, ids: (0, g + base, 0, 0))
    ]


def attend_kernel(order, ids, x_ref, *refs):
    n_w = len(order) // 2 + 1
    bias_ref, qf_ref, kf_ref, q_ref, k_ref, v_ref, ho_ref, lse_ref, w_all, keys, vals, rows = refs[n_w:]
    lay_out(order, ids[2], refs[:n_w], w_all)

    @pl.when(pl.program_id(0) == 0)
    def _():
        keys[:, PAIR:] = kf_ref[0]

    for t in range(LEN // TILE):
        at = slice(t * TILE, (t + 1) * TILE)
        got = dot(x_ref[0, at], w_all[...])
        q_ref[0, at] = (got[:, :PAIR] + bias_ref[0, 0:1]).astype(BF)
        key = got[:, PAIR : 2 * PAIR].astype(BF)
        k_ref[0, at] = key
        keys[at, :PAIR] = key
        val = (got[:, 2 * PAIR :] + bias_ref[0, 1:2]).astype(BF)
        v_ref[0, at] = val
        for head in range(2):
            vals[head, at, :] = jnp.where(head_mask((TILE, PAIR), head), val, BF(1))

    def one_tile(t, carry):
        at = pl.ds(pl.multiple_of(t * TILE, TILE), TILE)
        query = q_ref[0, at] * BF(0.125)

        def with_keys(start, count):
            near = pl.ds(start, count)
            low_lane = head_mask((TILE, PAIR), 0)
            wide0 = jnp.concatenate([jnp.where(head_mask((TILE, PAIR), 0), query, BF(0)), qf_ref[0, at]], axis=1)
            scores0 = dot(wide0, keys[near, :], NT)
            wide1 = jnp.concatenate([jnp.where(head_mask((TILE, PAIR), 1), query, BF(0)), qf_ref[0, at]], axis=1)
            scores1 = dot(wide1, keys[near, :], NT)
            top0 = jnp.max(scores0, axis=1, keepdims=True)
            probs0 = jnp.exp(scores0 - top0).astype(BF)
            top1 = jnp.max(scores1, axis=1, keepdims=True)
            probs1 = jnp.exp(scores1 - top1).astype(BF)
            out0 = dot(probs0, vals[0, near, :])
            out1 = dot(probs1, vals[1, near, :])
            total = pltpu.roll(jnp.where(low_lane, out1, out0), HEAD_DIM, 1)
            ho_ref[0, at] = (jnp.where(low_lane, out0, out1) / total).astype(BF)
            both = (jnp.where(low_lane, top0, top1) + jnp.log(total)).T
            lse_ref[0, 0:1, at] = both[0:1]
            lse_ref[0, 1:2, at] = both[HEAD_DIM : HEAD_DIM + 1]

        by_span(ids, t, with_keys)
        return carry

    lax.fori_loop(0, LEN // TILE, one_tile, 0)
    for head in range(2):
        for c in range(LEN // PAIR):
            at = head * (LEN // PAIR) + c
            rows[at : at + 1] = lse_ref[0, head : head + 1, c * PAIR : (c + 1) * PAIR]
    rest = rows[...]
    for k in range(3):
        part = rest.astype(BF)
        ho_ref[0, LEN + k * LOGS : LEN + (k + 1) * LOGS] = part
        rest = rest - part.astype(F32)


def sent_logs(ho_ref, logs):
    part = lambda k: ho_ref[0, LEN + k * LOGS : LEN + (k + 1) * LOGS].astype(F32)
    rows = part(0) + part(1) + part(2)
    for head in range(2):
        for c in range(LEN // PAIR):
            at = head * (LEN // PAIR) + c
            logs[2 + head : 3 + head, c * PAIR : (c + 1) * PAIR] = rows[at : at + 1]


def attend(ids, tokens, w_parts, bias, qf, kf, order, part=(0, 1), after=(), into=()):
    groups, tall, _ = w_parts[0].shape
    count = groups // part[1]
    base = part[0] * count
    pair = pl.BlockSpec((1, LEN, PAIR), lambda g, ids: (g, 0, 0))
    feats = pl.BlockSpec((1, LEN, PAIR), lambda g, ids: (ids[0], 0, 0))
    return kernel_call(
        functools.partial(attend_kernel, order),
        ids,
        (tokens, *w_parts, bias, qf, kf),
        [pl.BlockSpec((1, LEN, D), lambda g, ids: (ids[0], 0, 0))]
        + column_specs(w_parts, base)
        + [pl.BlockSpec((1, 2, PAIR), lambda g, ids: (g + base, 0, 0)), feats, feats],
        after,
        into,
        [
            pltpu.VMEM((D, 3 * PAIR), BF),
            pltpu.VMEM((LEN, 2 * PAIR), BF),
            pltpu.VMEM((2, LEN, PAIR), BF),
            pltpu.VMEM((LOGS, PAIR), F32),
        ],
        grid=(count,),
        out_specs=[
            pair,
            pair,
            pair,
            pl.BlockSpec((1, LEN + 3 * LOGS, PAIR), lambda g, ids: (g, 0, 0)),
            pl.BlockSpec((1, 2, LEN), lambda g, ids: (g, 0, 0)),
        ],
        out_shape=[jax.ShapeDtypeStruct((count, LEN, PAIR), BF)] * 3
        + [jax.ShapeDtypeStruct((count, LEN + 3 * LOGS, PAIR), BF), jax.ShapeDtypeStruct((count, 2, LEN), F32)],
        mib=63,
        name="attend",
    )


def norm_stats(value):
    center = value - jnp.mean(value, axis=-1, keepdims=True)
    spread = jnp.mean(center * center, axis=-1, keepdims=True)
    inverse = lax.rsqrt(spread + 1e-05)
    return center * inverse, inverse


def norm_backward(upstream, normal, inverse, gain):
    scaled = upstream * gain
    return inverse * (
        scaled
        - jnp.mean(scaled, axis=-1, keepdims=True)
        - normal * jnp.mean(scaled * normal, axis=-1, keepdims=True)
    )


CHUNK = 1024


def unpack(order, my_dp, w_refs, w_out, w_up, w_down):
    groups, span, _ = w_refs[0].shape
    wide = FF // groups
    for j in range(len(order)):
        row = rows_at(order, j, my_dp, span)
        for g in range(groups):
            w_out[row, g * PAIR : (g + 1) * PAIR] = w_refs[j][g, :, :PAIR]
            w_up[row, g * wide : (g + 1) * wide] = w_refs[j][g, :, PAIR : PAIR + wide]
            w_down[row, g * wide : (g + 1) * wide] = w_refs[j][g, :, PAIR + wide :]


def up_half(x_ref, heads, cot_ref, par_ref, ffb_ref, w_out, w_up, w_down, keep_hidden, slope_ref):
    gain_one, gain_two = par_ref[0:1], par_ref[1:2]
    shift_att, shift_ffn, shift_one, shift_two = (par_ref[k : k + 1] for k in range(2, 6))
    attention = dot(heads, w_out[...], NT) + shift_att
    normal_one, inverse_one = norm_stats(x_ref[0].astype(F32) + attention)
    normed = normal_one * gain_one + shift_one
    normed_low = normed.astype(BF)
    branch = shift_ffn
    for c in range(FF // CHUNK):
        at = slice(c * CHUNK, (c + 1) * CHUNK)
        pre = dot(normed_low, w_up[:, at]) + ffb_ref[:, at]
        phi = 0.5 * (1.0 + lax.erf(pre * 0.7071067811865476))
        hidden = (pre * phi).astype(BF)
        if keep_hidden is not None:
            keep_hidden(at, hidden)
        slope_ref[:, at] = phi + pre * jnp.exp(-0.5 * pre * pre) * 0.3989422804014327
        branch = branch + dot(hidden, w_down[:, at], NT)
    normal_two, inverse_two = norm_stats(normed + branch)
    final_low = (normal_two * gain_two + shift_two).astype(BF)
    upstream = cot_ref[0].astype(F32)
    g_final = norm_backward(upstream, normal_two, inverse_two, gain_two)
    return normal_one, inverse_one, normed_low, normal_two, final_low, upstream, g_final


def down_half(g_final, normal_one, inverse_one, par_ref, w_out, w_up, w_down, slope_ref, keep_pre):
    g_final_low = g_final.astype(BF)
    g_normed = g_final
    for c in range(FF // CHUNK):
        at = slice(c * CHUNK, (c + 1) * CHUNK)
        g_pre = (dot(g_final_low, w_down[:, at]) * slope_ref[:, at]).astype(BF)
        if keep_pre is not None:
            keep_pre(at, g_pre)
        g_normed = g_normed + dot(g_pre, w_up[:, at], NT)
    g_attention = norm_backward(g_normed, normal_one, inverse_one, par_ref[0:1])
    g_attention_low = g_attention.astype(BF)
    g_heads = dot(g_attention_low, w_out[...]).astype(BF)
    return g_final_low, g_normed, g_attention, g_attention_low, g_heads


def fold(acc, k, term, first):
    part = jnp.sum(term.reshape(TOKENS_AT_ONCE // 8, 8, D), axis=0)

    @pl.when(first)
    def _():
        acc[k] = part

    @pl.when(jnp.logical_not(first))
    def _():
        acc[k] += part


def is_middle(ids):
    return (ids[1] == 1) | (ids[1] == 2)


def heads_of(ids, ho_refs):
    there = [k ^ ids[0] ^ ids[1] for k in range(ho_refs[0].shape[0])]
    if len(ho_refs) == 1:
        return jnp.concatenate([ho_refs[0][k] for k in there], axis=1)
    return jnp.concatenate([jnp.where(is_middle(ids), ho_refs[1][k], ho_refs[0][k]) for k in there], axis=1)


def forward_kernel(order, ids, x_ref, ho_ref, *refs):
    half = len(order) // 2
    w_refs, refs = [*refs[:half], *(refs[half].at[j] for j in range(half))], refs[half + 1 :]
    par_ref, ffb_ref, out_ref, w_out, w_up, w_down = refs

    @pl.when(pl.program_id(0) == 0)
    def _():
        unpack(order, ids[2], w_refs, w_out, w_up, w_down)

    shift_att, shift_ffn, shift_one, shift_two = (par_ref[k : k + 1] for k in range(2, 6))
    attention = dot(heads_of(ids, [ho_ref]), w_out[...], NT) + shift_att
    normed = norm_stats(x_ref[0].astype(F32) + attention)[0] * par_ref[0:1] + shift_one
    normed_low = normed.astype(BF)
    branch = shift_ffn
    for c in range(FF // CHUNK):
        at = slice(c * CHUNK, (c + 1) * CHUNK)
        pre = dot(normed_low, w_up[:, at]) + ffb_ref[:, at]
        hidden = (pre * (0.5 * (1.0 + lax.erf(pre * 0.7071067811865476)))).astype(BF)
        branch = branch + dot(hidden, w_down[:, at], NT)
    out_ref[...] = (norm_stats(normed + branch)[0] * par_ref[1:2] + shift_two).astype(BF)


def forward_only(ids, tokens, heads_out, w_parts, params, ff_shift, order, after=(), into=()):
    full = lambda shape: pl.BlockSpec(shape, lambda t, ids: (0,) * len(shape))
    return kernel_call(
        functools.partial(forward_kernel, order),
        ids,
        (tokens, heads_out, *w_parts, params, ff_shift),
        [
            pl.BlockSpec((1, TOKENS_AT_ONCE, D), lambda t, ids: (ids[0], t, 0)),
            pl.BlockSpec((heads_out.shape[0], TOKENS_AT_ONCE, PAIR), lambda t, ids: (0, t, 0)),
        ]
        + [full(a.shape) for a in w_parts]
        + [full((6, D)), full((1, FF))],
        after,
        into,
        [pltpu.VMEM((D, D), BF), pltpu.VMEM((D, FF), BF), pltpu.VMEM((D, FF), BF)],
        grid=(LEN // TOKENS_AT_ONCE,),
        out_specs=[pl.BlockSpec((TOKENS_AT_ONCE, D), lambda t, ids: (t, 0))],
        out_shape=[jax.ShapeDtypeStruct((LEN, D), BF)],
        mib=63,
        name="forward_only",
    )[0]


def tokenwise_kernel(order, n_ho, keep, ids, x_ref, cot_ref, *refs):
    ho_refs, refs = refs[:n_ho], refs[n_ho:]
    half = len(order) // 2
    w_refs, refs = [*refs[:half], *(refs[half].at[j] for j in range(half))], refs[half + 1 :]
    par_ref, ffb_ref, full_ref, gatt_ref, gh_ref, *refs = refs
    if keep:
        near_ref, far_ref, sums_ref, ff_ref, w_out, w_up, w_down, slope, *refs = refs
        acc, ffs_ref, hid_all, pre_all, ho_all, up_t, down_t, att_t, gw_all = refs
    else:
        w_out, w_up, w_down, slope = refs
    step = pl.program_id(0)
    tiles = LEN // TOKENS_AT_ONCE
    groups = gh_ref.shape[0]
    my_dp = ids[2]

    @pl.when(step == 0)
    def _():
        unpack(order, my_dp, w_refs, w_out, w_up, w_down)

    def tokens_step():
        rows = pl.ds(pl.multiple_of(jnp.minimum(step, tiles - 1) * TOKENS_AT_ONCE, TOKENS_AT_ONCE), TOKENS_AT_ONCE)
        heads = heads_of(ids, ho_refs)
        keep_hidden = keep_pre = None
        if keep:

            def keep_hidden(at, hidden):
                hid_all[rows, at] = hidden

            def keep_pre(at, g_pre):
                pre_all[rows, at] = g_pre
                here = jnp.sum(g_pre.astype(F32), axis=0, keepdims=True)

                @pl.when(step == 0)
                def _():
                    ffs_ref[:, at] = here

                @pl.when(step > 0)
                def _():
                    ffs_ref[:, at] += here

        normal_one, inverse_one, normed_low, normal_two, final_low, upstream, g_final = up_half(
            x_ref, heads, cot_ref, par_ref, ffb_ref, w_out, w_up, w_down, keep_hidden, slope
        )
        full_ref[0] = final_low
        g_final_low, g_normed, g_attention, g_attention_low, g_heads = down_half(
            g_final, normal_one, inverse_one, par_ref, w_out, w_up, w_down, slope, keep_pre
        )
        gatt_ref[...] = g_attention
        for g in range(groups):
            gh_ref[g] = g_heads[:, g * PAIR : (g + 1) * PAIR]
        if keep:
            ho_all[rows, :] = heads
            down_t[:, rows] = g_final_low.T
            att_t[:, rows] = g_attention_low.T
            up_t[:, rows] = normed_low.T
            terms = (g_normed * normal_one, upstream * normal_two, g_attention, g_final, g_normed, upstream)
            for k, term in enumerate(terms):
                fold(acc, k, term, step == 0)

            @pl.when(step == tiles - 1)
            def _():
                for k in range(6):
                    total = jnp.sum(acc[k], axis=0, keepdims=True)
                    for c in range(D // PAIR):
                        at = k * (D // PAIR) + c
                        sums_ref[at : at + 1] = total[:, c * PAIR : (c + 1) * PAIR]
                per_group = FF // groups // PAIR
                for c in range(FF // PAIR):
                    ff_ref[c // per_group, c % per_group : c % per_group + 1] = ffs_ref[:, c * PAIR : (c + 1) * PAIR]

    if not keep:
        tokens_step()
        return

    pl.when(step < tiles)(tokens_step)

    @pl.when(step >= tiles)
    def _():
        half, _, span, _ = near_ref.shape
        wide = FF // groups
        block = pl.ds(pl.multiple_of((step - tiles) * wide, wide), wide)
        pair = pl.ds(pl.multiple_of((step - tiles) * PAIR, PAIR), PAIR)
        gw_all[:, :PAIR] = dot(att_t[...], ho_all[:, pair]).astype(BF)
        gw_all[:, PAIR : PAIR + wide] = dot(up_t[...], pre_all[:, block]).astype(BF)
        gw_all[:, PAIR + wide :] = dot(down_t[...], hid_all[:, block]).astype(BF)
        for j in range(half):
            near_ref[j, 0] = gw_all[rows_at(order, j, my_dp, span), :]
            far_ref[j, 0] = gw_all[rows_at(order, half + j, my_dp, span), :]


def tokenwise(ids, tokens, heads_out, cotangent, w_parts, params, ff_shift, order, keep, after=(), into=()):
    tiles = LEN // TOKENS_AT_ONCE
    groups, span, cols = w_parts[0].shape
    early = lambda t: jnp.minimum(t, tiles - 1)
    late = lambda t: jnp.maximum(t - tiles, 0)
    full = lambda shape: pl.BlockSpec(shape, lambda t, ids: (0,) * len(shape))
    row = pl.BlockSpec((1, TOKENS_AT_ONCE, D), lambda t, ids: (ids[0], early(t), 0))
    flat = pl.BlockSpec((TOKENS_AT_ONCE, D), lambda t, ids: (early(t), 0))
    pairs = lambda n: pl.BlockSpec((n, TOKENS_AT_ONCE, PAIR), lambda t, ids: (0, early(t), 0))
    out_specs = [row, flat, pairs(groups)]
    out_shape = [
        jax.ShapeDtypeStruct(tokens.shape, BF),
        jax.ShapeDtypeStruct((LEN, D), F32),
        jax.ShapeDtypeStruct((groups, LEN, PAIR), BF),
    ]
    scratch = [
        pltpu.VMEM((D, D), BF),
        pltpu.VMEM((D, FF), BF),
        pltpu.VMEM((D, FF), BF),
        pltpu.VMEM((TOKENS_AT_ONCE, FF), F32),
    ]
    if keep:
        half = len(order) // 2
        part = pl.BlockSpec((half, 1, span, cols), lambda t, ids: (0, late(t), 0, 0))
        norm_sums, ff_sums = (6 * D // PAIR, PAIR), (groups, FF // groups // PAIR, PAIR)
        out_specs += [part, part, full(norm_sums), full(ff_sums)]
        out_shape += [jax.ShapeDtypeStruct((half, groups, span, cols), BF)] * 2
        out_shape += [jax.ShapeDtypeStruct(norm_sums, F32), jax.ShapeDtypeStruct(ff_sums, F32)]
        scratch += [
            pltpu.VMEM((6, 8, D), F32),
            pltpu.VMEM((1, FF), F32),
            pltpu.VMEM((LEN, FF), BF),
            pltpu.VMEM((LEN, FF), BF),
            pltpu.VMEM((LEN, D), BF),
            pltpu.VMEM((D, LEN), BF),
            pltpu.VMEM((D, LEN), BF),
            pltpu.VMEM((D, LEN), BF),
            pltpu.VMEM((D, cols), BF),
        ]
    return kernel_call(
        functools.partial(tokenwise_kernel, order, len(heads_out), keep),
        ids,
        (tokens, cotangent, *heads_out, *w_parts, params, ff_shift),
        [row, row]
        + [pairs(a.shape[0]) for a in heads_out]
        + [full(a.shape) for a in w_parts]
        + [full((6, D)), full((1, FF))],
        after,
        into,
        scratch,
        grid=(tiles + groups if keep else tiles,),
        out_specs=out_specs,
        out_shape=out_shape,
        mib=63,
        name="tokenwise_keep" if keep else "tokenwise",
    )


def attend_back_kernel(order, keep, whole_row, ids, x_ref, *refs):
    n_w = len(order) // 2 + 1
    w_refs, (qf_ref, kf_ref, *refs) = refs[:n_w], refs[n_w:]
    if keep:
        q_ref, k_ref, v_ref, ho_ref, lse_ref, sums_ref, ff_ref, gh_ref, gatt_ref, *refs = refs
        tg_ref, send_ref, again_ref, near_ref, far_ref, *refs = refs
        w_all, keys, keys_t, delta, dk, dv, grads, w_wide, grads_wide, x_t, gw_all, extra = refs
    else:
        bias_ref, ho_ref, ho_mid, gh_ref, gatt_ref, tg_ref, *refs = refs
        w_all, keys, keys_t, delta, dk, dv, grads, w_wide, grads_wide, q_ref, k_ref, v_ref = refs
    my_dp = ids[2]
    if whole_row:
        tg_ref = tg_ref.at[0]
    block = pl.ds(pl.multiple_of(pl.program_id(0) * 3 * PAIR, 3 * PAIR), 3 * PAIR)
    lay_out(order, my_dp, w_refs, w_all)
    w_wide[:, block] = w_all[...]

    @pl.when(pl.program_id(0) == 0)
    def _():
        keys[:, PAIR:] = kf_ref[0]
        if keep:
            x_t[...] = x_ref[0].T
            extra[...] = jnp.zeros_like(extra)
            extra[:12, :PAIR] = sums_ref[:12]
            extra[:12, PAIR : 2 * PAIR] = sums_ref[12:]

    if keep:
        heads = ho_ref[0, :LEN]
        delta[2:4] = lse_ref[0]
    else:
        for t in range(LEN // TILE):
            at = slice(t * TILE, (t + 1) * TILE)
            got = dot(x_ref[0, at], w_all[...])
            q_ref[0, at] = (got[:, :PAIR] + bias_ref[0, 0:1]).astype(BF)
            k_ref[0, at] = got[:, PAIR : 2 * PAIR].astype(BF)
            v_ref[0, at] = (got[:, 2 * PAIR :] + bias_ref[0, 1:2]).astype(BF)
        heads = jnp.where(is_middle(ids), ho_mid[0, :LEN], ho_ref[0, :LEN])

        @pl.when(is_middle(ids))
        def _():
            sent_logs(ho_mid, delta)

        @pl.when(jnp.logical_not(is_middle(ids)))
        def _():
            sent_logs(ho_ref, delta)

    keys[:, :PAIR] = k_ref[0]
    keys_t[...] = k_ref[0].T
    prod = (gh_ref[0].astype(F32) * heads.astype(F32)).T
    delta[0:1] = jnp.sum(prod[:HEAD_DIM], axis=0, keepdims=True)
    delta[1:2] = jnp.sum(prod[HEAD_DIM:], axis=0, keepdims=True)
    dk[...] = jnp.zeros_like(dk)
    dv[...] = jnp.zeros_like(dv)

    def one_tile(t, carry):
        at = pl.ds(pl.multiple_of(t * TILE, TILE), TILE)
        query, back = q_ref[0, at], gh_ref[0, at]

        def with_keys(start, count):
            near = pl.ds(start, count)
            mine0 = jnp.where(head_mask((TILE, PAIR), 0), query, BF(0))
            back0 = jnp.where(head_mask((TILE, PAIR), 0), back, BF(0))
            wide0 = jnp.concatenate([mine0 * BF(0.125), qf_ref[0, at]], axis=1)
            scores0 = dot(keys[near, :], wide0, NT)
            g_probs0 = dot(v_ref[0, near], back0, NT)
            mine1 = jnp.where(head_mask((TILE, PAIR), 1), query, BF(0))
            back1 = jnp.where(head_mask((TILE, PAIR), 1), back, BF(0))
            wide1 = jnp.concatenate([mine1 * BF(0.125), qf_ref[0, at]], axis=1)
            scores1 = dot(keys[near, :], wide1, NT)
            g_probs1 = dot(v_ref[0, near], back1, NT)
            probs0 = jnp.exp(scores0 - delta[2:3, at])
            g_raw0 = (probs0 * (g_probs0 - delta[0 : 0 + 1, at])).astype(BF)
            low0 = probs0.astype(BF)
            probs1 = jnp.exp(scores1 - delta[3:4, at])
            g_raw1 = (probs1 * (g_probs1 - delta[1 : 1 + 1, at])).astype(BF)
            low1 = probs1.astype(BF)
            d_query0 = dot(keys_t[0 * HEAD_DIM : (0 + 1) * HEAD_DIM, near], g_raw0)
            d_query1 = dot(keys_t[1 * HEAD_DIM : (1 + 1) * HEAD_DIM, near], g_raw1)
            dv[near, :] += dot(jnp.concatenate([low0, low1], axis=1), jnp.concatenate([back0, back1], axis=0))
            dk[near, :] += dot(jnp.concatenate([g_raw0, g_raw1], axis=1), jnp.concatenate([mine0, mine1], axis=0))
            d_query = [d_query0, d_query1]
            grads[at, :PAIR] = (jnp.concatenate(d_query, axis=0).T * 0.125).astype(BF)

        by_span(ids, t, with_keys)
        return carry

    lax.fori_loop(0, LEN // TILE, one_tile, 0)
    grads[:, PAIR : 2 * PAIR] = (dk[...] * 0.125).astype(BF)
    grads[:, 2 * PAIR :] = dv[...].astype(BF)
    grads_wide[:, block] = grads[...]

    @pl.when(pl.program_id(0) == pl.num_programs(0) - 1)
    def _():
        for t in range(LEN // TILE):
            at = slice(t * TILE, (t + 1) * TILE)
            tg_ref[at, :] = gatt_ref[at, :] + dot(grads_wide[at, :], w_wide[...], NT)

    if keep:
        half, span = len(order) // 2, D // len(order)
        gw_all[...] = dot(x_t[...], grads[...]).astype(BF)
        extra[0:1, 2 * PAIR :] = jnp.sum(grads[:, :PAIR].astype(F32), axis=0, keepdims=True)
        extra[1:2, 2 * PAIR :] = jnp.sum(grads[:, 2 * PAIR :].astype(F32), axis=0, keepdims=True)
        extra[2 : 2 + ff_ref.shape[1], 2 * PAIR :] = ff_ref[0]
        vectors = extra[...].astype(BF)
        for j in range(half):
            near_ref[j, 0, :span] = gw_all[rows_at(order, j, my_dp, span), :]
            near_ref[j, 0, span:] = vectors
            far_ref[j, 0, :span] = gw_all[rows_at(order, half + j, my_dp, span), :]
            far_ref[j, 0, span:] = vectors

        @pl.when(pl.program_id(0) == pl.num_programs(0) - 1)
        def _():
            send = tg_ref[...].astype(BF)
            send_ref[...] = send
            again_ref[...] = send


def attend_back(ids, tokens, w_parts, qf, kf, saved, g_heads, g_att, order, keep, part=(0, 1), after=(), into=()):
    groups, tall, _ = w_parts[0].shape
    half = len(order) // 2
    count = groups // part[1]
    base = part[0] * count
    whole_row = part[0] == part[1] - 1
    there = lambda g, ids: (g + base) ^ ids[0] ^ ids[1]
    pair = pl.BlockSpec((1, LEN, PAIR), lambda g, ids: (there(g, ids), 0, 0))
    pair_logs = pl.BlockSpec((1, LEN + 3 * LOGS, PAIR), lambda g, ids: (there(g, ids), 0, 0))
    feats = pl.BlockSpec((1, LEN, PAIR), lambda g, ids: (ids[0], 0, 0))
    full = pl.BlockSpec((LEN, D), lambda g, ids: (0, 0))
    out_specs = [pl.BlockSpec((1, LEN, D), lambda g, ids: (ids[0], 0, 0)) if whole_row else full]
    out_shape = [jax.ShapeDtypeStruct(tokens.shape if whole_row else (LEN, D), F32)]
    scratch = [
        pltpu.VMEM((D, 3 * PAIR), BF),
        pltpu.VMEM((LEN, 2 * PAIR), BF),
        pltpu.VMEM((PAIR, LEN), BF),
        pltpu.VMEM((4, LEN), F32),
        pltpu.VMEM((LEN, PAIR), F32),
        pltpu.VMEM((LEN, PAIR), F32),
        pltpu.VMEM((LEN, 3 * PAIR), BF),
        pltpu.VMEM((D, count * 3 * PAIR), BF),
        pltpu.VMEM((LEN, count * 3 * PAIR), BF),
    ]
    if keep:
        saved_specs = [
            pair,
            pair,
            pair,
            pair_logs,
            pl.BlockSpec((1, 2, LEN), lambda g, ids: (g, 0, 0)),
            pl.BlockSpec(saved[5].shape, lambda g, ids: (0, 0)),
            pl.BlockSpec((1, *saved[6].shape[1:]), lambda g, ids: (g, 0, 0)),
        ]
        out_specs += [full, full] + [pl.BlockSpec((half, 1, tall, 3 * PAIR), lambda g, ids: (0, g, 0, 0))] * 2
        out_shape += [jax.ShapeDtypeStruct((LEN, D), BF)] * 2
        out_shape += [jax.ShapeDtypeStruct((half, groups, tall, 3 * PAIR), BF)] * 2
        scratch += [pltpu.VMEM((D, LEN), BF), pltpu.VMEM((D, 3 * PAIR), BF), pltpu.VMEM((EXTRA, 3 * PAIR), F32)]
    else:
        saved_specs = [pl.BlockSpec((1, 2, PAIR), lambda g, ids: (g + base, 0, 0)), pair_logs, pair_logs]
        scratch += [pltpu.VMEM((1, LEN, PAIR), BF)] * 3
    return kernel_call(
        functools.partial(attend_back_kernel, order, keep, whole_row),
        ids,
        (tokens, *w_parts, qf, kf, *saved, g_heads, g_att),
        [pl.BlockSpec((1, LEN, D), lambda g, ids: (ids[0], 0, 0))]
        + column_specs(w_parts, base)
        + [feats, feats]
        + saved_specs
        + [pl.BlockSpec((1, LEN, PAIR), lambda g, ids: (g + base, 0, 0)), full],
        after,
        into,
        scratch,
        grid=(count,),
        out_specs=out_specs,
        out_shape=out_shape,
        mib=63,
        flops=20_000_000_000,
        name="attend_back_keep" if keep else "attend_back",
    )


RATES = (D ** (-0.5), (D // 64) ** (-0.5), D ** (-0.5), FF ** (-0.5), 0.3, 0.3, 0.3, 0.3)
DECAYS = (0.01, 0.01, 0.01, 0.01, 0.0, 0.0, 0.0, 0.0)


def adam_step(weight, grad_sum, first, second, rate, decay):
    first_new = beta_one * first + (1.0 - beta_one) * grad_sum
    second_new = beta_two * second + (1.0 - beta_two) * grad_sum * grad_sum
    first_hat = first_new / (1.0 - beta_one**STEP)
    second_hat = second_new / (1.0 - beta_two**STEP)
    weight_new = weight - rate * (first_hat / (jnp.sqrt(second_hat) + 1e-08) + decay * weight)
    return (weight_new, first_new, second_new)


def adam_kernel(ids, *refs):
    terms, olds, news, whole, mine = refs[:4], refs[4:28], refs[28:52], refs[52], refs[53]
    span = olds[2].shape[0]
    wide, per = olds[2].shape[1], olds[5].shape[1]
    total_ab = lambda at: terms[0][:, at].astype(F32) + terms[1][:, at].astype(F32)
    total_qkv = lambda rows, at: terms[2][rows, at].astype(F32) + terms[3][rows, at].astype(F32)

    def step(slot, at, grad):
        old = [olds[8 * k + slot][at] for k in range(3)]
        new = adam_step(old[0], grad, old[1], old[2], RATES[slot], DECAYS[slot])
        for k in range(3):
            news[8 * k + slot][at] = new[k]

    for k in range(3):
        step(0, k, total_qkv(slice(0, span), slice(k * PAIR, (k + 1) * PAIR)))
    step(1, ..., total_ab(slice(0, PAIR)))
    step(2, ..., total_ab(slice(PAIR, PAIR + wide)))
    step(3, ..., total_ab(slice(PAIR + wide, PAIR + 2 * wide)))
    whole[...] = total_qkv(slice(span, span + EXTRA), slice(0, 3 * PAIR))
    first_norm = ids[2] * span
    turns = (first_norm, first_norm, ids[2] * per)
    for k in range(3):
        back = lax.rem(PAIR - lax.rem(turns[k], PAIR), PAIR)
        mine[k * EXTRA : (k + 1) * EXTRA] = pltpu.roll(whole[:, k * PAIR : (k + 1) * PAIR], back, 1)
    for k in range(6):
        at = (k // 3) * EXTRA + (k % 3) * (D // PAIR) + first_norm // PAIR
        slot, row = (6, k) if k < 2 else (7, k - 2)
        step(slot, slice(row, row + 1), mine[pl.ds(at, 1), :span])
    pieces = lambda row: [mine[2 * EXTRA + row : 2 * EXTRA + row + 1, h * HEAD_DIM : h * HEAD_DIM + per] for h in (0, 1)]
    for kind in range(2):
        for head, grad in enumerate(pieces(kind)):
            step(4, (kind, slice(head, head + 1)), grad)
    for row in range(olds[5].shape[0] // 2):
        for head, grad in enumerate(pieces(2 + row)):
            step(5, slice(2 * row + head, 2 * row + head + 1), grad)


def adam(ids, last, after, *sets):
    turn = lambda a: (a[0].transpose(1, 0, 2), a[1].T, a[2], a[3].T, *a[4:])
    olds = [array for group in sets for array in turn(group)]
    inputs = (*last[0], *last[1], *olds)
    full = lambda a: pl.BlockSpec(a.shape, lambda t, ids: (0,) * a.ndim)
    news = kernel_call(
        adam_kernel, ids, inputs, [full(a) for a in inputs], after, (),
        [pltpu.VMEM((EXTRA, 3 * PAIR), F32), pltpu.VMEM((3 * EXTRA, PAIR), F32)],
        grid=(1,),
        out_specs=[full(a) for a in olds],
        out_shape=[jax.ShapeDtypeStruct(a.shape, F32) for a in olds],
        mib=63,
        name="adam",
    )
    return [array for k in range(3) for array in turn(news[8 * k : 8 * k + 8])]


def rows_of(ids):
    z = ids[1]
    by = lambda a, b, c, d: jnp.where(z == 0, a, jnp.where(z == 1, b, jnp.where(z == 2, c, d)))
    return z, by(1, 2, 1, 2), by(2, 0, 3, 1), by(3, 3, 0, 0)


PLACED = 256


def place_kernel(ids, grad_straight, grad_middle, grad_end, out_straight, out_middle, out_end, _, __, tg_ref, lo_ref, sems, one, two, three, four):
    t, last = pl.program_id(0), pl.num_programs(0) - 1
    _, _, straight, through = rows_of(ids)
    slot = lax.rem(t, 2)
    inside = is_middle(ids)

    def copies(step, slot):
        ways = ((one, tg_ref, straight), (two, tg_ref, through), (three, lo_ref, straight), (four, lo_ref, through))
        return [
            pltpu.make_async_copy(buf.at[slot], ref.at[row, pl.ds(step * PLACED, PLACED)], sems.at[k, slot])
            for k, (buf, ref, row) in enumerate(ways)
        ]

    @pl.when(t >= 2)
    def _():
        for copy in copies(t - 2, slot):
            copy.wait()

    one[slot] = grad_straight[...].astype(F32)
    two[slot] = jnp.where(inside, grad_middle[...], grad_end[...]).astype(F32)
    three[slot] = out_straight[...]
    four[slot] = jnp.where(inside, out_middle[...], out_end[...])
    for copy in copies(t, slot):
        copy.start()

    @pl.when(t == last)
    def _():
        for copy in copies(t - 1, 1 - slot) + copies(t, slot):
            copy.wait()


def place(ids, grads, outs, tokens_grad, layer_out):
    block = pl.BlockSpec((PLACED, D), lambda t, ids: (t, 0))
    chosen = [
        pl.BlockSpec((PLACED, D), lambda t, ids: (jnp.where(is_middle(ids), t, 0), 0)),
        pl.BlockSpec((PLACED, D), lambda t, ids: (jnp.where(is_middle(ids), 0, t), 0)),
    ]
    anywhere = pl.BlockSpec(memory_space=pl.ANY)
    return pl.pallas_call(
        place_kernel,
        grid_spec=pltpu.PrefetchScalarGridSpec(
            num_scalar_prefetch=1,
            grid=(LEN // PLACED,),
            in_specs=[block, *chosen, block, *chosen] + [anywhere] * 2,
            out_specs=[anywhere, anywhere],
            scratch_shapes=[
                pltpu.SemaphoreType.DMA((4, 2)),
                pltpu.VMEM((2, PLACED, D), F32),
                pltpu.VMEM((2, PLACED, D), F32),
                pltpu.VMEM((2, PLACED, D), BF),
                pltpu.VMEM((2, PLACED, D), BF),
            ],
        ),
        out_shape=[jax.ShapeDtypeStruct(a.shape, a.dtype) for a in (tokens_grad, layer_out)],
        input_output_aliases={7: 0, 8: 1},
        compiler_params=vmem(63),
        name="place",
    )(ids, *grads, *outs, tokens_grad, layer_out)


def pack_kernel(qkv, out_t, up, down_t, qv, ff, gains, shifts, first_ref, second_ref):
    span, wide = up.shape
    for k in range(3):
        first_ref[:span, k * PAIR : (k + 1) * PAIR] = qkv[k].astype(BF)
    first_ref[span:, :] = jnp.zeros((EXTRA, 3 * PAIR), BF)
    first_ref[span : span + 2, :span] = gains[...].astype(BF)
    first_ref[span + 2 : span + 6, :span] = shifts[...].astype(BF)
    first_ref[span : span + ff.shape[0], PAIR : PAIR + ff.shape[1]] = ff[...].astype(BF)
    for k in range(2):
        first_ref[span + 2 * k : span + 2 * k + 2, 2 * PAIR : 2 * PAIR + qv.shape[2]] = qv[k].astype(BF)
    second_ref[:, :PAIR] = out_t[...].astype(BF)
    second_ref[:, PAIR : PAIR + wide] = up[...].astype(BF)
    second_ref[:, PAIR + wide :] = down_t[...].astype(BF)


def pack(w_qkv, w_out, w_up, w_down, qv_bias, ff_bias, norm_gains, norm_shifts):
    span, wide = w_up.shape
    return pl.pallas_call(
        pack_kernel,
        out_shape=[
            jax.ShapeDtypeStruct((span + EXTRA, 3 * PAIR), BF),
            jax.ShapeDtypeStruct((span, PAIR + 2 * wide), BF),
        ],
        name="pack",
    )(w_qkv.transpose(1, 0, 2), w_out.T, w_up, w_down.T, qv_bias, ff_bias, norm_gains, norm_shifts)


def features(segment_ids, pad_lengths):
    place = jnp.arange(LEN, dtype=jnp.int32)[None, :, None]
    lane = jnp.arange(PAIR, dtype=jnp.int32)[None, None, :]
    segment = segment_ids[:, :, None]
    padding = place >= (LEN - pad_lengths)[:, None, None]
    high, low = place // 32, place % 32
    hit = (
        ((lane < 4) & (lane == segment))
        | ((lane >= 4) & (lane < 36) & (lane - 4 == high))
        | ((lane >= 36) & (lane < 68) & (lane - 36 == low))
    )
    counts = jnp.where(padding, (lane >= 4) & (lane < 68), lane < 4)
    qf = jnp.where(hit, -FAR, 0.0).astype(BF)
    kf = jnp.where(counts & ~hit, 1.0, 0.0).astype(BF)
    return qf, kf


def per_device(
    tokens, segment_ids, pad_lengths, cotangent,
    w_qkv, w_out, w_up, w_down, qv_bias, ff_bias, norm_gains, norm_shifts,
    first_qkv, first_out, first_up, first_down, first_qv_bias, first_ff_bias, first_gains, first_shifts,
    second_qkv, second_out, second_up, second_down, second_qv_bias, second_ff_bias, second_gains, second_shifts,
):
    n_dp, n_mp = lax.axis_size("dp"), lax.axis_size("mp")
    my_dp, my_mp = lax.axis_index("dp"), lax.axis_index("mp")
    order = dp_order(n_dp)
    half = n_dp // 2
    span = D // n_dp
    wide, per = FF // n_mp, HEAD_DIM // n_dp
    ff_rows = wide // HEAD_DIM

    places = ((jnp.array(order, jnp.int32)[:, None] ^ my_dp) == jnp.arange(n_dp, dtype=jnp.int32)[None]).astype(BF)

    def to_near(value):
        return flip(value, "dp", routes(n_dp)[0])

    part_qkv, part_ab = pack(w_qkv, w_out, w_up, w_down, qv_bias, ff_bias, norm_gains, norm_shifts)
    far_qkv = gather_far(gather_mp(part_qkv))
    all_qkv = [*far_qkv, to_near(jnp.stack(far_qkv))]
    far_ab = gather_far(gather_mp_steps(part_ab))
    small_here = jnp.concatenate(
        [jnp.stack([a[:, span : span + 8] for a in all_qkv[:half]]), all_qkv[half][:, :, span : span + 8]]
    ).reshape(n_dp, -1)
    small_all = dot(places, small_here, (((0,), (0,)), ((), ()))).reshape(n_dp, n_mp, 8, 3 * PAIR)
    bias_rows = (
        small_all[:, :, :4, 2 * PAIR : 2 * PAIR + per].reshape(n_dp, n_mp, 2, 2, per).transpose(1, 2, 3, 0, 4)
    ).reshape(n_mp, 2, PAIR)
    ff_shift = small_all[:, :, :ff_rows, PAIR : PAIR + per].transpose(1, 2, 0, 3).reshape(1, FF)
    params = small_all[:, 0, :6, :span].transpose(1, 0, 2).reshape(6, D)
    qf, kf = features(segment_ids, pad_lengths)

    def ids_of(row):
        low, number = reach(lax.dynamic_index_in_dim(segment_ids, row, 0, keepdims=False))
        return jnp.concatenate([jnp.stack([row, my_mp, my_dp]).astype(jnp.int32), low, number])

    second = jnp.where((my_mp == 0) | (my_mp == 2), 1, 2)
    mine, other = ids_of(my_mp), ids_of(second)

    saved = attend(mine, tokens, all_qkv, bias_rows, qf, kf, order)
    far_ab = gate(far_ab, saved[4])
    all_ab = [*far_ab, to_near(jnp.stack(far_ab))]
    to_ends, to_middles = [(1, 0), (2, 3)], [(1, 2), (2, 1)]
    across, straight = [(0, 2), (3, 1)], [(0, 1), (3, 2), (1, 3), (2, 0)]
    heads_end, heads_mid = (lax.ppermute(saved[3], "mp", way) for way in (to_ends, to_middles))
    own_out = forward_only(mine, tokens, saved[3], all_ab, params, ff_shift, order)
    out_middle = lax.ppermute(own_out, "mp", across)
    layer_out, g_att, g_heads, near_ab, far_grad_ab, sums, ff_sums = tokenwise(
        mine, tokens, [saved[3]], cotangent, all_ab, params, ff_shift, order, True, after=(own_out,)
    )
    out_straight = lax.ppermute(own_out, "mp", straight)
    came_ab = to_near(far_grad_ab)
    tokens_grad, own_send, send_again, near_qkv, far_grad_qkv = attend_back(
        mine, tokens, all_qkv, qf, kf, (*saved, sums, ff_sums), g_heads, g_att, order, True,
        after=(heads_end, heads_mid, out_middle),
    )
    held_ab = [add_up(near_ab[j], came_ab[j]).astype(BF) for j in range(half)]
    own_send, out_middle, out_straight, far_grad_qkv = gate((own_send, out_middle, out_straight, far_grad_qkv))
    came_qkv = to_near(far_grad_qkv)
    grad_middle = lax.ppermute(own_send, "mp", across)
    out_end = lax.ppermute(out_middle, "mp", to_ends)
    kept_ab, sent_ab = scatter_start(held_ab)
    late = len(sent_ab) - len(kept_ab)
    far_sums_ab = [flip(value, "dp", y) for value, y in sent_ab[:late]]
    layer_out, g_att2, g_heads2 = tokenwise(
        other, tokens, [heads_end, heads_mid], cotangent, all_ab, params, ff_shift, order, False,
        after=(own_send,), into=((layer_out, 0),),
    )
    late_ab = [value for value, _ in sent_ab[late:]]
    n_late = len(late_ab)
    send_again, grad_middle, out_end, came_qkv, *moved = gate(
        (send_again, grad_middle, out_end, came_qkv, *late_ab, *far_sums_ab), g_heads2
    )
    late_ab, far_sums_ab = moved[:n_late], moved[n_late:]
    grad_straight = lax.ppermute(send_again, "mp", straight)
    grad_end = lax.ppermute(grad_middle, "mp", to_ends)
    late_ab = [flip(value, "dp", y) for value, (_, y) in zip(late_ab, sent_ab[late:])]
    far_bits = [bit for group in routes(n_dp)[1] for bit in group]
    kept_qkv = near_qkv.shape[0] // 2
    held_qkv = [add_up(near_qkv[k * kept_qkv : (k + 1) * kept_qkv], came_qkv[k * kept_qkv : (k + 1) * kept_qkv]).astype(BF) for k in range(2)]
    came_half = flip(held_qkv[1], "dp", far_bits[-1])
    of_other = (bias_rows, heads_end, heads_mid)
    (half_grad,) = attend_back(
        other, tokens, all_qkv, qf, kf, of_other, g_heads2, g_att2, order, False, (0, 2),
        after=(grad_middle, *held_qkv),
    )
    came_half, *late_ab = gate((came_half, *late_ab), half_grad)
    column_ab = scatter_end(kept_ab, [*far_sums_ab, *late_ab])
    column_qkv = add_up(held_qkv[0], came_half).astype(BF)
    for bit in far_bits[-2::-1]:
        kept_qkv = column_qkv.shape[0] // 2
        came_half = flip(column_qkv[kept_qkv:], "dp", bit)
        column_qkv = (column_qkv[:kept_qkv], came_half)
        if bit != far_bits[0]:
            column_qkv = add_up(*column_qkv).astype(BF)
    come_mp = lambda a: flip(jnp.stack([a[1], a[3]]), "mp", 1)
    keep_mp = lambda a, b: add_up(jnp.stack([a[0], a[2]]), b).astype(BF)
    came_mp_ab = come_mp(column_ab)
    (tokens_grad,) = attend_back(
        other, tokens, all_qkv, qf, kf, of_other, g_heads2, half_grad, order, False, (1, 2),
        after=(column_qkv[0],), into=((tokens_grad, 0),),
    )
    came_mp_ab, came_half = gate((came_mp_ab, column_qkv[1]), tokens_grad)
    column_qkv = add_up(column_qkv[0], came_half)[0].astype(BF)
    pair_ab, pair_qkv = keep_mp(column_ab, came_mp_ab), keep_mp(column_qkv, come_mp(column_qkv))
    last = [(a[0], flip(a[1], "mp", 2)) for a in (pair_ab, pair_qkv)]
    tokens_grad, layer_out = place(
        mine, (grad_straight, grad_middle, grad_end), (out_straight, out_middle, out_end), tokens_grad, layer_out
    )

    masters = (w_qkv, w_out, w_up, w_down, qv_bias, ff_bias, norm_gains, norm_shifts)
    firsts = (first_qkv, first_out, first_up, first_down, first_qv_bias, first_ff_bias, first_gains, first_shifts)
    seconds = (second_qkv, second_out, second_up, second_down, second_qv_bias, second_ff_bias, second_gains, second_shifts)
    updated = adam(mine, last, (tokens_grad,), masters, firsts, seconds)
    return (layer_out, tokens_grad, *updated)


def solution(mesh):
    weights = (
        P("dp", None, "mp"),
        P("mp", "dp"),
        P("dp", "mp"),
        P("mp", "dp"),
        P(None, "mp", "dp"),
        P("mp", "dp"),
        P(None, "dp"),
        P(None, "dp"),
    )
    rows = P("dp", None, None)
    return jax.shard_map(
        per_device,
        mesh=mesh,
        in_specs=(rows, P("dp", None), P("dp"), rows) + weights * 3,
        out_specs=(rows, rows) + weights * 3,
        check_vma=False,
    )
```
